32 devices in a mesh: dp: 8 (over z, core), expert: 4 (over y, x).
Axes of the slice: x: 2, y: 2, z: 4, core: 2. Of those that a mesh axis runs over, the one named last changes fastest.
Arguments:
- tokens: bfloat16 [64, 128, 768], P(('dp', 'expert')), may hold values from -6 to 6
- teacher: bfloat16 [64, 128, 768], P(('dp', 'expert')), may hold values from -6 to 6
- routes: int32 [64, 128, 1], P(('dp', 'expert')), may hold values from 0 to 3; in each aligned block of 128 rows (0 to 127, 128 to 255, ..., all dimensions but the last counted through in order) at most 64 rows name the same one
- piece_start: int32 [64], P(('dp', 'expert')), may hold values from 0 to 96
- valid_mask: int32 [64, 128], P(('dp', 'expert')), may hold values from 0 to 1, as said below
- lower_gain: bfloat16 [768], P(('dp', 'expert')), may hold values from 0.5 to 1.5
- lower_bias: bfloat16 [768], P(('dp', 'expert')), may hold values from -0.59765625 to 0.59765625
- lower_triple: bfloat16 [768, 2304], P(('dp', 'expert')), may hold values from -0.21875 to 0.21875
- lower_output: bfloat16 [768, 768], P(('dp', 'expert')), may hold values from -0.875 to 0.875
- feed_gain: bfloat16 [768], P(('dp', 'expert')), may hold values from 0.5 to 1.5
- feed_bias: bfloat16 [768], P(('dp', 'expert')), may hold values from -0.59765625 to 0.59765625
- feed_expand: bfloat16 [768, 3072], P(('dp', 'expert')), may hold values from -0.21875 to 0.21875
- feed_shrink: bfloat16 [3072, 768], P(('dp', 'expert')), may hold values from -0.21875 to 0.21875
- upper_gain: bfloat16 [768], P(('dp', 'expert')), may hold values from 0.5 to 1.5
- upper_bias: bfloat16 [768], P(('dp', 'expert')), may hold values from -0.59765625 to 0.59765625
- upper_triple: bfloat16 [768, 2304], P(('dp', 'expert')), may hold values from -0.21875 to 0.21875
- upper_output: bfloat16 [768, 768], P(('dp', 'expert')), may hold values from -0.875 to 0.875
- mixer_gain: bfloat16 [768], P(('dp', 'expert')), may hold values from 0.5 to 1.5
- mixer_bias: bfloat16 [768], P(('dp', 'expert')), may hold values from -0.59765625 to 0.59765625
- router: bfloat16 [768, 4], P(('dp', 'expert')), may hold values from -0.15625 to 0.15625
- expert_expand: bfloat16 [4, 768, 3072], P('expert', 'dp'), may hold values from -0.21875 to 0.21875
- expert_shrink: bfloat16 [4, 3072, 768], P('expert', 'dp'), may hold values from -0.21875 to 0.21875
Outputs:
- states: bfloat16 [64, 128, 768], P(('dp', 'expert'))
- tokens_delta: float32 [64, 128, 768], P(('dp', 'expert'))
- lower_gain_delta: float32 [768], P(('dp', 'expert'))
- lower_bias_delta: float32 [768], P(('dp', 'expert'))
- lower_triple_delta: float32 [768, 2304], P(('dp', 'expert'))
- lower_output_delta: float32 [768, 768], P(('dp', 'expert'))
- feed_gain_delta: float32 [768], P(('dp', 'expert'))
- feed_bias_delta: float32 [768], P(('dp', 'expert'))
- feed_expand_delta: float32 [768, 3072], P(('dp', 'expert'))
- feed_shrink_delta: float32 [3072, 768], P(('dp', 'expert'))
- upper_gain_delta: float32 [768], P(('dp', 'expert'))
- upper_bias_delta: float32 [768], P(('dp', 'expert'))
- upper_triple_delta: float32 [768, 2304], P(('dp', 'expert'))
- upper_output_delta: float32 [768, 768], P(('dp', 'expert'))
- mixer_gain_delta: float32 [768], P(('dp', 'expert'))
- mixer_bias_delta: float32 [768], P(('dp', 'expert'))
- router_delta: float32 [768, 4], P(('dp', 'expert'))
- expert_expand_delta: float32 [4, 768, 3072], P('expert', 'dp')
- expert_shrink_delta: float32 [4, 3072, 768], P('expert', 'dp')
- mean_loss: float32 [], replicated
The draws below stay inside these ranges and needn't reach their ends.
Inputs may be any that keep to these rules, and one draw needn't show every extreme that they name: `routes`: in each sequence no expert is chosen by more than 64 tokens; in some sequence one is chosen by exactly 64. `valid_mask`: the first token of every sequence is valid.
All inputs are finite; a program needn't handle non-finite values.
Results may differ from the reference program's by a relative error of at most 0.013.
Values may be sent and summed in bfloat16 or wider, within the bound.
No kernel may reach another device: no remote copies, remote signals or barrier semaphores. Data moves between devices by JAX's collectives and lax.ppermute only.
A program may use at most 192 MiB of HBM per device.

```python
import math
import jax
import jax.numpy as jnp
import numpy as np
from jax import lax

D = 768
H = 12
HD = 64
FF = 3072
LEN = 128
EXPERTS = 4
CAP = 64
PIECE = 32
SEQS = 64
TOKENS = 8192


def draw_valid_mask(key, part):
    sequence = jnp.arange(SEQS, dtype=jnp.int32)[:, None]
    level = 300 + 600 * sequence // max(SEQS - 1, 1)
    roll = jax.random.randint(key, (SEQS, LEN), 0, 1000, dtype=jnp.int32)
    keep = (roll < level).astype(jnp.int32)
    first = jnp.arange(LEN, dtype=jnp.int32)[None, :] == 0
    return jnp.where(first, 1, keep).astype(jnp.int32)


def place_ends(values, key, low, largest):
    index_at = [jax.random.randint(jax.random.fold_in(key, axis), (), 0, length) for axis, length in enumerate(values.shape)]
    widest = values.shape.index(max(values.shape))
    next_to = index_at[:widest] + [(index_at[widest] + 1) % values.shape[widest]] + index_at[widest + 1:]
    return values.at[tuple(index_at)].set(low).at[tuple(next_to)].set(largest)


def steps_of(rng, dims, pieces, low, top_value):
    loudness, own = 1.0, jax.random.fold_in(rng, 6)
    for dim, parts in pieces:
        draws = jnp.exp(jax.random.uniform(jax.random.fold_in(own, dim), (parts,), jnp.float32, low / len(pieces), top_value / len(pieces)))
        loudness = loudness * jnp.repeat(draws, dims[dim] // parts).reshape([-1 if axis == dim else 1 for axis in range(len(dims))])
    return loudness


def deal_out(key, own, number, rows, number_of, top, bound, lean):
    order = jax.random.permutation(key, number_of)
    crowded, usual = shares(number_of, rows * top, bound, lean, True), shares(number_of, rows * top, bound, lean, False)
    places = jnp.arange(number_of)

    def named(sizes, offset_by):
        used = int((sizes > 0).sum())
        fixed = max(1, used // 4)
        shifted = fixed + (places - fixed + offset_by * (used - fixed)) % max(1, number_of - fixed)
        return jnp.zeros((number_of,), jnp.int32).at[order[jnp.where(places < fixed, places, shifted)]].set(jnp.asarray(sizes, jnp.int32))

    sizes = jnp.where(number % 4 == 0, named(crowded, number // 4), named(usual, number - number // 4 - 1))
    mixed = jax.random.permutation(jax.random.fold_in(own, 3), number_of)
    donor, sink = mixed[0:number_of // 2 * 2:2], mixed[1:number_of // 2 * 2:2]
    room = jnp.minimum(sizes[donor] - 1, bound - sizes[sink]) // 2
    room = jnp.where((donor == order[0]) | (sink == order[0]) | (sizes[sink] == 0), 0, jnp.maximum(room, 0))
    shifted = jax.random.randint(jax.random.fold_in(own, 4), (number_of // 2,), 0, 1 << 20) % (room + 1)
    sizes = sizes.at[donor].add(-shifted).at[sink].add(shifted)
    items = jnp.searchsorted(jnp.cumsum(sizes), jnp.arange(rows * top), side="right").astype(jnp.int32)
    grid = items.reshape(top, rows).T
    grid = grid[jax.random.permutation(jax.random.fold_in(own, 1), rows)]
    offset_by = jax.random.randint(jax.random.fold_in(own, 2), (rows, 1), 0, top)
    return jnp.take_along_axis(grid, (jnp.arange(top)[None, :] + offset_by) % top, axis=1)


def shares(amount, total, bound, slope, full):
    loads = [(1 << 20) // math.isqrt(standing ** slope) + 1 for standing in range(1, amount + 1)]
    largest = bound if full else min(bound, max(-(-total // amount), total * loads[0] // sum(loads)))
    least = 1 if total - largest >= amount - 1 else 0
    counts, surplus = [largest] + [least] * (amount - 1), total - largest - least * (amount - 1)
    while surplus > 0:
        free = [i for i in range(1, amount) if counts[i] < largest] or [i for i in range(1, amount) if counts[i] < bound]
        whole, left = sum([loads[i] for i in free]), surplus
        for i in free:
            extra = min(bound - counts[i], max(1, left * loads[i] // whole), surplus)
            counts[i] = counts[i] + extra
            surplus = surplus - extra
    return np.array(counts)


def gaussian(rng, dims, scale, most, cuts=(), kind=jnp.bfloat16):
    entries = jax.random.normal(rng, dims, jnp.float32) * scale
    if len(cuts) > 0:
        entries = steps_of(rng, dims, cuts, -0.22, 0.18) * entries
    return jnp.clip(entries, min=-most, max=most).astype(kind)


def setup_inputs(seed: int = 0) -> dict:
    arg_keys = jax.random.split(jax.random.key(seed), 23)
    tokens = gaussian(arg_keys[0], (SEQS, LEN, D), 1.0, 6.0, ((0, 32),))
    teacher = gaussian(arg_keys[1], (SEQS, LEN, D), 1.0, 6.0, ((0, 32),))
    routes_keys = jax.random.split(jax.random.fold_in(arg_keys[2], 1), SEQS * LEN // LEN)
    routes_turns = jax.random.permutation(jax.random.fold_in(arg_keys[2], 3), SEQS * LEN // LEN)
    routes = jax.vmap(lambda own, number: deal_out(jax.random.fold_in(arg_keys[2], 2), own, number, LEN, EXPERTS, 1, CAP, 2))(routes_keys, routes_turns).reshape((SEQS, LEN, 1))
    piece_start = place_ends(jax.random.randint(arg_keys[3], (SEQS,), 0, LEN - PIECE + 1), jax.random.fold_in(arg_keys[3], 1), 0, LEN - PIECE).astype(jnp.int32)
    valid_mask = draw_valid_mask(jax.random.fold_in(arg_keys[22], 71), 0)
    lower_gain = jnp.clip(1.0 + 0.1 * jax.random.normal(arg_keys[5], (D,), jnp.float32), 0.5, 1.5).astype(jnp.bfloat16)
    lower_bias = gaussian(arg_keys[6], (D,), 0.1, 0.59765625, ((0, 32),))
    lower_triple = gaussian(arg_keys[7], (D, 3 * D), D ** -0.5, 0.21875, ((0, 32),))
    lower_output = gaussian(arg_keys[8], (D, D), (D // 16) ** -0.5, 0.875, ((0, 32),))
    feed_gain = jnp.clip(1.0 + 0.1 * jax.random.normal(arg_keys[9], (D,), jnp.float32), 0.5, 1.5).astype(jnp.bfloat16)
    feed_bias = gaussian(arg_keys[10], (D,), 0.1, 0.59765625, ((0, 32),))
    feed_expand = gaussian(arg_keys[11], (D, FF), D ** -0.5, 0.21875, ((0, 32),))
    feed_shrink = gaussian(arg_keys[12], (FF, D), (FF // 4) ** -0.5, 0.21875, ((0, 32),))
    upper_gain = jnp.clip(1.0 + 0.1 * jax.random.normal(arg_keys[13], (D,), jnp.float32), 0.5, 1.5).astype(jnp.bfloat16)
    upper_bias = gaussian(arg_keys[14], (D,), 0.1, 0.59765625, ((0, 32),))
    upper_triple = gaussian(arg_keys[15], (D, 3 * D), D ** -0.5, 0.21875, ((0, 32),))
    upper_output = gaussian(arg_keys[16], (D, D), (D // 16) ** -0.5, 0.875, ((0, 32),))
    mixer_gain = jnp.clip(1.0 + 0.1 * jax.random.normal(arg_keys[17], (D,), jnp.float32), 0.5, 1.5).astype(jnp.bfloat16)
    mixer_bias = gaussian(arg_keys[18], (D,), 0.1, 0.59765625, ((0, 32),))
    router = gaussian(arg_keys[19], (D, EXPERTS), (2 * D) ** -0.5, 0.15625, ((0, 32),))
    expert_expand = gaussian(arg_keys[20], (EXPERTS, D, FF), D ** -0.5, 0.21875, ((0, 4), (1, 8)))
    expert_shrink = gaussian(arg_keys[21], (EXPERTS, FF, D), (FF // 4) ** -0.5, 0.21875, ((0, 4), (1, 8)))
    return {"tokens": tokens, "teacher": teacher, "routes": routes, "piece_start": piece_start, "valid_mask": valid_mask, "lower_gain": lower_gain, "lower_bias": lower_bias, "lower_triple": lower_triple, "lower_output": lower_output, "feed_gain": feed_gain, "feed_bias": feed_bias, "feed_expand": feed_expand, "feed_shrink": feed_shrink, "upper_gain": upper_gain, "upper_bias": upper_bias, "upper_triple": upper_triple, "upper_output": upper_output, "mixer_gain": mixer_gain, "mixer_bias": mixer_bias, "router": router, "expert_expand": expert_expand, "expert_shrink": expert_shrink}


@jax.custom_vjp
def low(v):
    return lax.optimization_barrier(v.astype(jnp.bfloat16)).astype(jnp.float32)

@jax.custom_vjp
def low_back(v):
    return v

def low_keep(v):
    return (low(v), None)

def low_pass(kept, grad):
    return (grad,)

def back_keep(v):
    return (v, None)

def back_low(kept, grad):
    return (low(grad),)
low.defvjp(low_keep, low_pass)
low_back.defvjp(back_keep, back_low)
HIGH = lax.Precision.HIGHEST

def layer_norm(values, norm_gain, norm_bias):
    centered = values - lax.optimization_barrier(jnp.mean(values, axis=-1, keepdims=True))
    spread = lax.optimization_barrier(jnp.mean(centered * centered, axis=-1, keepdims=True))
    return centered * lax.rsqrt(spread + 1e-05) * norm_gain + norm_bias

def gelu_tanh(values):
    return jax.nn.gelu(values, approximate=True)

def attention_block(stream, norm_gain, norm_bias, triple, output, allowed):
    groups = stream.shape[0]
    normed = low(layer_norm(stream, norm_gain, norm_bias))
    packed = low_back(low(jnp.einsum('gld,de->gle', normed, triple, precision=HIGH)))
    packed = packed.reshape(groups, LEN, 3, H, HD)
    queries = packed[:, :, 0]
    key_rows = packed[:, :, 1]
    value_rows = packed[:, :, 2]
    scores = low_back(jnp.einsum('gqhd,gkhd->ghqk', queries, key_rows, precision=HIGH) * HD ** (-0.5))
    scores = jnp.where(allowed[:, None], scores, -1e+30)
    weights = low(jax.nn.softmax(scores, axis=-1))
    context = low_back(low(jnp.einsum('ghqk,gkhd->gqhd', weights, value_rows, precision=HIGH)))
    context = context.reshape(groups, LEN, H * HD)
    return stream + low_back(jnp.einsum('gld,de->gle', context, output, precision=HIGH))

def feed_block(stream, norm_gain, norm_bias, expand, shrink):
    normed = low(layer_norm(stream, norm_gain, norm_bias))
    inner_pre = low_back(jnp.einsum('gld,df->glf', normed, expand, precision=HIGH))
    active = low(gelu_tanh(inner_pre))
    return stream + low_back(jnp.einsum('glf,fd->gld', active, shrink, precision=HIGH))

def mixture_block(stream, norm_gain, norm_bias, router, expand, shrink, onehot, dispatch, valid_block, expert_share, balance_scale):
    groups = stream.shape[0]
    normed = low(layer_norm(stream, norm_gain, norm_bias))
    logits = jnp.einsum('gld,de->gle', normed, router, precision=HIGH)
    gate_value = jax.nn.sigmoid(lax.optimization_barrier(jnp.sum(logits * onehot, axis=-1)))
    expert_probs = jax.nn.softmax(logits, axis=-1)
    routed = low_back(normed)
    buffer = jnp.einsum('gsl,gld->gsd', dispatch, routed, precision=HIGH).reshape(groups, EXPERTS, CAP, D)
    inner_pre = low_back(jnp.einsum('gecd,edf->gecf', buffer, expand, precision=HIGH))
    active = low(gelu_tanh(inner_pre))
    result = low_back(low(jnp.einsum('gecf,efd->gecd', active, shrink, precision=HIGH)))
    result = result.reshape(groups, EXPERTS * CAP, D)
    combined = jnp.einsum('gsl,gsd->gld', dispatch, result, precision=HIGH)
    balance = balance_scale * jnp.sum(valid_block[..., None] * expert_probs * expert_share)
    return (stream + gate_value[..., None] * combined, balance)

def objective(params, token_block, teacher_block, allowed, onehot, dispatch, valid_block, expert_share, loss_ratio, balance_scale):
    lower_gain, lower_bias, lower_triple, lower_output, feed_gain, feed_bias, feed_expand, feed_shrink, upper_gain, upper_bias, upper_triple, upper_output, mixer_gain, mixer_bias, router, expert_expand, expert_shrink = params
    stream = attention_block(token_block, lower_gain, lower_bias, lower_triple, lower_output, allowed)
    stream = feed_block(stream, feed_gain, feed_bias, feed_expand, feed_shrink)
    stream = attention_block(stream, upper_gain, upper_bias, upper_triple, upper_output, allowed)
    final, balance = mixture_block(stream, mixer_gain, mixer_bias, router, expert_expand, expert_shrink, onehot, dispatch, valid_block, expert_share, balance_scale)
    difference = final - teacher_block
    distill = loss_ratio * (0.5 * jnp.sum(valid_block[..., None] * difference * difference))
    return (distill + balance, (final, distill))

def reference(tokens, teacher, routes, piece_start, valid_mask, lower_gain, lower_bias, lower_triple, lower_output, feed_gain, feed_bias, feed_expand, feed_shrink, upper_gain, upper_bias, upper_triple, upper_output, mixer_gain, mixer_bias, router, expert_expand, expert_shrink):
    params = tuple((weight.astype(jnp.float32) for weight in (lower_gain, lower_bias, lower_triple, lower_output, feed_gain, feed_bias, feed_expand, feed_shrink, upper_gain, upper_bias, upper_triple, upper_output, mixer_gain, mixer_bias, router, expert_expand, expert_shrink)))
    valid_all = valid_mask.astype(jnp.float32)
    numbers = jnp.arange(EXPERTS, dtype=jnp.int32)
    route_all = routes[..., 0]
    onehot_all = (route_all[..., None] == numbers).astype(jnp.float32)
    valid_count = jnp.sum(valid_all)
    expert_share = lax.optimization_barrier(jnp.sum(valid_all[..., None] * onehot_all, axis=(0, 1))) / valid_count
    loss_ratio = TOKENS / valid_count
    balance_scale = TOKENS * D * 0.1 * EXPERTS / valid_count
    position = jnp.arange(LEN, dtype=jnp.int32)
    group_size = max((size for size in range(1, SEQS + 1) if SEQS % size == 0 and size * LEN <= 4096))
    steps_total = SEQS // group_size
    slot_numbers = jnp.arange(EXPERTS * CAP, dtype=jnp.int32)

    def one_group(carry, inputs):
        grads_sum, loss_sum = carry
        token_block, teacher_block, route_block, start_block, valid_block = inputs
        inside = (position[None, :] >= start_block[:, None]) & (position[None, :] < start_block[:, None] + PIECE)
        allowed = (position[None, :, None] >= position[None, None, :]) | inside[:, :, None] & inside[:, None, :]
        chosen = (route_block[..., None] == numbers).astype(jnp.int32)
        slot_index = lax.optimization_barrier(jnp.sum((jnp.cumsum(chosen, axis=1) - 1) * chosen, axis=-1))
        target = route_block * CAP + slot_index
        dispatch = (slot_numbers[None, :, None] == target[:, None, :]).astype(jnp.float32)
        onehot = chosen.astype(jnp.float32)
        teacher32 = teacher_block.astype(jnp.float32)

        def closed(weights_in, stream_in):
            return objective(weights_in, stream_in, teacher32, allowed, onehot, dispatch, valid_block, expert_share, loss_ratio, balance_scale)
        loss_value, pullback, aux = jax.vjp(closed, params, token_block.astype(jnp.float32), has_aux=True)
        final, distill = aux
        grad_params, grad_tokens = pullback(jnp.ones_like(loss_value))
        grads_sum = jax.tree.map(jnp.add, grads_sum, grad_params)
        return ((grads_sum, loss_sum + distill), (final.astype(jnp.bfloat16), grad_tokens))
    zero_grads = jax.tree.map(jnp.zeros_like, params)
    blocked = (tokens.reshape(steps_total, group_size, LEN, D), teacher.reshape(steps_total, group_size, LEN, D), route_all.reshape(steps_total, group_size, LEN), piece_start.reshape(steps_total, group_size), valid_all.reshape(steps_total, group_size, LEN))
    (grads, loss_total), (finals, token_grads) = lax.scan(one_group, (zero_grads, jnp.zeros((), jnp.float32)), blocked)
    states = finals.reshape(SEQS, LEN, D)
    tokens_delta = token_grads.reshape(SEQS, LEN, D)
    mean_loss = loss_total / (TOKENS * D)
    return (states, tokens_delta, grads[0], grads[1], grads[2], grads[3], grads[4], grads[5], grads[6], grads[7], grads[8], grads[9], grads[10], grads[11], grads[12], grads[13], grads[14], grads[15], grads[16], mean_loss)
```

```python
import jax
import jax.numpy as jnp
from jax import lax
from jax.sharding import PartitionSpec as P

H = 12
HD = 64
HIGH = lax.Precision.HIGHEST
AXES = ("dp", "expert")
F32 = jnp.float32
BF16 = jnp.bfloat16


def place():
    depth = lax.axis_size("dp") // 2
    row = lax.axis_index("dp")
    return depth, lax.axis_size("expert"), row // 2, row % 2, lax.axis_index("expert")


def pairs(target):
    depth, across = lax.axis_size("dp") // 2, lax.axis_size("expert")
    out = []
    for z in range(depth):
        for c in range(2):
            for e in range(across):
                to = target(z, c, e)
                if to is not None and 0 <= to[0] < depth:
                    out.append(((z * 2 + c) * across + e, (to[0] * 2 + to[1]) * across + to[2]))
    return out


def hop(values, target):
    return lax.ppermute(values, AXES, pairs(target))


def swap_cores(values):
    return hop(values, lambda z, c, e: (z, 1 - c, e))


def first_side(values):
    return hop(values, lambda z, c, e: (z, c, e ^ (1 + c)))


def second_side(values):
    return hop(values, lambda z, c, e: (z, c, e ^ (2 - c)))


def gather_line(own):
    depth, _, z, _, _ = place()
    ups, downs = [own], [own]
    for _ in range(depth - 1):
        ups.append(hop(ups[-1], lambda z, c, e: (z + 1, c, e)))
        downs.append(hop(downs[-1], lambda z, c, e: (z - 1, c, e)))
    slots = []
    for j in range(depth):
        value = own
        for t in range(1, j + 1):
            value = jnp.where(z == j - t, downs[t], value)
        for t in range(1, depth - j):
            value = jnp.where(z == j + t, ups[t], value)
        slots.append(value)
    return jnp.stack(slots)


def gather_sides(line, buffer):
    depth, across, z, c, e = place()
    if across != 4:
        whole = lax.all_gather(line, "expert", axis=1)
        both = jnp.stack([whole, swap_cores(whole)])
        both = jnp.where(c == 0, both, both[::-1])
        return jnp.moveaxis(both, 0, 1)
    one = first_side(line)
    two, three = second_side(line), second_side(one)
    there = (e, e ^ (1 + c), e ^ (2 - c), e ^ 3)
    over = (e, e ^ (2 - c), e ^ (1 + c), e ^ 3)
    for part, mine, theirs in zip((line, one, two, three), there, over):
        buffer = lax.dynamic_update_slice(buffer, part[:, None, None], (0, c, mine, 0, 0))
        buffer = lax.dynamic_update_slice(
            buffer, swap_cores(part)[:, None, None], (0, 1 - c, theirs, 0, 0)
        )
    return buffer


def gather_dense(own):
    depth, across, _, _, _ = place()
    rows, columns = own.shape
    buffer = jnp.zeros((depth, 2, across, rows, columns), own.dtype)
    return gather_sides(gather_line(own), buffer).reshape(-1, columns)


def add(first, second):
    return (first.astype(F32) + second.astype(F32)).astype(BF16)


def scatter_line(line):
    depth, _, z, _, _ = place()
    total = lax.dynamic_index_in_dim(line, z, 0, False).astype(F32)
    for sign in (1, -1):
        come = None
        for k in range(depth - 1, 0, -1):
            at = jnp.clip(z + sign * k, 0, depth - 1)
            part = lax.dynamic_index_in_dim(line, at, 0, False)
            if come is not None:
                part = add(part, come)
            come = hop(
                part,
                lambda z, c, e: (z + sign, c, e) if 0 <= z + sign * k < depth else None,
            )
        total = total + come.astype(F32)
    return total


def scatter_dense(grad):
    depth, across, z, c, e = place()
    columns = grad.shape[1]
    grad = grad.reshape(depth, 2, across, -1, columns)
    mine = lax.dynamic_index_in_dim(grad, c, 1, False)
    other = swap_cores(lax.dynamic_index_in_dim(grad, 1 - c, 1, False))
    if across != 4:
        line = lax.psum_scatter(add(mine, other), "expert", scatter_dimension=1, tiled=True)
        return scatter_line(line[:, 0])
    pick = lambda a, at: lax.dynamic_index_in_dim(a, at, 1, False)
    half = lambda at: add(pick(mine, at), pick(other, at))
    near = add(half(e), second_side(half(e ^ (2 - c))))
    far = add(half(e ^ (1 + c)), second_side(half(e ^ 3)))
    return scatter_line(add(near, first_side(far)))


def total_over_devices(value):
    depth, across, _, _, _ = place()
    value = value + swap_cores(value)
    if across & (across - 1) or depth & (depth - 1):
        value = lax.psum(value, "expert")
        values = lax.all_gather(value, "dp")[::2]
        return jnp.sum(values, axis=0)
    step = 1
    while step < across:
        value = value + hop(value, lambda z, c, e: (z, c, e ^ step))
        step *= 2
    step = 1
    while step < depth:
        value = value + hop(value, lambda z, c, e: (z ^ step, c, e))
        step *= 2
    return value


def exchange(rows):
    return lax.all_to_all(rows, "expert", split_axis=0, concat_axis=0, tiled=True)


def dot(a, b):
    return jnp.dot(a, b, preferred_element_type=F32)


def dot_nt(a, b):
    return lax.dot_general(a, b, (((1,), (1,)), ((), ())), preferred_element_type=F32)


def dot_tn(a, b):
    return lax.dot_general(a, b, (((0,), (0,)), ((), ())), preferred_element_type=F32)


def norm(values, gain, bias):
    centered = values - jnp.mean(values, axis=-1, keepdims=True)
    spread = jnp.mean(centered * centered, axis=-1, keepdims=True)
    return centered * lax.rsqrt(spread + 1e-05) * gain + bias


def norm_backward(stream, gain, bias, grad):
    _, back = jax.vjp(norm, stream, gain, bias)
    return back(grad)


def gelu(values):
    return jax.nn.gelu(values, approximate=True)


def gelu_backward(values, grad):
    _, back = jax.vjp(gelu, values)
    return back(grad)[0]


def scores_of(packed, allowed):
    scores = jnp.einsum("mqhd,mkhd->mhqk", packed[:, :, 0], packed[:, :, 1], preferred_element_type=F32)
    return jnp.where(allowed[:, None], scores * HD ** (-0.5), -1e30)


def attend_forward(stream, gain, bias, triple, output, allowed):
    tokens, features = stream.shape
    groups, length, _ = allowed.shape
    normed = norm(stream, gain, bias).astype(BF16)
    packed = dot(normed, triple).astype(BF16).reshape(groups, length, 3, H, HD)
    scores = scores_of(packed, allowed)
    highest = jnp.max(scores, axis=-1, keepdims=True)
    exponent = jnp.exp(scores - highest)
    row_total = jnp.sum(exponent, axis=-1, keepdims=True)
    weights = (exponent / row_total).astype(BF16)
    logsum = highest + jnp.log(row_total)
    context = jnp.einsum("mhqk,mkhd->mqhd", weights, packed[:, :, 2], preferred_element_type=F32)
    context = context.astype(BF16).reshape(tokens, features)
    return stream + dot(context, output), (normed, packed, logsum, context)


def attend_backward(stream, gain, bias, triple, output, allowed, stored, upstream):
    normed, packed, logsum, context = stored
    tokens, features = stream.shape
    groups, length, _ = allowed.shape
    scale = HD ** (-0.5)
    branch = upstream.astype(BF16)
    output_grad = dot_tn(context, branch).astype(BF16)
    context_grad = dot_nt(branch, output).astype(BF16).reshape(groups, length, H, HD)
    probs = jnp.exp(scores_of(packed, allowed) - logsum)
    value_grad = jnp.einsum("mhqk,mqhd->mkhd", probs.astype(BF16), context_grad, preferred_element_type=F32)
    prob_grad = jnp.einsum("mqhd,mkhd->mhqk", context_grad, packed[:, :, 2], preferred_element_type=F32)
    score_grad = (probs * (prob_grad - jnp.sum(probs * prob_grad, axis=-1, keepdims=True))).astype(BF16)
    query_grad = jnp.einsum("mhqk,mkhd->mqhd", score_grad, packed[:, :, 1], preferred_element_type=F32) * scale
    key_grad = jnp.einsum("mhqk,mqhd->mkhd", score_grad, packed[:, :, 0], preferred_element_type=F32) * scale
    packed_grad = jnp.stack([query_grad, key_grad, value_grad], axis=2).astype(BF16)
    packed_grad = packed_grad.reshape(tokens, 3 * features)
    triple_grad = dot_tn(normed, packed_grad).astype(BF16)
    back, gain_grad, bias_grad = norm_backward(stream, gain, bias, dot_nt(packed_grad, triple))
    return upstream + back, gain_grad, bias_grad, triple_grad, output_grad


def feed_forward(stream, gain, bias, expand, shrink):
    normed = norm(stream, gain, bias).astype(BF16)
    inner = dot(normed, expand)
    active = gelu(inner).astype(BF16)
    return stream + dot(active, shrink), (normed, inner)


def feed_backward(stream, gain, bias, expand, shrink, stored, upstream):
    normed, inner = stored
    branch = upstream.astype(BF16)
    shrink_grad = dot_tn(gelu(inner).astype(BF16), branch).astype(BF16)
    inner_grad = gelu_backward(inner, dot_nt(branch, shrink)).astype(BF16)
    expand_grad = dot_tn(normed, inner_grad).astype(BF16)
    back, gain_grad, bias_grad = norm_backward(stream, gain, bias, dot_nt(inner_grad, expand))
    return upstream + back, gain_grad, bias_grad, expand_grad, shrink_grad


def body(
    tokens,
    teacher,
    routes,
    piece_start,
    valid_mask,
    lower_gain,
    lower_bias,
    lower_triple,
    lower_output,
    feed_gain,
    feed_bias,
    feed_expand,
    feed_shrink,
    upper_gain,
    upper_bias,
    upper_triple,
    upper_output,
    mixer_gain,
    mixer_bias,
    router,
    expert_expand,
    expert_shrink,
):
    count, length, features = tokens.shape
    local = count * length
    experts = router.shape[1]
    share_rows = router.shape[0]
    devices = lax.axis_size("dp") * lax.axis_size("expert")
    capacity = max(2, 2 * length // experts)
    total_tokens = local * devices
    valid = valid_mask.astype(F32)
    route = routes[..., 0]
    chosen = (route[..., None] == jnp.arange(experts, dtype=jnp.int32)).astype(F32)

    counts = jnp.concatenate([jnp.sum(valid[..., None] * chosen, axis=1), jnp.sum(valid, axis=1)[:, None]], axis=1)
    counts = jnp.pad(counts.astype(BF16), ((0, share_rows - count), (0, 0)))
    vectors = [lower_gain, lower_bias, feed_gain, feed_bias, upper_gain, upper_bias, mixer_gain, mixer_bias]
    extra = jnp.concatenate([jnp.stack(vectors, axis=1), router, counts], axis=1)
    extra_width = -(-extra.shape[1] // 128) * 128
    extra = jnp.pad(extra, ((0, 0), (0, extra_width - extra.shape[1])))

    lower = gather_dense(jnp.concatenate([lower_triple, lower_output, extra], axis=1))
    middle = gather_dense(jnp.concatenate([feed_expand, upper_triple, upper_output], axis=1))
    shrink_full = gather_dense(feed_shrink)
    expert_in = lax.all_gather(expert_expand[0], "dp", axis=0, tiled=True)
    expert_out = lax.all_gather(expert_shrink[0], "dp", axis=0, tiled=True)
    wide = 3 * features
    triple_one, output_one, extra_full = lower[:, :wide], lower[:, wide : wide + features], lower[:, wide + features :]
    inner_width = feed_expand.shape[1]
    expand_full = middle[:, :inner_width]
    triple_two = middle[:, inner_width : inner_width + wide]
    output_two = middle[:, inner_width + wide :]
    rows = extra_full[:, :8].astype(F32).T
    gains = [rows[k] for k in range(8)]
    router_full = extra_full[:, 8 : 8 + experts]
    sums = extra_full.reshape(devices, share_rows, -1)[:, :count, 8 + experts : 9 + 2 * experts]
    sums = jnp.sum(sums.astype(F32), axis=(0, 1))
    valid_total = sums[experts]
    expert_share = sums[:experts] / valid_total
    loss_ratio = total_tokens / valid_total
    balance_scale = total_tokens * features * 0.1 * experts / valid_total

    position = jnp.arange(length, dtype=jnp.int32)
    inside = (position >= piece_start[:, None]) & (position < piece_start[:, None] + length // 4)
    allowed = (position[:, None] >= position[None, :]) | (inside[:, :, None] & inside[:, None, :])

    earlier = (position[:, None] > position[None, :]).astype(BF16)
    before = jnp.einsum("qk,mke->mqe", earlier, chosen.astype(BF16), preferred_element_type=F32)
    slot = jnp.sum(before * chosen, axis=-1).astype(jnp.int32)
    target = route * (count * capacity) + jnp.arange(count, dtype=jnp.int32)[:, None] * capacity + slot
    places = jnp.arange(experts * count * capacity, dtype=jnp.int32)
    dispatch = (places[:, None] == target.reshape(-1)[None, :]).astype(BF16)
    chosen = chosen.reshape(local, experts)
    valid = valid.reshape(local, 1)

    stream_in = tokens.reshape(local, features).astype(F32)
    stream_one, stored_one = attend_forward(stream_in, gains[0], gains[1], triple_one, output_one, allowed)
    stream_two, stored_two = feed_forward(stream_one, gains[2], gains[3], expand_full, shrink_full)
    stream_three, stored_three = attend_forward(stream_two, gains[4], gains[5], triple_two, output_two, allowed)
    normed = norm(stream_three, gains[6], gains[7]).astype(BF16)
    arrived = exchange(dot(dispatch, normed).astype(BF16))
    logits = dot(normed, router_full)
    gate = jax.nn.sigmoid(jnp.sum(logits * chosen, axis=1, keepdims=True))
    expert_probs = jax.nn.softmax(logits, axis=1)
    inner = dot(arrived, expert_in)
    active = gelu(inner).astype(BF16)
    returned = exchange(dot(active, expert_out).astype(BF16))
    combined = dot_tn(dispatch, returned)
    final = stream_three + gate * combined
    difference = final - teacher.reshape(local, features).astype(F32)
    squared = 0.5 * jnp.sum(valid * difference * difference)
    upstream = loss_ratio * valid * difference

    gate_grad = jnp.sum(upstream * combined, axis=1, keepdims=True)
    landed = exchange(dot(dispatch, (gate * upstream).astype(BF16)).astype(BF16))
    inner_grad = gelu_backward(inner, dot_nt(landed, expert_out)).astype(BF16)
    rows_grad = exchange(dot_nt(inner_grad, expert_in).astype(BF16))
    expert_out_grad = dot_tn(active, landed).astype(BF16)
    expert_in_grad = dot_tn(arrived, inner_grad).astype(BF16)
    expert_out_grad = lax.psum_scatter(expert_out_grad, "dp", scatter_dimension=0, tiled=True)
    expert_in_grad = lax.psum_scatter(expert_in_grad, "dp", scatter_dimension=0, tiled=True)
    routed_grad = dot_tn(dispatch, rows_grad)
    logits_grad = chosen * (gate_grad * gate * (1.0 - gate)) + balance_scale * valid * expert_probs * (
        expert_share - jnp.sum(expert_probs * expert_share, axis=1, keepdims=True)
    )
    router_grad = lax.dot_general(normed.astype(F32), logits_grad, (((0,), (0,)), ((), ())), precision=HIGH)
    normed_grad = routed_grad + lax.dot_general(
        logits_grad, router_full.astype(F32), (((1,), (1,)), ((), ())), precision=HIGH
    )
    back, mixer_gain_grad, mixer_bias_grad = norm_backward(stream_three, gains[6], gains[7], normed_grad)
    grad_three = upstream + back

    grad_two, upper_gain_grad, upper_bias_grad, triple_two_grad, output_two_grad = attend_backward(
        stream_two, gains[4], gains[5], triple_two, output_two, allowed, stored_three, grad_three
    )
    upper_part = scatter_dense(jnp.concatenate([triple_two_grad, output_two_grad], axis=1))
    grad_one, feed_gain_grad, feed_bias_grad, expand_grad, shrink_grad = feed_backward(
        stream_one, gains[2], gains[3], expand_full, shrink_full, stored_two, grad_two
    )
    shrink_part = scatter_dense(shrink_grad)
    expand_part = scatter_dense(expand_grad)
    grad_in, lower_gain_grad, lower_bias_grad, triple_one_grad, output_one_grad = attend_backward(
        stream_in, gains[0], gains[1], triple_one, output_one, allowed, stored_one, grad_one
    )
    small = [
        lower_gain_grad,
        lower_bias_grad,
        feed_gain_grad,
        feed_bias_grad,
        upper_gain_grad,
        upper_bias_grad,
        mixer_gain_grad,
        mixer_bias_grad,
    ]
    small = jnp.concatenate([jnp.stack(small, axis=1), router_grad], axis=1).astype(BF16)
    small = jnp.pad(small, ((0, 0), (0, extra_width - small.shape[1])))
    lower_part = scatter_dense(jnp.concatenate([triple_one_grad, output_one_grad, small], axis=1))
    small = lower_part[:, wide + features :]

    squared_total = total_over_devices(jnp.full((8, 128), squared))[0, 0]
    mean_loss = loss_ratio * squared_total / (total_tokens * features)
    return (
        final.astype(BF16).reshape(tokens.shape),
        grad_in.reshape(tokens.shape),
        small[:, 0],
        small[:, 1],
        lower_part[:, :wide],
        lower_part[:, wide : wide + features],
        small[:, 2],
        small[:, 3],
        expand_part,
        shrink_part,
        small[:, 4],
        small[:, 5],
        upper_part[:, :wide],
        upper_part[:, wide:],
        small[:, 6],
        small[:, 7],
        small[:, 8 : 8 + experts],
        expert_in_grad.astype(F32)[None],
        expert_out_grad.astype(F32)[None],
        mean_loss,
    )


def solution(mesh):
    both = ("dp", "expert")
    token = P(both, None, None)
    vector = P(both)
    matrix = P(both, None)
    expert = P("expert", "dp", None)
    dense = (vector, vector, matrix, matrix, vector, vector, matrix, matrix)
    weights = dense + (vector, vector, matrix, matrix, vector, vector, matrix, expert, expert)
    return jax.shard_map(
        body,
        mesh=mesh,
        in_specs=(token, token, token, vector, matrix) + weights,
        out_specs=(token, token) + weights + (P(),),
        check_vma=False,
    )
```

```python
import math

import jax
import jax.numpy as jnp
from jax import lax
from jax.experimental import pallas as pl
from jax.experimental.pallas import tpu as pltpu
from jax.sharding import PartitionSpec as P

HD = 64
AXES = ("dp", "expert")
F32 = jnp.float32
BF16 = jnp.bfloat16


def place():
    depth = lax.axis_size("dp") // 2
    row = lax.axis_index("dp")
    return depth, lax.axis_size("expert"), row // 2, row % 2, lax.axis_index("expert")


def pairs(target):
    depth, across = lax.axis_size("dp") // 2, lax.axis_size("expert")
    out = []
    for z in range(depth):
        for c in range(2):
            for e in range(across):
                to = target(z, c, e)
                if to is not None and 0 <= to[0] < depth:
                    out.append(((z * 2 + c) * across + e, (to[0] * 2 + to[1]) * across + to[2]))
    return out


def hop(values, target):
    return lax.ppermute(values, AXES, pairs(target))


def swap_cores(values):
    return hop(values, lambda z, c, e: (z, 1 - c, e))


def first_side(values):
    return hop(values, lambda z, c, e: (z, c, e ^ (1 + c)))


def second_side(values):
    return hop(values, lambda z, c, e: (z, c, e ^ (2 - c)))


def after(value, *others):
    return lax.optimization_barrier((value, *others))[0]


def shift(values, by):
    depth = place()[0]
    return hop(values, lambda z, c, e: ((z + by) % depth, c, e))


def gather_line(own):
    return jnp.stack([own] + [shift(own, k) for k in range(1, place()[0])])


def gather_sides(line):
    if place()[1] != 4:
        return [lax.all_gather(line, "expert", axis=1)]
    one = first_side(line)
    return [line, one, second_side(line), second_side(one)]


def gather_cores(parts):
    parts = [*parts, *(swap_cores(p) for p in parts)]
    return [p.reshape(-1, p.shape[-1]) for p in parts]


def order(rows):
    depth, across, z, c, e = place()
    k = jnp.arange(depth, dtype=jnp.int32)
    layer = (z - k) % depth
    if across == 4:
        there = jnp.stack([e, e ^ (1 + c), e ^ (2 - c), e ^ 3])
        over = jnp.stack([e, e ^ (2 - c), e ^ (1 + c), e ^ 3])
    else:
        there = over = jnp.arange(across, dtype=jnp.int32)
    first = (layer * 2 + c)[None, :] * across + there[:, None]
    second = (layer * 2 + 1 - c)[None, :] * across + over[:, None]
    if across != 4:
        first, second = first.T, second.T
    return jnp.concatenate([first.reshape(-1), second.reshape(-1)]) * rows


def add(first, second):
    return (first.astype(F32) + second.astype(F32)).astype(BF16)


def scatter_line(line):
    return [line[0]] + [shift(line[k], -k) for k in range(1, place()[0])]


def total(parts):
    return sum(p.astype(F32) for p in parts[1:]) + parts[0].astype(F32)


def scatter_cores(mine, other):
    depth, across, _, _, _ = place()
    other = swap_cores(other)
    if across != 4:
        return [add(mine, other).reshape(depth, across, -1, mine.shape[1])]
    half = mine.shape[0] // 2
    return [add(mine[:half], other[:half]), add(mine[half:], other[half:])]


def scatter_far(parts):
    return [parts[0], second_side(parts[1])] if len(parts) == 2 else parts


def scatter_near(parts):
    depth = place()[0]
    if len(parts) == 1:
        return lax.psum_scatter(parts[0], "expert", scatter_dimension=1, tiled=True)[:, 0]
    half = parts[0].shape[0] // 2
    mine, come = parts
    line = add(add(mine[:half], come[:half]), first_side(add(mine[half:], come[half:])))
    return line.reshape(depth, -1, line.shape[1])


def total_hops():
    depth, across, _, _, _ = place()
    if across & (across - 1) or depth & (depth - 1):
        return None
    hops = [lambda z, c, e: (z, 1 - c, e)]
    step = 1
    while step < across:
        hops.append(lambda z, c, e, step=step: (z, c, e ^ step))
        step *= 2
    step = 1
    while step < depth:
        hops.append(lambda z, c, e, step=step: (z ^ step, c, e))
        step *= 2
    return hops


def exchange(blocks):
    return [blocks[0]] + [
        hop(blocks[k], lambda z, c, e: (z, c, e ^ k)) for k in range(1, len(blocks))
    ]


LIMIT = 60 * 1024 * 1024
LIGHT = 1000


def cost(flops, moved, light=1):
    return pl.CostEstimate(flops=flops // light, bytes_accessed=moved // light, transcendentals=0)


WHOLE = pl.BlockSpec(memory_space=pltpu.VMEM)
SCALAR = pl.BlockSpec(memory_space=pltpu.SMEM)


def dot(a, b):
    return jnp.dot(a, b, preferred_element_type=F32)


def dot_nt(a, b):
    return lax.dot_general(a, b, (((1,), (1,)), ((), ())), preferred_element_type=F32)


def dot_tn(a, b):
    return lax.dot_general(a, b, (((0,), (0,)), ((), ())), preferred_element_type=F32)


def call(kernel, outs, ins, flops, grid=(), in_specs=None, out_specs=None, scratch=(), light=1):
    moved = sum(a.size * a.dtype.itemsize for a in (*ins, *outs))
    return pl.pallas_call(
        kernel,
        out_shape=outs,
        grid=grid,
        in_specs=in_specs or [WHOLE] * len(ins),
        out_specs=out_specs or [WHOLE] * len(outs),
        scratch_shapes=scratch,
        compiler_params=pltpu.CompilerParams(vmem_limit_bytes=LIMIT),
        cost_estimate=cost(flops, moved, light),
    )(*ins)


ANYWHERE = pl.BlockSpec(memory_space=pl.ANY)


def start_parts(parts, whole, sems, first=0):
    copies, at = [], 0
    for k, part in enumerate(parts):
        rows = part.shape[0]
        copies.append(pltpu.make_async_copy(part.at[:, first : first + whole.shape[1]], whole.at[at : at + rows], sems.at[k]))
        at += rows
    for copy in copies:
        copy.start()

    def wait():
        for copy in copies:
            copy.wait()

    return wait


def start_blocks(parts, places, whole, sems):
    count = places.shape[0] // len(parts)
    copies = []
    for k, part in enumerate(parts):
        rows = part.shape[0] // count
        for b in range(count):
            at = pl.multiple_of(places[k * count + b], 16)
            copies.append(
                pltpu.make_async_copy(
                    part.at[b * rows : (b + 1) * rows], whole.at[pl.ds(at, rows)], sems.at[k * count + b]
                )
            )
    for copy in copies:
        copy.start()

    def wait():
        for copy in copies:
            copy.wait()

    return wait


def mixed(values, mix):
    return dot(values, mix).astype(BF16)


def unmixed(values, mix):
    high = values.astype(BF16)
    low = (values - high.astype(F32)).astype(BF16)
    return dot_nt(low, mix) + dot_nt(high, mix)


def shaped(shape, dtype):
    return jax.ShapeDtypeStruct(shape, dtype)


def normalize(x):
    centered = x - jnp.mean(x, axis=-1, keepdims=True)
    scale = lax.rsqrt(jnp.mean(centered * centered, axis=-1, keepdims=True) + 1e-05)
    return centered * scale, scale


def norm_back(x, gain, grad, gains_ref, upstream):
    unit, scale = normalize(x)
    gains_ref[0:1, :] = jnp.sum(grad * unit, axis=0, keepdims=True)
    gains_ref[1:2, :] = jnp.sum(grad, axis=0, keepdims=True)
    inner = grad * gain
    middle = jnp.mean(inner, axis=-1, keepdims=True)
    tilt = jnp.mean(inner * unit, axis=-1, keepdims=True)
    return upstream + scale * (inner - middle - unit * tilt)


ROOT = math.sqrt(2.0 / math.pi)


def gelu(x):
    return 0.5 * x * (1.0 + jnp.tanh(ROOT * (x + 0.044715 * (x * x * x))))


def gelu_both(x):
    square = x * x
    slope = jnp.tanh(ROOT * x * (1.0 + 0.044715 * square))
    half = 0.5 * (1.0 + slope)
    return x * half, half + 0.5 * x * (1.0 - slope * slope) * (ROOT * (1.0 + 0.134145 * square))


def allowed_pair(start, length):
    row = lax.broadcasted_iota(jnp.int32, (2 * length, length), 0)
    row = jnp.where(row >= length, row - length, row)
    column = lax.broadcasted_iota(jnp.int32, (2 * length, length), 1)
    piece = length // 4
    inside = (row >= start) & (row < start + piece) & (column >= start) & (column < start + piece)
    return (column <= row) | inside


def apart(pair):
    low = lax.broadcasted_iota(jnp.int32, pair.shape, 1) < HD
    zero = jnp.zeros_like(pair)
    return jnp.concatenate([jnp.where(low, pair, zero), jnp.where(low, zero, pair)], axis=0)


def together(stacked):
    half = stacked.shape[0] // 2
    low = lax.broadcasted_iota(jnp.int32, (half, stacked.shape[1]), 1) < HD
    return jnp.where(low, stacked[:half], stacked[half:])


def softmax_pair(queries, keys, allowed):
    scores = jnp.where(allowed, dot_nt(queries, keys) * HD ** (-0.5), -1e30)
    exponent = jnp.exp(scores - jnp.max(scores, axis=-1, keepdims=True))
    return exponent / jnp.sum(exponent, axis=-1, keepdims=True)


def attend_forward(at, stream, rows, parts, first, mix, start, length):
    tokens, features = stream.shape
    wide = 3 * features
    width = parts[0].shape[1] - first
    count = len(parts)

    def kernel(*refs):
        start_ref, stream_ref, mix_ref = refs[:3]
        part_refs = refs[3 : 3 + count]
        out_ref, normed_ref, packed_ref, context_ref = refs[-6:-2]
        rows_ref, weights_ref, sems = refs[-7 if rows is None else 3 + count], refs[-2], refs[-1]
        wait = start_parts(part_refs, weights_ref, sems, first)
        x = stream_ref[...].astype(F32)
        unit = normalize(x)[0]
        mix = mix_ref[...]
        wait()
        if rows is None:
            rows_ref[...] = lax.dot_general(
                weights_ref[:, wide + features :], mix, (((0,), (1,)), ((), ())), preferred_element_type=F32
            )
        normed = (unit * rows_ref[at : at + 1, :] + rows_ref[at + 1 : at + 2, :]).astype(BF16)
        normed = mixed(normed, mix)
        normed_ref[...] = normed
        for j in range(3):
            columns = slice(j * features, (j + 1) * features)
            packed_ref[:, columns] = dot(normed, weights_ref[:, columns]).astype(BF16)
        for s in range(tokens // length):
            allowed = allowed_pair(start_ref[s], length)
            here = slice(s * length, (s + 1) * length)
            for p in range(features // (2 * HD)):
                at_q, at_k, at_v = (slice(j * features + p * 2 * HD, j * features + (p + 1) * 2 * HD) for j in range(3))
                probs = softmax_pair(apart(packed_ref[here, at_q]), packed_ref[here, at_k], allowed)
                context_ref[here, at_q] = together(dot(probs.astype(BF16), packed_ref[here, at_v])).astype(BF16)
        context = mixed(context_ref[...], mix)
        context_ref[...] = context
        out_ref[...] = x + dot(context, weights_ref[:, wide : wide + features])

    outs = [
        shaped((tokens, features), F32),
        shaped((tokens, features), BF16),
        shaped((tokens, wide), BF16),
        shaped((tokens, features), BF16),
    ]
    ins = [start, stream, mix, *parts]
    specs = [SCALAR, WHOLE, WHOLE] + [ANYWHERE] * count
    if rows is None:
        outs = [shaped((width - wide - features, features), F32)] + outs
    else:
        ins, specs = ins + [rows], specs + [WHOLE]
    scratch = [
        pltpu.VMEM((features, width), BF16),
        pltpu.SemaphoreType.DMA((count,)),
    ]
    return call(kernel, outs, ins, 10 * tokens * features * features, (), specs, None, scratch)


def attend_backward(at, stream, rows, parts, first, mix, start, length, stored, upstream, extra=()):
    normed, packed, context = stored
    tokens, features = stream.shape
    wide = 3 * features
    width = parts[0].shape[1] - first
    small = width - wide - features if extra else 0
    count = len(parts)

    def kernel(*refs):
        start_ref = refs[0]
        part_refs = refs[1 : 1 + count]
        mix_ref, stream_ref, rows_ref, normed_ref, packed_ref, context_ref, up_ref = refs[1 + count : 8 + count]
        extra_refs = refs[8 + count : 8 + count + len(extra)]
        out_ref, mine_ref, other_ref, gains_ref, delta_ref, weights_ref, sems = refs[8 + count + len(extra) :]
        wait = start_parts(part_refs, weights_ref, sems, first)

        def put(columns, values):
            mine_ref[:, columns] = values[: features // 2].astype(BF16)
            other_ref[:, columns] = values[features // 2 :].astype(BF16)

        upstream = up_ref[...]
        branch = upstream.astype(BF16)
        mix = mix_ref[...]
        put(slice(wide, wide + features), dot_tn(context_ref[...], branch))
        wait()
        context_grad = dot_nt(branch, weights_ref[:, wide : wide + features]).astype(BF16)
        context_grad = dot_nt(context_grad, mix).astype(BF16)
        scale = HD ** (-0.5)
        for s in range(tokens // length):
            allowed = allowed_pair(start_ref[s], length)
            here = slice(s * length, (s + 1) * length)
            for p in range(features // (2 * HD)):
                at_q, at_k, at_v = (slice(j * features + p * 2 * HD, j * features + (p + 1) * 2 * HD) for j in range(3))
                queries, keys, values = apart(packed_ref[here, at_q]), packed_ref[here, at_k], packed_ref[here, at_v]
                probs = softmax_pair(queries, keys, allowed)
                out_grad = apart(context_grad[here, at_q])
                delta_ref[here, at_v] = dot_tn(probs.astype(BF16), out_grad).astype(BF16)
                prob_grad = dot_nt(out_grad, values)
                middle = jnp.sum(probs * prob_grad, axis=-1, keepdims=True)
                score_grad = (probs * (prob_grad - middle)).astype(BF16)
                delta_ref[here, at_q] = (together(dot(score_grad, keys)) * scale).astype(BF16)
                delta_ref[here, at_k] = (dot_tn(score_grad, queries) * scale).astype(BF16)
        turned = normed_ref[...].T
        normed_grad = jnp.zeros((tokens, features), F32)
        for j in range(3):
            columns = slice(j * features, (j + 1) * features)
            put(columns, dot(turned, delta_ref[:, columns]))
            normed_grad += dot_nt(delta_ref[:, columns], weights_ref[:, columns])
        out_ref[...] = norm_back(
            stream_ref[...].astype(F32), rows_ref[at : at + 1, :], unmixed(normed_grad, mix), gains_ref, upstream
        )
        if extra:
            mixer_ref, upper_ref, feed_ref = extra_refs
            lines = [gains_ref[0:2, :], feed_ref[0:2, :], upper_ref[0:2, :], mixer_ref[6:, :]]
            lines = dot(jnp.concatenate(lines, axis=0).astype(BF16), mix)
            put(slice(wide + features, width), lines.T)

    outs = [
        shaped((tokens, features), F32),
        shaped((features // 2, wide + features + small), BF16),
        shaped((features // 2, wide + features + small), BF16),
        shaped((8, features), F32),
    ]
    ins = [start, *parts, mix, stream, rows, normed, packed, context, upstream, *extra]
    specs = [SCALAR] + [ANYWHERE] * count + [WHOLE] * (7 + len(extra))
    scratch = [
        pltpu.VMEM((tokens, wide), BF16),
        pltpu.VMEM((features, width), BF16),
        pltpu.SemaphoreType.DMA((count,)),
    ]
    return call(kernel, outs, ins, 22 * tokens * features * features, (), specs, None, scratch, LIGHT)


def feed_forward(stream, rows, expand, shrink, places, mix, depth):
    tokens, features = stream.shape
    inner_width = sum(p.shape[0] for p in shrink)
    step = inner_width // depth
    count, blocks = len(expand), places.shape[0]

    def kernel(*refs):
        places_ref = refs[0]
        expand_refs, shrink_refs = refs[1 : 1 + count], refs[1 + count : -10]
        mix_ref, stream_ref, rows_ref, out_ref, normed_ref, inner_ref = refs[-10:-4]
        expand_ref, shrink_ref, expand_sems, shrink_sems = refs[-4:]
        j = pl.program_id(0)

        @pl.when(j == 0)
        def _():
            wait_expand = start_parts(expand_refs, expand_ref, expand_sems)
            wait_shrink = start_blocks(shrink_refs, places_ref, shrink_ref, shrink_sems)
            x = stream_ref[...]
            normed = (normalize(x)[0] * rows_ref[2:3, :] + rows_ref[3:4, :]).astype(BF16)
            normed_ref[...] = mixed(normed, mix_ref[...])
            out_ref[...] = x
            wait_expand()
            wait_shrink()

        here = pl.ds(pl.multiple_of(j * step, 128), step)
        inner = dot(normed_ref[...], expand_ref[:, here])
        inner_ref[...] = inner
        out_ref[...] += dot(gelu(inner).astype(BF16), shrink_ref[here, :])

    fixed = lambda a: pl.BlockSpec(a.shape, lambda j: (0, 0))
    outs = [
        shaped((tokens, features), F32),
        shaped((tokens, features), BF16),
        shaped((tokens, inner_width), F32),
    ]
    return call(
        kernel,
        outs,
        [places, *expand, *shrink, mix, stream, rows],
        4 * tokens * features * inner_width,
        (depth,),
        [SCALAR] + [ANYWHERE] * (count + len(shrink)) + [fixed(mix), fixed(stream), fixed(rows)],
        [fixed(outs[0]), fixed(outs[1]), pl.BlockSpec((tokens, step), lambda j: (0, j))],
        [
            pltpu.VMEM((features, inner_width), BF16),
            pltpu.VMEM((inner_width, features), BF16),
            pltpu.SemaphoreType.DMA((count,)),
            pltpu.SemaphoreType.DMA((blocks,)),
        ],
    )


def feed_backward(stream, rows, expand, shrink, places, mix, depth, stored, upstream):
    normed, inner = stored
    tokens, features = stream.shape
    inner_width = sum(p.shape[0] for p in shrink)
    step = inner_width // depth
    count, blocks = len(expand), places.shape[0]
    pieces = max(1, blocks // depth)
    piece = step // pieces
    side, half = max(1, pieces // 2), min(piece, step // 2)

    def kernel(places_ref, *refs):
        expand_refs, shrink_refs = refs[:count], refs[count:-19]
        mix_ref, stream_ref, rows_ref, normed_ref, inner_ref, up_ref = refs[-19:-13]
        out_ref, mine_ref, other_ref, near_ref, over_ref, gains_ref = refs[-13:-7]
        total_ref, turned_ref, active_ref, expand_ref, shrink_ref, expand_sems, shrink_sems = refs[-7:]
        j = pl.program_id(0)

        @pl.when(j == 0)
        def _():
            wait_shrink = start_blocks(shrink_refs, places_ref, shrink_ref, shrink_sems)
            wait_expand = start_parts(expand_refs, expand_ref, expand_sems)
            turned_ref[...] = normed_ref[...].T
            total_ref[...] = jnp.zeros_like(total_ref)
            wait_shrink()
            wait_expand()

        here = pl.ds(pl.multiple_of(j * step, 128), step)
        branch = up_ref[...].astype(BF16)
        active, slope = gelu_both(inner_ref[...])
        active_ref[...] = active.astype(BF16).T
        for p in range(pieces):
            start = 0
            if pieces > 1:
                layer = lax.rem(places_ref[0] // step - j + depth, depth)
                start = pl.multiple_of(places_ref[p * depth + layer] - j * step, 16)
            part = active_ref[pl.ds(start, piece), :]
            grad = dot(part, branch).astype(BF16)
            if pieces == 1:
                near_ref[0, 0] = grad[: step // 2]
                over_ref[0, 0] = grad[step // 2 :]
            elif p < pieces // 2:
                near_ref[p, 0] = grad
            else:
                over_ref[p - pieces // 2, 0] = grad
        inner_grad = (dot_nt(branch, shrink_ref[here, :]) * slope).astype(BF16)
        expand_grad = dot(turned_ref[...], inner_grad).astype(BF16)
        mine_ref[...] = expand_grad[: features // 2]
        other_ref[...] = expand_grad[features // 2 :]
        total_ref[...] += dot_nt(inner_grad, expand_ref[:, here])

        @pl.when(j == depth - 1)
        def _():
            grad = unmixed(total_ref[...], mix_ref[...])
            out_ref[...] = norm_back(stream_ref[...], rows_ref[2:3, :], grad, gains_ref, up_ref[...])

    def layer(j, places_ref):
        if pieces == 1:
            return (0, j, 0, 0)
        return (0, lax.rem(places_ref[0] // step - j + depth, depth), 0, 0)

    fixed = lambda a: pl.BlockSpec(a.shape, lambda j, places_ref: (0, 0))
    columns = lambda height: pl.BlockSpec((height, step), lambda j, places_ref: (0, j))
    outs = [
        shaped((tokens, features), F32),
        shaped((features // 2, inner_width), BF16),
        shaped((features // 2, inner_width), BF16),
        shaped((side, depth, half, features), BF16),
        shaped((side, depth, half, features), BF16),
        shaped((8, features), F32),
    ]
    ins = [places, *expand, *shrink, mix, stream, rows, normed, inner, upstream]
    flops = 8 * tokens * features * inner_width
    out, mine, other, near, over, gains = pl.pallas_call(
        kernel,
        out_shape=outs,
        grid_spec=pltpu.PrefetchScalarGridSpec(
            num_scalar_prefetch=1,
            grid=(depth,),
            in_specs=[ANYWHERE] * (count + len(shrink))
            + [fixed(mix), fixed(stream), fixed(rows), fixed(normed), columns(tokens), fixed(upstream)],
            out_specs=[
                fixed(outs[0]),
                columns(features // 2),
                columns(features // 2),
                pl.BlockSpec((side, 1, half, features), layer),
                pl.BlockSpec((side, 1, half, features), layer),
                fixed(outs[5]),
            ],
            scratch_shapes=[
                pltpu.VMEM((tokens, features), F32),
                pltpu.VMEM((features, tokens), BF16),
                pltpu.VMEM((step, tokens), BF16),
                pltpu.VMEM((features, inner_width), BF16),
                pltpu.VMEM((inner_width, features), BF16),
                pltpu.SemaphoreType.DMA((count,)),
                pltpu.SemaphoreType.DMA((blocks,)),
            ],
        ),
        compiler_params=pltpu.CompilerParams(vmem_limit_bytes=LIMIT),
        cost_estimate=cost(flops, sum(a.size * a.dtype.itemsize for a in (*ins, *outs)), LIGHT),
    )(*ins)
    if pieces == 1:
        shrink_grad = [jnp.concatenate([near, over], axis=2).reshape(inner_width, features)]
    else:
        shrink_grad = [near.reshape(-1, features), over.reshape(-1, features)]
    return out, (mine, other), shrink_grad, gains


LANE = 8


def gate_of(logits, meta):
    lane = lax.broadcasted_iota(jnp.int32, logits.shape, 1)
    chosen = lane == meta[:, 0:1] + LANE
    return jax.nn.sigmoid(jnp.sum(jnp.where(chosen, logits, 0.0), axis=-1, keepdims=True)), chosen


def put_blocks(refs, columns, values):
    rows = values.shape[0] // len(refs)
    for k, ref in enumerate(refs):
        ref[:, columns] = values[k * rows : (k + 1) * rows]


def mixer_before(stream, rows, facts, teacher, meta, target, slots, experts):
    tokens, features = stream.shape

    def kernel(stream_ref, rows_ref, facts_ref, teacher_ref, meta_ref, target_ref, *refs):
        normed_ref, logits_ref = refs[:2]
        ahead_refs, back_refs = refs[2 : 2 + experts], refs[2 + experts :]
        x = stream_ref[...]
        normed = (normalize(x)[0] * rows_ref[6:7, :] + rows_ref[7:8, :]).astype(BF16)
        normed_ref[...] = normed
        dispatch = lax.broadcasted_iota(jnp.int32, (slots, tokens), 0) == target_ref[...]
        dispatch = dispatch.astype(F32).astype(BF16)
        put_blocks(ahead_refs, slice(None), dot(dispatch, normed).astype(BF16))
        logits = dot_nt(normed, rows_ref[...].astype(BF16))
        logits_ref[...] = logits
        meta = meta_ref[...]
        gate = gate_of(logits, meta)[0]
        factor = facts_ref[1:2, 0:1] * meta[:, 2:3].astype(F32) * gate
        offset = (factor * (x - teacher_ref[...].astype(F32))).astype(BF16)
        slope = factor * gate
        high = slope.astype(BF16)
        low = (slope - high.astype(F32)).astype(BF16)
        lane = lax.broadcasted_iota(jnp.int32, (tokens, 128), 1)
        slope = jnp.where(lane == 0, high.astype(F32), jnp.where(lane == 1, low.astype(F32), 0.0)).astype(BF16)
        put_blocks(back_refs, slice(0, features), dot(dispatch, offset).astype(BF16))
        put_blocks(back_refs, slice(features, None), dot(dispatch, slope).astype(BF16))

    outs = [
        shaped((tokens, features), BF16),
        shaped((tokens, rows.shape[0]), F32),
    ]
    outs += [shaped((slots // experts, features), BF16)] * experts
    outs += [shaped((slots // experts, features + 128), BF16)] * experts
    ins = [stream, rows, facts, teacher, meta, target]
    normed, logits, *blocks = call(kernel, outs, ins, 4 * slots * tokens * features)
    return normed, logits, blocks[:experts], blocks[experts:]


def expert_forward(blocks, expand, shrink, depth):
    experts = len(blocks)
    rows, features = blocks[0].shape
    slots = experts * rows
    inner_width = shrink.shape[0]
    step = inner_width // depth

    def kernel(*refs):
        block_refs, (expand_ref, shrink_ref) = refs[:experts], refs[experts : experts + 2]
        out_refs = refs[experts + 2 : 2 * experts + 2]
        arrived_ref, inner_ref, total_ref = refs[2 * experts + 2 :]
        j = pl.program_id(0)

        @pl.when(j == 0)
        def _():
            for k in range(experts):
                arrived_ref[k * rows : (k + 1) * rows, :] = block_refs[k][...]

        inner = dot(arrived_ref[...], expand_ref[...])
        inner_ref[...] = inner
        part = dot(gelu(inner).astype(BF16), shrink_ref[...])

        @pl.when(j == 0)
        def _():
            total_ref[...] = part

        @pl.when(j > 0)
        def _():
            total_ref[...] += part

        @pl.when(j == depth - 1)
        def _():
            put_blocks(out_refs, slice(None), total_ref[...].astype(BF16))

    fixed = lambda a: pl.BlockSpec(a.shape, lambda j: (0, 0))
    outs = [shaped((rows, features), BF16)] * experts
    outs += [shaped((slots, features), BF16), shaped((slots, inner_width), F32)]
    *result, arrived, inner = call(
        kernel,
        outs,
        [*blocks, expand, shrink],
        4 * slots * features * inner_width,
        (depth,),
        [fixed(b) for b in blocks]
        + [
            pl.BlockSpec((features, step), lambda j: (0, j)),
            pl.BlockSpec((step, features), lambda j: (j, 0)),
        ],
        [fixed(o) for o in outs[:-1]] + [pl.BlockSpec((slots, step), lambda j: (0, j))],
        [pltpu.VMEM((slots, features), F32)],
    )
    return result, arrived, inner


def expert_backward(back, result, inner, expand, shrink, depth):
    experts = len(back)
    rows, features = result[0].shape
    slots = experts * rows
    inner_width = shrink.shape[0]
    step = inner_width // depth

    def kernel(*refs):
        back_refs, result_refs = refs[:experts], refs[experts : 2 * experts]
        inner_ref, expand_ref, shrink_ref = refs[2 * experts : 2 * experts + 3]
        out_refs = refs[2 * experts + 3 : 3 * experts + 3]
        landed_ref, active_ref, inner_grad_ref, total_ref = refs[3 * experts + 3 :]
        j = pl.program_id(0)

        @pl.when(j == 0)
        def _():
            for k in range(experts):
                terms = back_refs[k][:, features:].astype(F32)
                slope = terms[:, 0:1] + terms[:, 1:2]
                landed = back_refs[k][:, :features].astype(F32) + slope * result_refs[k][...].astype(F32)
                landed_ref[k * rows : (k + 1) * rows, :] = landed.astype(BF16)
            total_ref[...] = jnp.zeros_like(total_ref)

        active, slope = gelu_both(inner_ref[...])
        active_ref[...] = active.astype(BF16)
        inner_grad = (dot_nt(landed_ref[...], shrink_ref[...]) * slope).astype(BF16)
        inner_grad_ref[...] = inner_grad
        total_ref[...] += dot_nt(inner_grad, expand_ref[...])

        @pl.when(j == depth - 1)
        def _():
            put_blocks(out_refs, slice(None), total_ref[...].astype(BF16))

    fixed = lambda a: pl.BlockSpec(a.shape, lambda j: (0, 0))
    columns = lambda height: pl.BlockSpec((height, step), lambda j: (0, j))
    outs = [shaped((rows, features), BF16)] * experts
    outs += [
        shaped((slots, features), BF16),
        shaped((slots, inner_width), BF16),
        shaped((slots, inner_width), BF16),
    ]
    *rows_grad, landed, active, inner_grad = call(
        kernel,
        outs,
        [*back, *result, inner, expand, shrink],
        4 * slots * features * inner_width,
        (depth,),
        [fixed(b) for b in (*back, *result)]
        + [
            columns(slots),
            columns(features),
            pl.BlockSpec((step, features), lambda j: (j, 0)),
        ],
        [fixed(o) for o in outs[:-2]] + [columns(slots), columns(slots)],
        [pltpu.VMEM((slots, features), F32)],
    )
    return rows_grad, landed, active, inner_grad


def expert_grads(arrived, active, landed, inner_grad, owners):
    slots, features = landed.shape
    inner_width = active.shape[1]
    shrink_rows, expand_rows = inner_width // owners, features // owners
    steps = inner_width // features
    each = owners // steps if owners % steps == 0 else 1

    def shrink_kernel(active_ref, landed_ref, out_ref):
        grad = dot_tn(active_ref[...], landed_ref[...]).astype(BF16)
        for k in range(each):
            out_ref[k] = grad[k * shrink_rows : (k + 1) * shrink_rows]

    [grads] = call(
        shrink_kernel,
        [shaped((owners, 2 * shrink_rows, features), BF16)],
        [active, landed],
        2 * slots * features * inner_width,
        (owners // each,),
        [pl.BlockSpec((slots, each * shrink_rows), lambda j: (0, j)), pl.BlockSpec(landed.shape, lambda j: (0, 0))],
        [pl.BlockSpec((each, shrink_rows, features), lambda j: (j, 0, 0))],
        light=LIGHT,
    )

    def expand_kernel(arrived_ref, inner_grad_ref, grads_ref, out_ref, turned_ref):
        @pl.when(pl.program_id(0) == 0)
        def _():
            turned_ref[...] = arrived_ref[...].T

        grad = dot(turned_ref[...], inner_grad_ref[...]).astype(BF16)
        for k in range(owners):
            out_ref[k] = grad[k * expand_rows : (k + 1) * expand_rows]

    first = shrink_rows // expand_rows
    moved = 2 * slots * (features + inner_width) + 2 * features * inner_width
    return pl.pallas_call(
        expand_kernel,
        out_shape=shaped(grads.shape, BF16),
        grid=(steps,),
        in_specs=[
            pl.BlockSpec(arrived.shape, lambda j: (0, 0)),
            pl.BlockSpec((slots, features), lambda j: (0, j)),
            ANYWHERE,
        ],
        out_specs=pl.BlockSpec((owners, expand_rows, features), lambda j: (0, first + j, 0)),
        scratch_shapes=[pltpu.VMEM((features, slots), BF16)],
        input_output_aliases={2: 0},
        compiler_params=pltpu.CompilerParams(vmem_limit_bytes=LIMIT),
        cost_estimate=cost(2 * slots * features * inner_width, moved, LIGHT),
    )(arrived, inner_grad, grads)


def mixer_after(stream, rows, facts, teacher, meta, normed, logits, returned, rows_grad, experts):
    tokens, features = stream.shape
    block = returned[0].shape[0]
    slots = experts * block

    def kernel(*refs):
        stream_ref, rows_ref, facts_ref, teacher_ref, meta_ref, normed_ref, logits_ref = refs[:7]
        returned_refs, rows_grad_refs = refs[7 : 7 + experts], refs[7 + experts : 7 + 2 * experts]
        states_ref, grad_ref, small_ref, squared_ref = refs[7 + 2 * experts :]
        x = stream_ref[...]
        meta = meta_ref[...]
        combine = lax.broadcasted_iota(jnp.int32, (tokens, slots), 1) == meta[:, 1:2]
        combine = combine.astype(F32).astype(BF16)
        combined = dot(combine, jnp.concatenate([r[...] for r in returned_refs], axis=0))
        logits = logits_ref[...]
        gate, chosen = gate_of(logits, meta)
        final = x + gate * combined
        states_ref[...] = final.astype(BF16)
        valid = meta[:, 2:3].astype(F32)
        difference = final - teacher_ref[...].astype(F32)
        masked = valid * difference
        squared = 0.5 * jnp.sum(jnp.sum(masked * difference, axis=-1, keepdims=True), axis=0, keepdims=True)
        squared_ref[...] = jnp.broadcast_to(squared, squared_ref.shape)
        upstream = facts_ref[1:2, 0:1] * masked
        gate_grad = jnp.sum(upstream * combined, axis=-1, keepdims=True)
        lane = lax.broadcasted_iota(jnp.int32, logits.shape, 1)
        real = (lane >= LANE) & (lane < LANE + experts)
        shown = jnp.where(real, logits, -1e30)
        exponent = jnp.exp(shown - jnp.max(shown, axis=-1, keepdims=True))
        probs = exponent / jnp.sum(exponent, axis=-1, keepdims=True)
        share = facts_ref[0:1, :]
        tilt = jnp.sum(probs * share, axis=-1, keepdims=True)
        logits_grad = facts_ref[2:3, 0:1] * valid * probs * (share - tilt)
        logits_grad = jnp.where(real, logits_grad, 0.0)
        logits_grad += jnp.where(chosen, gate_grad * gate * (1.0 - gate), 0.0)
        first = logits_grad.astype(BF16)
        left = logits_grad - first.astype(F32)
        second = left.astype(BF16)
        third = (left - second.astype(F32)).astype(BF16)
        weights = rows_ref[...].astype(BF16)
        normed = normed_ref[...]
        normed_grad = dot(combine, jnp.concatenate([r[...] for r in rows_grad_refs], axis=0))
        normed_grad += dot(third, weights) + dot(second, weights) + dot(first, weights)
        small_ref[...] = dot_tn(third, normed) + dot_tn(second, normed) + dot_tn(first, normed)
        grad_ref[...] = norm_back(x, rows_ref[6:7, :], normed_grad, small_ref.at[6:8], upstream)

    outs = [
        shaped((tokens, features), BF16),
        shaped((tokens, features), F32),
        shaped(rows.shape, F32),
        shaped((8, 128), F32),
    ]
    ins = [stream, rows, facts, teacher, meta, normed, logits, *returned, *rows_grad]
    return call(kernel, outs, ins, 4 * slots * tokens * features)


def body(
    tokens,
    teacher,
    routes,
    piece_start,
    valid_mask,
    lower_gain,
    lower_bias,
    lower_triple,
    lower_output,
    feed_gain,
    feed_bias,
    feed_expand,
    feed_shrink,
    upper_gain,
    upper_bias,
    upper_triple,
    upper_output,
    mixer_gain,
    mixer_bias,
    router,
    expert_expand,
    expert_shrink,
):
    count, length, features = tokens.shape
    local = count * length
    experts = router.shape[1]
    share_rows = router.shape[0]
    devices = lax.axis_size("dp") * lax.axis_size("expert")
    capacity = max(2, 2 * length // experts)
    total_tokens = local * devices
    valid = valid_mask.astype(F32)
    route = routes[..., 0]
    chosen = (route[..., None] == jnp.arange(experts, dtype=jnp.int32)).astype(F32)

    counts = jnp.concatenate([jnp.sum(valid[..., None] * chosen, axis=1), jnp.sum(valid, axis=1)[:, None]], axis=1)
    counts = jnp.pad(counts.astype(BF16), ((0, share_rows - count), (0, 0)))
    vectors = [lower_gain, lower_bias, feed_gain, feed_bias, upper_gain, upper_bias, mixer_gain, mixer_bias]
    extra = jnp.concatenate([jnp.stack(vectors, axis=1), router, counts], axis=1)
    extra_width = -(-extra.shape[1] // 128) * 128
    extra = jnp.pad(extra, ((0, 0), (0, extra_width - extra.shape[1])))

    wide = 3 * features
    depth = lax.axis_size("dp") // 2

    row_order = (order(share_rows)[:, None] + jnp.arange(share_rows, dtype=jnp.int32)).reshape(1, features)
    mix = (jnp.arange(features, dtype=jnp.int32)[:, None] == row_order).astype(BF16)
    shrink_rows = feed_shrink.shape[0]
    inner_width = feed_expand.shape[1]
    lower = gather_line(jnp.concatenate([lower_triple, lower_output, extra], axis=1))
    expand_full = gather_line(after(feed_expand, lower))
    shrink_full = gather_line(after(feed_shrink, lower))
    upper = jnp.concatenate([upper_triple, upper_output], axis=1)
    upper = gather_line(after(upper, expand_full, shrink_full))
    early = [expand_full, shrink_full]
    expert_in = lax.all_gather(after(expert_expand[0], *early), "dp", axis=0, tiled=True)
    expert_out = lax.all_gather(after(expert_shrink[0], *early), "dp", axis=0, tiled=True)
    lower = gather_cores(gather_sides(lower))

    position = jnp.arange(length, dtype=jnp.int32)
    earlier = (position[:, None] > position[None, :]).astype(BF16)
    before = jnp.einsum("qk,mke->mqe", earlier, chosen.astype(BF16), preferred_element_type=F32)
    slot = jnp.sum(before * chosen, axis=-1).astype(jnp.int32)
    target = (route ^ lax.axis_index("expert")) * (count * capacity) + jnp.arange(count, dtype=jnp.int32)[:, None] * capacity + slot
    slots = experts * count * capacity
    meta = jnp.stack([route.reshape(-1), target.reshape(-1), valid_mask.reshape(-1)], axis=1)
    target = target.reshape(1, local)

    stream_in = tokens.reshape(local, features)
    labels = teacher.reshape(local, features)
    rows, stream_one, *stored_one = attend_forward(0, stream_in, None, lower, 0, mix, piece_start, length)
    lane = jnp.arange(features, dtype=jnp.int32)
    sums = rows[LANE + experts : LANE + 2 * experts + 1]
    sums = jnp.sum(jnp.where(lane % share_rows < count, sums, 0.0), axis=1)
    valid_total = sums[experts]
    loss_ratio = total_tokens / valid_total
    balance_scale = total_tokens * features * 0.1 * experts / valid_total
    share = jnp.pad(sums[:experts] / valid_total, (LANE, extra_width - LANE - experts))
    facts = jnp.stack([share, jnp.full_like(share, loss_ratio), jnp.full_like(share, balance_scale)])
    facts = jnp.pad(facts, ((0, 5), (0, 0)))

    expand_full, shrink_full = gather_sides(expand_full), gather_sides(shrink_full)
    expand_full = gather_cores([after(p, stream_one) for p in expand_full])
    shrink_full = gather_cores([after(p, stream_one) for p in shrink_full])
    places = order(shrink_rows)
    if shrink_rows % 16:
        whole = jnp.concatenate(shrink_full, axis=0).reshape(devices, shrink_rows, features)
        shrink_full = [jnp.zeros_like(whole).at[places // shrink_rows].set(whole).reshape(-1, features)]
        places = jnp.zeros((1,), jnp.int32)
    stream_two, *stored_two = feed_forward(stream_one, rows, expand_full, shrink_full, places, mix, depth)
    upper = gather_sides(upper)
    upper = gather_cores([after(p, stream_two) for p in upper])
    stream_three, *stored_three = attend_forward(4, stream_two, rows, upper, 0, mix, piece_start, length)
    normed, logits, ahead, back = mixer_before(
        stream_three, rows, facts, labels, meta, target, slots, experts
    )
    ahead = exchange(ahead)
    back = exchange([after(b, *ahead) for b in back])
    result, arrived, inner = expert_forward(ahead, expert_in, expert_out, depth)
    returned = exchange(result)
    rows_grad, landed, active, inner_grad = expert_backward(back, result, inner, expert_in, expert_out, depth)
    rows_grad = exchange(rows_grad)
    owners = lax.axis_size("dp")
    expert_grad = expert_grads(arrived, active, landed, inner_grad, owners)
    rows_grad = [after(r, expert_grad) for r in rows_grad]
    expert_grad = lax.psum_scatter(expert_grad, "dp", scatter_dimension=0, tiled=True)[0]
    states, grad_three, mixer_small, squared = mixer_after(
        stream_three, rows, facts, labels, meta, normed, logits, returned, rows_grad, experts
    )
    grad_two, *upper_grad, upper_small = attend_backward(
        4, stream_two, rows, upper, 0, mix, piece_start, length, stored_three, grad_three
    )
    at_once = lax.optimization_barrier
    hops = total_hops()

    def hop_loss(value, first, last):
        for target in hops[first:last] if hops else ():
            value = value + hop(value, target)
        return value

    upper_part = scatter_cores(*upper_grad)

    grad_two, *upper_part = at_once((grad_two, *upper_part))
    upper_part = scatter_far(upper_part)
    squared = hop_loss(squared, 0, 1)
    grad_one, expand_grad, shrink_grad, feed_small = feed_backward(
        stream_one, rows, expand_full, shrink_full, places, mix, depth, stored_two, grad_two
    )
    if shrink_rows % 16:
        blocks = order(shrink_rows) // shrink_rows
        pick = (blocks[:, None] == jnp.arange(devices, dtype=jnp.int32)).astype(BF16)
        shrink_grad = dot(pick, shrink_grad[0].reshape(devices, -1)).astype(BF16).reshape(2, -1, features)
        shrink_grad = [shrink_grad[0], shrink_grad[1]]

    upper_part, squared, grad_one, expand_grad, shrink_grad = at_once(
        (upper_part, squared, grad_one, expand_grad, shrink_grad)
    )
    upper_part = scatter_near(upper_part)
    squared = hop_loss(squared, 1, 2)
    expand_part, shrink_part = scatter_cores(*expand_grad), scatter_cores(*shrink_grad)

    upper_part, squared, expand_part, shrink_part, grad_one = at_once(
        (upper_part, squared, expand_part, shrink_part, grad_one)
    )
    upper_part = scatter_line(upper_part)
    expand_part, shrink_part = scatter_far(expand_part), scatter_far(shrink_part)
    grad_in, *lower_grad, _ = attend_backward(
        0, stream_in, rows, lower, 0, mix, piece_start, length, stored_one, grad_one, (mixer_small, upper_small, feed_small)
    )

    upper_part, expand_part, shrink_part, grad_in, lower_grad, squared = at_once(
        (upper_part, expand_part, shrink_part, grad_in, lower_grad, squared)
    )
    upper_part = total(upper_part)
    lower_part = scatter_cores(*lower_grad)
    expand_part, shrink_part = scatter_near(expand_part), scatter_near(shrink_part)
    squared = hop_loss(squared, 2, 3)

    lower_part, expand_part, shrink_part, squared = at_once((lower_part, expand_part, shrink_part, squared))
    lower_part = scatter_far(lower_part)
    expand_part = scatter_line(expand_part)
    squared = hop_loss(squared, 3, 4)

    lower_part, expand_part, shrink_part, squared = at_once((lower_part, expand_part, shrink_part, squared))
    expand_part = total(expand_part)
    lower_part = scatter_near(lower_part)
    shrink_part = scatter_line(shrink_part)
    squared = hop_loss(squared, 4, None)

    lower_part, shrink_part, squared = at_once((lower_part, shrink_part, squared))
    lower_part, shrink_part = total(scatter_line(lower_part)), total(shrink_part)
    if hops is None:
        squared = lax.psum(squared, AXES)
    small = lower_part[:, wide + features :]
    owned = expert_shrink.shape[1]
    expert_in_grad = expert_grad[owned:].reshape(-1, expert_expand.shape[1], features)
    expert_in_grad = jnp.moveaxis(expert_in_grad, 0, 1).reshape(expert_expand.shape[1:])

    squared_total = squared[0, 0]
    mean_loss = loss_ratio * squared_total / (total_tokens * features)
    return (
        states.reshape(tokens.shape),
        grad_in.reshape(tokens.shape),
        small[:, 0],
        small[:, 1],
        lower_part[:, :wide],
        lower_part[:, wide : wide + features],
        small[:, 2],
        small[:, 3],
        expand_part,
        shrink_part,
        small[:, 4],
        small[:, 5],
        upper_part[:, :wide],
        upper_part[:, wide:],
        small[:, 6],
        small[:, 7],
        small[:, 8 : 8 + experts],
        expert_in_grad.astype(F32)[None],
        expert_grad[:owned].astype(F32)[None],
        mean_loss,
    )


def solution(mesh):
    both = ("dp", "expert")
    token = P(both, None, None)
    vector = P(both)
    matrix = P(both, None)
    expert = P("expert", "dp", None)
    dense = (vector, vector, matrix, matrix, vector, vector, matrix, matrix)
    weights = dense + (vector, vector, matrix, matrix, vector, vector, matrix, expert, expert)
    return jax.shard_map(
        body,
        mesh=mesh,
        in_specs=(token, token, token, vector, matrix) + weights,
        out_specs=(token, token) + weights + (P(),),
        check_vma=False,
    )
```

```python
import math

import jax
import jax.numpy as jnp
from jax import lax
from jax.experimental import pallas as pl
from jax.experimental.pallas import tpu as pltpu
from jax.sharding import PartitionSpec as P

HD = 64
AXES = ("dp", "expert")
F32 = jnp.float32
BF16 = jnp.bfloat16


def place():
    depth = lax.axis_size("dp") // 2
    row = lax.axis_index("dp")
    return depth, lax.axis_size("expert"), row // 2, row % 2, lax.axis_index("expert")


def pairs(target):
    depth, across = lax.axis_size("dp") // 2, lax.axis_size("expert")
    out = []
    for z in range(depth):
        for c in range(2):
            for e in range(across):
                to = target(z, c, e)
                if to is not None and 0 <= to[0] < depth:
                    out.append(((z * 2 + c) * across + e, (to[0] * 2 + to[1]) * across + to[2]))
    return out


def hop(values, target):
    return lax.ppermute(values, AXES, pairs(target))


def swap_cores(values):
    return hop(values, lambda z, c, e: (z, 1 - c, e))


def first_side(values):
    return hop(values, lambda z, c, e: (z, c, e ^ (1 + c)))


def second_side(values):
    return hop(values, lambda z, c, e: (z, c, e ^ (2 - c)))


at_once = lax.optimization_barrier


def after(value, *others):
    return lax.optimization_barrier((value, *others))[0]


def shift(values, by):
    depth = place()[0]
    return hop(values, lambda z, c, e: ((z + by) % depth, c, e))


def pull_line(own):
    return [shift(own, k) for k in range(1, place()[0])]


def gather_lines(own):
    depth, _, z, c, _ = place()
    both = lax.all_gather(own, "dp", axis=0, tiled=True).reshape(depth, 2, *own.shape)
    zero = jnp.zeros_like(z)
    at = lambda k, core: lax.dynamic_slice(both, ((z - k) % depth, core, zero, zero), (1, 1, *own.shape))[0]
    return [jnp.concatenate([at(k, core) for k in range(depth)]) for core in (c, 1 - c)]


def pull_near(line):
    return first_side(line) if place()[1] == 4 else line


def pull_far(line, near, over=None):
    if place()[1] != 4:
        whole = lax.all_gather(line, "expert", axis=1)
        return [whole], None, [swap_cores(whole)]
    pair = jnp.stack([line, near])
    side = [swap_cores(pair)] if over is None else [over, swap_cores(near)]
    return [pair], second_side(pair), side


def pull_over(far):
    return None if far is None else swap_cores(far)


def in_order(pair, far, pair_over, far_over):
    return [p.reshape(-1, p.shape[-1]) for p in (*pair, far, *pair_over, far_over) if p is not None]


def order(rows):
    depth, across, z, c, e = place()
    k = jnp.arange(depth, dtype=jnp.int32)
    layer = (z - k) % depth
    if across == 4:
        there = jnp.stack([e, e ^ (1 + c), e ^ (2 - c), e ^ 3])
        over = jnp.stack([e, e ^ (2 - c), e ^ (1 + c), e ^ 3])
    else:
        there = over = jnp.arange(across, dtype=jnp.int32)
    first = (layer * 2 + c)[None, :] * across + there[:, None]
    second = (layer * 2 + 1 - c)[None, :] * across + over[:, None]
    if across != 4:
        first, second = first.T, second.T
    return jnp.concatenate([first.reshape(-1), second.reshape(-1)]) * rows


def add(first, second):
    return (first.astype(F32) + second.astype(F32)).astype(BF16)


def scatter_line(line):
    return [line[0]] + [shift(line[k], -k) for k in range(1, place()[0])]


def total(parts):
    return sum(p.astype(F32) for p in parts[1:]) + parts[0].astype(F32)


def scatter_cores(mine, other):
    return sum_cores(mine, swap_cores(other))


def sum_cores(mine, other):
    depth, across, _, _, _ = place()
    if across != 4:
        return [add(mine, other).reshape(depth, across, -1, mine.shape[1])]
    half = mine.shape[0] // 2
    return [add(mine[:half], other[:half]), add(mine[half:], other[half:])]


def scatter_far(parts):
    return [parts[0], second_side(parts[1])] if len(parts) == 2 else parts


def scatter_near(parts):
    depth = place()[0]
    if len(parts) == 1:
        return lax.psum_scatter(parts[0], "expert", scatter_dimension=1, tiled=True)[:, 0]
    half = parts[0].shape[0] // 2
    mine, come = parts
    line = add(add(mine[:half], come[:half]), first_side(add(mine[half:], come[half:])))
    return line.reshape(depth, -1, line.shape[1])


def total_hops():
    depth, across, _, _, _ = place()
    if across & (across - 1) or depth & (depth - 1):
        return None
    hops = [lambda z, c, e: (z, 1 - c, e)]
    step = 1
    while step < across:
        hops.append(lambda z, c, e, step=step: (z, c, e ^ step))
        step *= 2
    step = 1
    while step < depth:
        hops.append(lambda z, c, e, step=step: (z ^ step, c, e))
        step *= 2
    return hops


def exchange(blocks):
    return [blocks[0]] + [
        hop(blocks[k], lambda z, c, e: (z, c, e ^ k)) for k in range(1, len(blocks))
    ]


LIMIT = 60 * 1024 * 1024
LIGHT = 1000


def cost(flops, moved, light=1):
    return pl.CostEstimate(flops=flops // light, bytes_accessed=moved // light, transcendentals=0)


WHOLE = pl.BlockSpec(memory_space=pltpu.VMEM)
SCALAR = pl.BlockSpec(memory_space=pltpu.SMEM)


def dot(a, b):
    return jnp.dot(a, b, preferred_element_type=F32)


def dot_nt(a, b):
    return lax.dot_general(a, b, (((1,), (1,)), ((), ())), preferred_element_type=F32)


def dot_tn(a, b):
    return lax.dot_general(a, b, (((0,), (0,)), ((), ())), preferred_element_type=F32)


def call(kernel, outs, ins, flops, grid=(), in_specs=None, out_specs=None, scratch=(), light=1):
    moved = sum(a.size * a.dtype.itemsize for a in (*ins, *outs))
    return pl.pallas_call(
        kernel,
        out_shape=outs,
        grid=grid,
        in_specs=in_specs or [WHOLE] * len(ins),
        out_specs=out_specs or [WHOLE] * len(outs),
        scratch_shapes=scratch,
        compiler_params=pltpu.CompilerParams(vmem_limit_bytes=LIMIT),
        cost_estimate=cost(flops, moved, light),
    )(*ins)


ANYWHERE = pl.BlockSpec(memory_space=pl.ANY)


def start_parts(parts, whole, sems, first=0):
    copies, at = [], 0
    for k, part in enumerate(parts):
        rows = part.shape[0]
        copies.append(pltpu.make_async_copy(part.at[:, first : first + whole.shape[1]], whole.at[at : at + rows], sems.at[k]))
        at += rows
    for copy in copies:
        copy.start()

    def wait():
        for copy in copies:
            copy.wait()

    return wait


def start_blocks(parts, places, whole, sems):
    rows = whole.shape[0] // places.shape[0]
    copies = []
    for part in parts:
        for b in range(part.shape[0] // rows):
            k = len(copies)
            at = pl.multiple_of(places[k], 16)
            copies.append(
                pltpu.make_async_copy(part.at[b * rows : (b + 1) * rows], whole.at[pl.ds(at, rows)], sems.at[k])
            )
    for copy in copies:
        copy.start()

    def wait():
        for copy in copies:
            copy.wait()

    return wait


def mixed(values, mix):
    return dot(values, mix).astype(BF16)


def unmixed(values, mix):
    high = values.astype(BF16)
    low = (values - high.astype(F32)).astype(BF16)
    return dot_nt(low, mix) + dot_nt(high, mix)


def shaped(shape, dtype):
    return jax.ShapeDtypeStruct(shape, dtype)


def normalize(x):
    centered = x - jnp.mean(x, axis=-1, keepdims=True)
    scale = lax.rsqrt(jnp.mean(centered * centered, axis=-1, keepdims=True) + 1e-05)
    return centered * scale, scale


def norm_back(x, gain, grad, gains_ref, upstream):
    unit, scale = normalize(x)
    gains_ref[0:1, :] = jnp.sum(grad * unit, axis=0, keepdims=True)
    gains_ref[1:2, :] = jnp.sum(grad, axis=0, keepdims=True)
    inner = grad * gain
    middle = jnp.mean(inner, axis=-1, keepdims=True)
    tilt = jnp.mean(inner * unit, axis=-1, keepdims=True)
    return upstream + scale * (inner - middle - unit * tilt)


ROOT = math.sqrt(2.0 / math.pi)


def gelu(x):
    return 0.5 * x * (1.0 + jnp.tanh(ROOT * (x + 0.044715 * (x * x * x))))


def gelu_both(x):
    square = x * x
    slope = jnp.tanh(ROOT * x * (1.0 + 0.044715 * square))
    half = 0.5 * (1.0 + slope)
    return x * half, half + 0.5 * x * (1.0 - slope * slope) * (ROOT * (1.0 + 0.134145 * square))


def allowed_pair(start, length):
    row = lax.broadcasted_iota(jnp.int32, (2 * length, length), 0)
    row = jnp.where(row >= length, row - length, row)
    column = lax.broadcasted_iota(jnp.int32, (2 * length, length), 1)
    piece = length // 4
    inside = (row >= start) & (row < start + piece) & (column >= start) & (column < start + piece)
    return (column <= row) | inside


def apart(pair):
    low = lax.broadcasted_iota(jnp.int32, pair.shape, 1) < HD
    zero = jnp.zeros_like(pair)
    return jnp.concatenate([jnp.where(low, pair, zero), jnp.where(low, zero, pair)], axis=0)


def together(stacked):
    half = stacked.shape[0] // 2
    low = lax.broadcasted_iota(jnp.int32, (half, stacked.shape[1]), 1) < HD
    return jnp.where(low, stacked[:half], stacked[half:])


def softmax_pair(queries, keys, allowed):
    scores = jnp.where(allowed, dot_nt(queries, keys) * HD ** (-0.5), -1e30)
    exponent = jnp.exp(scores - jnp.max(scores, axis=-1, keepdims=True))
    return exponent / jnp.sum(exponent, axis=-1, keepdims=True)


def attend_forward(at, stream, rows, parts, first, mix, start, length):
    tokens, features = stream.shape
    wide = 3 * features
    width = parts[0].shape[1] - first
    count = len(parts)

    def kernel(*refs):
        start_ref, stream_ref, mix_ref = refs[:3]
        part_refs = refs[3 : 3 + count]
        out_ref, normed_ref, packed_ref, context_ref = refs[-6:-2]
        rows_ref, weights_ref, sems = refs[-7 if rows is None else 3 + count], refs[-2], refs[-1]
        wait = start_parts(part_refs, weights_ref, sems, first)
        x = stream_ref[...].astype(F32)
        unit = normalize(x)[0]
        mix = mix_ref[...]
        wait()
        if rows is None:
            rows_ref[...] = lax.dot_general(
                weights_ref[:, wide + features :], mix, (((0,), (1,)), ((), ())), preferred_element_type=F32
            )
        normed = (unit * rows_ref[at : at + 1, :] + rows_ref[at + 1 : at + 2, :]).astype(BF16)
        normed = mixed(normed, mix)
        normed_ref[...] = normed
        for j in range(3):
            columns = slice(j * features, (j + 1) * features)
            packed_ref[:, columns] = dot(normed, weights_ref[:, columns]).astype(BF16)
        for s in range(tokens // length):
            allowed = allowed_pair(start_ref[s], length)
            here = slice(s * length, (s + 1) * length)
            for p in range(features // (2 * HD)):
                at_q, at_k, at_v = (slice(j * features + p * 2 * HD, j * features + (p + 1) * 2 * HD) for j in range(3))
                probs = softmax_pair(apart(packed_ref[here, at_q]), packed_ref[here, at_k], allowed)
                context_ref[here, at_q] = together(dot(probs.astype(BF16), packed_ref[here, at_v])).astype(BF16)
        context = mixed(context_ref[...], mix)
        context_ref[...] = context
        out_ref[...] = x + dot(context, weights_ref[:, wide : wide + features])

    outs = [
        shaped((tokens, features), F32),
        shaped((tokens, features), BF16),
        shaped((tokens, wide), BF16),
        shaped((tokens, features), BF16),
    ]
    ins = [start, stream, mix, *parts]
    specs = [SCALAR, WHOLE, WHOLE] + [ANYWHERE] * count
    if rows is None:
        outs = [shaped((width - wide - features, features), F32)] + outs
    else:
        ins, specs = ins + [rows], specs + [WHOLE]
    scratch = [
        pltpu.VMEM((features, width), BF16),
        pltpu.SemaphoreType.DMA((count,)),
    ]
    return call(kernel, outs, ins, 10 * tokens * features * features, (), specs, None, scratch, LIGHT)


def attend_backward(at, stream, rows, parts, first, mix, start, length, stored, upstream, extra=()):
    normed, packed, context = stored
    tokens, features = stream.shape
    wide = 3 * features
    width = parts[0].shape[1] - first
    small = width - wide - features if extra else 0
    count = len(parts)

    def kernel(*refs):
        start_ref = refs[0]
        part_refs = refs[1 : 1 + count]
        mix_ref, stream_ref, rows_ref, normed_ref, packed_ref, context_ref, up_ref = refs[1 + count : 8 + count]
        extra_refs = refs[8 + count : 8 + count + len(extra)]
        out_ref, mine_ref, other_ref, gains_ref, delta_ref, weights_ref, sems = refs[8 + count + len(extra) :]
        wait = start_parts(part_refs, weights_ref, sems, first)

        def put(columns, values):
            mine_ref[:, columns] = values[: features // 2].astype(BF16)
            other_ref[:, columns] = values[features // 2 :].astype(BF16)

        upstream = up_ref[...]
        branch = upstream.astype(BF16)
        mix = mix_ref[...]
        put(slice(wide, wide + features), dot_tn(context_ref[...], branch))
        wait()
        context_grad = dot_nt(branch, weights_ref[:, wide : wide + features]).astype(BF16)
        context_grad = dot_nt(context_grad, mix).astype(BF16)
        scale = HD ** (-0.5)
        for s in range(tokens // length):
            allowed = allowed_pair(start_ref[s], length)
            here = slice(s * length, (s + 1) * length)
            for p in range(features // (2 * HD)):
                at_q, at_k, at_v = (slice(j * features + p * 2 * HD, j * features + (p + 1) * 2 * HD) for j in range(3))
                queries, keys, values = apart(packed_ref[here, at_q]), packed_ref[here, at_k], packed_ref[here, at_v]
                probs = softmax_pair(queries, keys, allowed)
                out_grad = apart(context_grad[here, at_q])
                delta_ref[here, at_v] = dot_tn(probs.astype(BF16), out_grad).astype(BF16)
                prob_grad = dot_nt(out_grad, values)
                middle = jnp.sum(probs * prob_grad, axis=-1, keepdims=True)
                score_grad = (probs * (prob_grad - middle)).astype(BF16)
                delta_ref[here, at_q] = (together(dot(score_grad, keys)) * scale).astype(BF16)
                delta_ref[here, at_k] = (dot_tn(score_grad, queries) * scale).astype(BF16)
        turned = normed_ref[...].T
        normed_grad = jnp.zeros((tokens, features), F32)
        for j in range(3):
            columns = slice(j * features, (j + 1) * features)
            put(columns, dot(turned, delta_ref[:, columns]))
            normed_grad += dot_nt(delta_ref[:, columns], weights_ref[:, columns])
        out_ref[...] = norm_back(
            stream_ref[...].astype(F32), rows_ref[at : at + 1, :], unmixed(normed_grad, mix), gains_ref, upstream
        )
        if extra:
            mixer_ref, upper_ref, feed_ref = extra_refs
            lines = [gains_ref[0:2, :], feed_ref[0:2, :], upper_ref[0:2, :], mixer_ref[6:, :]]
            lines = dot(jnp.concatenate(lines, axis=0).astype(BF16), mix)
            put(slice(wide + features, width), lines.T)

    outs = [
        shaped((tokens, features), F32),
        shaped((features // 2, wide + features + small), BF16),
        shaped((features // 2, wide + features + small), BF16),
        shaped((8, features), F32),
    ]
    ins = [start, *parts, mix, stream, rows, normed, packed, context, upstream, *extra]
    specs = [SCALAR] + [ANYWHERE] * count + [WHOLE] * (7 + len(extra))
    scratch = [
        pltpu.VMEM((tokens, wide), BF16),
        pltpu.VMEM((features, width), BF16),
        pltpu.SemaphoreType.DMA((count,)),
    ]
    return call(kernel, outs, ins, 22 * tokens * features * features, (), specs, None, scratch, LIGHT)


def feed_forward(stream, rows, expand, shrink, places, mix, depth):
    tokens, features = stream.shape
    inner_width = sum(p.shape[0] for p in shrink)
    step = inner_width // depth
    count, blocks = len(expand), places.shape[0]

    def kernel(*refs):
        places_ref = refs[0]
        expand_refs, shrink_refs = refs[1 : 1 + count], refs[1 + count : -10]
        mix_ref, stream_ref, rows_ref, out_ref, normed_ref, inner_ref = refs[-10:-4]
        expand_ref, shrink_ref, expand_sems, shrink_sems = refs[-4:]
        j = pl.program_id(0)

        @pl.when(j == 0)
        def _():
            wait_expand = start_parts(expand_refs, expand_ref, expand_sems)
            wait_shrink = start_blocks(shrink_refs, places_ref, shrink_ref, shrink_sems)
            x = stream_ref[...]
            normed = (normalize(x)[0] * rows_ref[2:3, :] + rows_ref[3:4, :]).astype(BF16)
            normed_ref[...] = mixed(normed, mix_ref[...])
            out_ref[...] = x
            wait_expand()
            wait_shrink()

        here = pl.ds(pl.multiple_of(j * step, 128), step)
        inner = dot(normed_ref[...], expand_ref[:, here])
        inner_ref[...] = inner
        out_ref[...] += dot(gelu(inner).astype(BF16), shrink_ref[here, :])

    fixed = lambda a: pl.BlockSpec(a.shape, lambda j: (0, 0))
    outs = [
        shaped((tokens, features), F32),
        shaped((tokens, features), BF16),
        shaped((tokens, inner_width), F32),
    ]
    return call(
        kernel,
        outs,
        [places, *expand, *shrink, mix, stream, rows],
        4 * tokens * features * inner_width,
        (depth,),
        [SCALAR] + [ANYWHERE] * (count + len(shrink)) + [fixed(mix), fixed(stream), fixed(rows)],
        [fixed(outs[0]), fixed(outs[1]), pl.BlockSpec((tokens, step), lambda j: (0, j))],
        [
            pltpu.VMEM((features, inner_width), BF16),
            pltpu.VMEM((inner_width, features), BF16),
            pltpu.SemaphoreType.DMA((count,)),
            pltpu.SemaphoreType.DMA((blocks,)),
        ],
        LIGHT,
    )


def feed_backward_shrink(shrink, places, depth, inner, upstream):
    tokens, features = upstream.shape
    inner_width = inner.shape[1]
    step = inner_width // depth
    count, blocks = len(shrink), places.shape[0]
    pieces = max(1, blocks // depth)
    piece = step // pieces
    side, half = max(1, pieces // 2), min(piece, step // 2)

    def kernel(places_ref, *refs):
        shrink_refs = refs[:count]
        inner_ref, up_ref, inner_grad_ref, near_ref, over_ref, active_ref, shrink_ref, sems = refs[count:]
        j = pl.program_id(0)

        @pl.when(j == 0)
        def _():
            start_blocks(shrink_refs, places_ref, shrink_ref, sems)()

        branch = up_ref[...].astype(BF16)
        active, slope = gelu_both(inner_ref[...])
        active_ref[...] = active.astype(BF16).T
        for p in range(pieces):
            start = 0
            if pieces > 1:
                start = pl.multiple_of(places_ref[p * depth + chunk_at(j, places_ref)] - j * step, 16)
            grad = dot(active_ref[pl.ds(start, piece), :], branch).astype(BF16)
            if pieces == 1:
                near_ref[0, 0] = grad[: step // 2]
                over_ref[0, 0] = grad[step // 2 :]
            elif p < pieces // 2:
                near_ref[p, 0] = grad
            else:
                over_ref[p - pieces // 2, 0] = grad
        here = pl.ds(pl.multiple_of(j * step, 128), step)
        inner_grad_ref[...] = (dot_nt(branch, shrink_ref[here, :]) * slope).astype(BF16)

    def chunk_at(j, places_ref):
        return lax.rem(places_ref[0] // step - j + depth, depth)

    def layer(j, places_ref):
        return (0, j if pieces == 1 else chunk_at(j, places_ref), 0, 0)

    columns = pl.BlockSpec((tokens, step), lambda j, places_ref: (0, j))
    outs = [
        shaped((tokens, inner_width), BF16),
        shaped((side, depth, half, features), BF16),
        shaped((side, depth, half, features), BF16),
    ]
    ins = [places, *shrink, inner, upstream]
    moved = sum(a.size * a.dtype.itemsize for a in (*ins, *outs))
    inner_grad, near, over = pl.pallas_call(
        kernel,
        out_shape=outs,
        grid_spec=pltpu.PrefetchScalarGridSpec(
            num_scalar_prefetch=1,
            grid=(depth,),
            in_specs=[ANYWHERE] * count
            + [columns, pl.BlockSpec(upstream.shape, lambda j, places_ref: (0, 0))],
            out_specs=[columns] + [pl.BlockSpec((side, 1, half, features), layer)] * 2,
            scratch_shapes=[
                pltpu.VMEM((step, tokens), BF16),
                pltpu.VMEM((inner_width, features), BF16),
                pltpu.SemaphoreType.DMA((blocks,)),
            ],
        ),
        compiler_params=pltpu.CompilerParams(vmem_limit_bytes=LIMIT),
        cost_estimate=cost(4 * tokens * features * inner_width, moved, LIGHT),
    )(*ins)
    if pieces == 1:
        shrink_grad = [jnp.concatenate([near, over], axis=2).reshape(inner_width, features)]
    else:
        shrink_grad = [near.reshape(-1, features), over.reshape(-1, features)]
    return inner_grad, shrink_grad


def feed_backward_expand(stream, rows, expand, mix, depth, normed, inner_grad, upstream):
    tokens, features = stream.shape
    inner_width = inner_grad.shape[1]
    step = inner_width // depth
    count = len(expand)

    def kernel(*refs):
        expand_refs = refs[:count]
        mix_ref, stream_ref, rows_ref, normed_ref, inner_grad_ref, up_ref = refs[count : count + 6]
        out_ref, mine_ref, other_ref, gains_ref, total_ref, turned_ref, expand_ref, sems = refs[count + 6 :]
        j = pl.program_id(0)

        @pl.when(j == 0)
        def _():
            wait = start_parts(expand_refs, expand_ref, sems)
            turned_ref[...] = normed_ref[...].T
            total_ref[...] = jnp.zeros_like(total_ref)
            wait()

        inner_grad = inner_grad_ref[...]
        expand_grad = dot(turned_ref[...], inner_grad).astype(BF16)
        mine_ref[...] = expand_grad[: features // 2]
        other_ref[...] = expand_grad[features // 2 :]
        here = pl.ds(pl.multiple_of(j * step, 128), step)
        total_ref[...] += dot_nt(inner_grad, expand_ref[:, here])

        @pl.when(j == depth - 1)
        def _():
            grad = unmixed(total_ref[...], mix_ref[...])
            out_ref[...] = norm_back(stream_ref[...], rows_ref[2:3, :], grad, gains_ref, up_ref[...])

    fixed = lambda a: pl.BlockSpec(a.shape, lambda j: (0, 0))
    columns = lambda height: pl.BlockSpec((height, step), lambda j: (0, j))
    outs = [
        shaped((tokens, features), F32),
        shaped((features // 2, inner_width), BF16),
        shaped((features // 2, inner_width), BF16),
        shaped((8, features), F32),
    ]
    out, mine, other, gains = call(
        kernel,
        outs,
        [*expand, mix, stream, rows, normed, inner_grad, upstream],
        4 * tokens * features * inner_width,
        (depth,),
        [ANYWHERE] * count
        + [fixed(mix), fixed(stream), fixed(rows), fixed(normed), columns(tokens), fixed(upstream)],
        [fixed(outs[0]), columns(features // 2), columns(features // 2), fixed(outs[3])],
        [
            pltpu.VMEM((tokens, features), F32),
            pltpu.VMEM((features, tokens), BF16),
            pltpu.VMEM((features, inner_width), BF16),
            pltpu.SemaphoreType.DMA((count,)),
        ],
        LIGHT,
    )
    return out, (mine, other), gains


LANE = 8


def gate_of(logits, meta):
    lane = lax.broadcasted_iota(jnp.int32, logits.shape, 1)
    chosen = lane == meta[:, 0:1] + LANE
    return jax.nn.sigmoid(jnp.sum(jnp.where(chosen, logits, 0.0), axis=-1, keepdims=True)), chosen


def put_blocks(refs, columns, values):
    rows = values.shape[0] // len(refs)
    for k, ref in enumerate(refs):
        ref[:, columns] = values[k * rows : (k + 1) * rows]


def mixer_before(stream, rows, facts, teacher, meta, target, slots, experts):
    tokens, features = stream.shape

    def kernel(stream_ref, rows_ref, facts_ref, teacher_ref, meta_ref, target_ref, *refs):
        normed_ref, logits_ref = refs[:2]
        ahead_refs, back_refs = refs[2 : 2 + experts], refs[2 + experts :]
        x = stream_ref[...]
        normed = (normalize(x)[0] * rows_ref[6:7, :] + rows_ref[7:8, :]).astype(BF16)
        normed_ref[...] = normed
        dispatch = lax.broadcasted_iota(jnp.int32, (slots, tokens), 0) == target_ref[...]
        dispatch = dispatch.astype(F32).astype(BF16)
        put_blocks(ahead_refs, slice(None), dot(dispatch, normed).astype(BF16))
        logits = dot_nt(normed, rows_ref[...].astype(BF16))
        logits_ref[...] = logits
        meta = meta_ref[...]
        gate = gate_of(logits, meta)[0]
        factor = facts_ref[1:2, 0:1] * meta[:, 2:3].astype(F32) * gate
        offset = (factor * (x - teacher_ref[...].astype(F32))).astype(BF16)
        slope = factor * gate
        high = slope.astype(BF16)
        low = (slope - high.astype(F32)).astype(BF16)
        lane = lax.broadcasted_iota(jnp.int32, (tokens, 128), 1)
        slope = jnp.where(lane == 0, high.astype(F32), jnp.where(lane == 1, low.astype(F32), 0.0)).astype(BF16)
        put_blocks(back_refs, slice(0, features), dot(dispatch, offset).astype(BF16))
        put_blocks(back_refs, slice(features, None), dot(dispatch, slope).astype(BF16))

    outs = [
        shaped((tokens, features), BF16),
        shaped((tokens, rows.shape[0]), F32),
    ]
    outs += [shaped((slots // experts, features), BF16)] * experts
    outs += [shaped((slots // experts, features + 128), BF16)] * experts
    ins = [stream, rows, facts, teacher, meta, target]
    normed, logits, *blocks = call(kernel, outs, ins, 4 * slots * tokens * features)
    return normed, logits, blocks[:experts], blocks[experts:]


def expert_specs(weights, step):
    owners, height, features = weights.shape
    shrink_rows = height // 2
    expand_rows = features // owners
    each = step // shrink_rows
    first = shrink_rows // expand_rows
    expand = pl.BlockSpec(
        (owners, expand_rows, step), lambda j: (0, first + j * step // features, j * step % features // step)
    )
    return expand, pl.BlockSpec((each, shrink_rows, features), lambda j: (j, 0, 0))


def expert_forward(blocks, weights, depth):
    experts = len(blocks)
    rows, features = blocks[0].shape
    slots = experts * rows
    owners, height, _ = weights.shape
    inner_width = owners * height // 2
    step = inner_width // depth

    def kernel(*refs):
        block_refs, (expand_ref, shrink_ref) = refs[:experts], refs[experts : experts + 2]
        out_refs = refs[experts + 2 : 2 * experts + 2]
        arrived_ref, inner_ref, total_ref = refs[2 * experts + 2 :]
        j = pl.program_id(0)

        @pl.when(j == 0)
        def _():
            for k in range(experts):
                arrived_ref[k * rows : (k + 1) * rows, :] = block_refs[k][...]

        inner = dot(arrived_ref[...], expand_ref[...].reshape(features, step))
        inner_ref[...] = inner
        part = dot(gelu(inner).astype(BF16), shrink_ref[...].reshape(step, features))

        @pl.when(j == 0)
        def _():
            total_ref[...] = part

        @pl.when(j > 0)
        def _():
            total_ref[...] += part

        @pl.when(j == depth - 1)
        def _():
            put_blocks(out_refs, slice(None), total_ref[...].astype(BF16))

    fixed = lambda a: pl.BlockSpec(a.shape, lambda j: (0, 0))
    outs = [shaped((rows, features), BF16)] * experts
    outs += [shaped((slots, features), BF16), shaped((slots, inner_width), F32)]
    *result, arrived, inner = call(
        kernel,
        outs,
        [*blocks, weights, weights],
        4 * slots * features * inner_width,
        (depth,),
        [fixed(b) for b in blocks] + [*expert_specs(weights, step)],
        [fixed(o) for o in outs[:-1]] + [pl.BlockSpec((slots, step), lambda j: (0, j))],
        [pltpu.VMEM((slots, features), F32)],
    )
    return result, arrived, inner


def expert_backward(back, result, inner, weights, depth):
    experts = len(back)
    rows, features = result[0].shape
    slots = experts * rows
    owners, height, _ = weights.shape
    inner_width = owners * height // 2
    step = inner_width // depth

    def kernel(*refs):
        back_refs, result_refs = refs[:experts], refs[experts : 2 * experts]
        inner_ref, expand_ref, shrink_ref = refs[2 * experts : 2 * experts + 3]
        out_refs = refs[2 * experts + 3 : 3 * experts + 3]
        inner_grad_ref, grads_ref, landed_ref, total_ref = refs[3 * experts + 3 :]
        j = pl.program_id(0)

        @pl.when(j == 0)
        def _():
            for k in range(experts):
                terms = back_refs[k][:, features:].astype(F32)
                slope = terms[:, 0:1] + terms[:, 1:2]
                landed = back_refs[k][:, :features].astype(F32) + slope * result_refs[k][...].astype(F32)
                landed_ref[k * rows : (k + 1) * rows, :] = landed.astype(BF16)
            total_ref[...] = jnp.zeros_like(total_ref)

        active, slope = gelu_both(inner_ref[...])
        landed = landed_ref[...]
        inner_grad = (dot_nt(landed, shrink_ref[...].reshape(step, features)) * slope).astype(BF16)
        inner_grad_ref[...] = inner_grad
        grads_ref[...] = dot_tn(active.astype(BF16), landed).astype(BF16)
        total_ref[...] += dot_nt(inner_grad, expand_ref[...].reshape(features, step))

        @pl.when(j == depth - 1)
        def _():
            put_blocks(out_refs, slice(None), total_ref[...].astype(BF16))

    fixed = lambda a: pl.BlockSpec(a.shape, lambda j: (0, 0))
    columns = lambda height: pl.BlockSpec((height, step), lambda j: (0, j))
    outs = [shaped((rows, features), BF16)] * experts
    outs += [shaped((slots, inner_width), BF16), shaped((inner_width, features), BF16)]
    *rows_grad, inner_grad, grads = call(
        kernel,
        outs,
        [*back, *result, inner, weights, weights],
        6 * slots * features * inner_width,
        (depth,),
        [fixed(b) for b in (*back, *result)]
        + [
            columns(slots),
            *expert_specs(weights, step),
        ],
        [fixed(o) for o in outs[:-2]]
        + [columns(slots), pl.BlockSpec((step, features), lambda j: (j, 0))],
        [pltpu.VMEM((slots, features), BF16), pltpu.VMEM((slots, features), F32)],
        LIGHT,
    )
    return rows_grad, inner_grad, grads


def expert_expand_grad(arrived, inner_grad):
    slots, features = arrived.shape
    inner_width = inner_grad.shape[1]

    def kernel(arrived_ref, inner_grad_ref, out_ref, turned_ref):
        @pl.when(pl.program_id(0) == 0)
        def _():
            turned_ref[...] = arrived_ref[...].T

        out_ref[...] = dot(turned_ref[...], inner_grad_ref[...]).astype(BF16)

    columns = lambda height: pl.BlockSpec((height, features), lambda j: (0, j))
    [grad] = call(
        kernel,
        [shaped((features, inner_width), BF16)],
        [arrived, inner_grad],
        2 * slots * features * inner_width,
        (inner_width // features,),
        [pl.BlockSpec(arrived.shape, lambda j: (0, 0)), columns(slots)],
        [columns(features)],
        [pltpu.VMEM((features, slots), BF16)],
        LIGHT,
    )
    return grad


def mixer_after(stream, rows, facts, teacher, meta, normed, logits, returned, rows_grad, experts):
    tokens, features = stream.shape
    block = returned[0].shape[0]
    slots = experts * block

    def kernel(*refs):
        stream_ref, rows_ref, facts_ref, teacher_ref, meta_ref, normed_ref, logits_ref = refs[:7]
        returned_refs, rows_grad_refs = refs[7 : 7 + experts], refs[7 + experts : 7 + 2 * experts]
        states_ref, grad_ref, small_ref, squared_ref = refs[7 + 2 * experts :]
        x = stream_ref[...]
        meta = meta_ref[...]
        combine = lax.broadcasted_iota(jnp.int32, (tokens, slots), 1) == meta[:, 1:2]
        combine = combine.astype(F32).astype(BF16)
        combined = dot(combine, jnp.concatenate([r[...] for r in returned_refs], axis=0))
        logits = logits_ref[...]
        gate, chosen = gate_of(logits, meta)
        final = x + gate * combined
        states_ref[...] = final.astype(BF16)
        valid = meta[:, 2:3].astype(F32)
        difference = final - teacher_ref[...].astype(F32)
        masked = valid * difference
        squared = 0.5 * jnp.sum(jnp.sum(masked * difference, axis=-1, keepdims=True), axis=0, keepdims=True)
        squared_ref[...] = jnp.broadcast_to(squared, squared_ref.shape)
        upstream = facts_ref[1:2, 0:1] * masked
        gate_grad = jnp.sum(upstream * combined, axis=-1, keepdims=True)
        lane = lax.broadcasted_iota(jnp.int32, logits.shape, 1)
        real = (lane >= LANE) & (lane < LANE + experts)
        shown = jnp.where(real, logits, -1e30)
        exponent = jnp.exp(shown - jnp.max(shown, axis=-1, keepdims=True))
        probs = exponent / jnp.sum(exponent, axis=-1, keepdims=True)
        share = facts_ref[0:1, :]
        tilt = jnp.sum(probs * share, axis=-1, keepdims=True)
        logits_grad = facts_ref[2:3, 0:1] * valid * probs * (share - tilt)
        logits_grad = jnp.where(real, logits_grad, 0.0)
        logits_grad += jnp.where(chosen, gate_grad * gate * (1.0 - gate), 0.0)
        first = logits_grad.astype(BF16)
        left = logits_grad - first.astype(F32)
        second = left.astype(BF16)
        third = (left - second.astype(F32)).astype(BF16)
        weights = rows_ref[...].astype(BF16)
        normed = normed_ref[...]
        normed_grad = dot(combine, jnp.concatenate([r[...] for r in rows_grad_refs], axis=0))
        normed_grad += dot(third, weights) + dot(second, weights) + dot(first, weights)
        small_ref[...] = dot_tn(third, normed) + dot_tn(second, normed) + dot_tn(first, normed)
        grad_ref[...] = norm_back(x, rows_ref[6:7, :], normed_grad, small_ref.at[6:8], upstream)

    outs = [
        shaped((tokens, features), BF16),
        shaped((tokens, features), F32),
        shaped(rows.shape, F32),
        shaped((8, 128), F32),
    ]
    ins = [stream, rows, facts, teacher, meta, normed, logits, *returned, *rows_grad]
    return call(kernel, outs, ins, 4 * slots * tokens * features)


def body(
    tokens,
    teacher,
    routes,
    piece_start,
    valid_mask,
    lower_gain,
    lower_bias,
    lower_triple,
    lower_output,
    feed_gain,
    feed_bias,
    feed_expand,
    feed_shrink,
    upper_gain,
    upper_bias,
    upper_triple,
    upper_output,
    mixer_gain,
    mixer_bias,
    router,
    expert_expand,
    expert_shrink,
):
    count, length, features = tokens.shape
    local = count * length
    experts = router.shape[1]
    share_rows = router.shape[0]
    devices = lax.axis_size("dp") * lax.axis_size("expert")
    capacity = max(2, 2 * length // experts)
    total_tokens = local * devices
    valid = valid_mask.astype(F32)
    route = routes[..., 0]
    chosen = (route[..., None] == jnp.arange(experts, dtype=jnp.int32)).astype(F32)

    counts = jnp.concatenate([jnp.sum(valid[..., None] * chosen, axis=1), jnp.sum(valid, axis=1)[:, None]], axis=1)
    counts = jnp.pad(counts.astype(BF16), ((0, share_rows - count), (0, 0)))
    vectors = [lower_gain, lower_bias, feed_gain, feed_bias, upper_gain, upper_bias, mixer_gain, mixer_bias]
    extra = jnp.concatenate([jnp.stack(vectors, axis=1), router, counts], axis=1)
    extra_width = -(-extra.shape[1] // 128) * 128
    extra = jnp.pad(extra, ((0, 0), (0, extra_width - extra.shape[1])))

    wide = 3 * features
    depth = lax.axis_size("dp") // 2

    row_order = (order(share_rows)[:, None] + jnp.arange(share_rows, dtype=jnp.int32)).reshape(1, features)
    mix = (jnp.arange(features, dtype=jnp.int32)[:, None] == row_order).astype(BF16)
    shrink_rows = feed_shrink.shape[0]
    inner_width = feed_expand.shape[1]
    inner_width = feed_expand.shape[1]
    lower_own = jnp.concatenate([lower_triple, lower_output, extra], axis=1)
    upper_own = jnp.concatenate([upper_triple, upper_output], axis=1)

    position = jnp.arange(length, dtype=jnp.int32)
    earlier = (position[:, None] > position[None, :]).astype(BF16)
    before = jnp.einsum("qk,mke->mqe", earlier, chosen.astype(BF16), preferred_element_type=F32)
    slot = jnp.sum(before * chosen, axis=-1).astype(jnp.int32)
    target = (route ^ lax.axis_index("expert")) * (count * capacity) + jnp.arange(count, dtype=jnp.int32)[:, None] * capacity + slot
    slots = experts * count * capacity
    meta = jnp.stack([route.reshape(-1), target.reshape(-1), valid_mask.reshape(-1)], axis=1)
    target = target.reshape(1, local)

    stream_in = tokens.reshape(local, features)
    labels = teacher.reshape(local, features)
    places = order(shrink_rows)
    pieces = expert_expand[0].reshape(-1, inner_width // features, features)
    experts_own = jnp.concatenate([expert_shrink[0], jnp.moveaxis(pieces, 1, 0).reshape(-1, features)])

    shrink_line, shrink_over = gather_lines(feed_shrink)
    wide_line, wide_over = gather_lines(jnp.concatenate([feed_expand, upper_own], axis=1))
    lower = pull_line(lower_own)

    lower, experts_own, mix, meta, target, places = at_once((lower, experts_own, mix, meta, target, places))
    experts_full = lax.all_gather(experts_own, "dp")
    lower = jnp.stack([lower_own, *lower])
    near = pull_near(lower)

    lower, near, shrink_line, shrink_over = at_once((lower, near, shrink_line, shrink_over))
    lower = pull_far(lower, near)
    shrink_near = pull_near(shrink_line)

    lower, shrink_line, shrink_near = at_once((lower, shrink_line, shrink_near))
    lower_over = pull_over(lower[1])

    lower, lower_over, wide_line, wide_over = at_once((lower, lower_over, wide_line, wide_over))
    lower = in_order(*lower, lower_over)
    shrink_full = pull_far(shrink_line, shrink_near, shrink_over)
    expand_line, expand_over = wide_line[..., :inner_width], wide_over[..., :inner_width]
    upper_line, upper_over = wide_line[..., inner_width:], wide_over[..., inner_width:]
    expand_near = pull_near(expand_line)
    rows, stream_one, *stored_one = attend_forward(0, stream_in, None, lower, 0, mix, piece_start, length)

    shrink_full, expand_line, expand_near, rows, stream_one = at_once(
        (shrink_full, expand_line, expand_near, rows, stream_one)
    )
    shrink_full = in_order(*shrink_full, pull_over(shrink_full[1]))
    expand_full = pull_far(expand_line, expand_near, expand_over)
    upper_near = pull_near(upper_line)
    lane = jnp.arange(features, dtype=jnp.int32)
    sums = rows[LANE + experts : LANE + 2 * experts + 1]
    sums = jnp.sum(jnp.where(lane % share_rows < count, sums, 0.0), axis=1)
    valid_total = sums[experts]
    loss_ratio = total_tokens / valid_total
    balance_scale = total_tokens * features * 0.1 * experts / valid_total
    share = jnp.pad(sums[:experts] / valid_total, (LANE, extra_width - LANE - experts))
    facts = jnp.stack([share, jnp.full_like(share, loss_ratio), jnp.full_like(share, balance_scale)])
    facts = jnp.pad(facts, ((0, 5), (0, 0)))

    shrink_full, expand_full, upper_line, upper_near, stream_one, facts = at_once(
        (shrink_full, expand_full, upper_line, upper_near, stream_one, facts)
    )
    expand_full = in_order(*expand_full, pull_over(expand_full[1]))

    expand_full, upper_line, upper_near, stream_one = at_once((expand_full, upper_line, upper_near, stream_one))
    upper = pull_far(upper_line, upper_near, upper_over)

    if shrink_rows % 16:
        whole = jnp.concatenate(shrink_full, axis=0).reshape(devices, shrink_rows, features)
        shrink_full = [jnp.zeros_like(whole).at[places // shrink_rows].set(whole).reshape(-1, features)]
        places = jnp.zeros((1,), jnp.int32)
    stream_two, *stored_two = feed_forward(stream_one, rows, expand_full, shrink_full, places, mix, depth)

    upper, stream_two = at_once((upper, stream_two))
    upper = in_order(*upper, pull_over(upper[1]))
    stream_three, *stored_three = attend_forward(4, stream_two, rows, upper, 0, mix, piece_start, length)
    normed, logits, ahead, back = mixer_before(
        stream_three, rows, facts, labels, meta, target, slots, experts
    )
    ahead = exchange(ahead)
    back = exchange([after(b, *ahead) for b in back])
    result, arrived, inner = expert_forward(ahead, experts_full, depth)
    returned = exchange(result)
    rows_grad, inner_grad, expert_out_grad = expert_backward(back, result, inner, experts_full, depth)
    returned, rows_grad, inner_grad, expert_out_grad = at_once((returned, rows_grad, inner_grad, expert_out_grad))
    expert_out_grad = lax.psum_scatter(expert_out_grad, "dp", scatter_dimension=0, tiled=True)
    rows_grad = exchange(rows_grad)
    states, grad_three, mixer_small, squared = mixer_after(
        stream_three, rows, facts, labels, meta, normed, logits, returned, rows_grad, experts
    )
    grad_two, *upper_grad, upper_small = attend_backward(
        4, stream_two, rows, upper, 0, mix, piece_start, length, stored_three, grad_three
    )
    hops = total_hops()

    def hop_loss(value, first, last):
        for target in hops[first:last] if hops else ():
            value = value + hop(value, target)
        return value

    inner_grad = after(inner_grad, grad_two)
    upper_mine, upper_other = upper_grad
    upper_other = swap_cores(upper_other)
    expert_in_grad = expert_expand_grad(arrived, inner_grad)

    upper_mine, upper_other, expert_in_grad, grad_two = at_once((upper_mine, upper_other, expert_in_grad, grad_two))
    expert_in_grad = lax.psum_scatter(expert_in_grad, "dp", scatter_dimension=0, tiled=True)
    upper_part = sum_cores(upper_mine, upper_other)

    grad_two, *upper_part = at_once((grad_two, *upper_part))
    upper_part = scatter_far(upper_part)
    squared = hop_loss(squared, 0, 1)
    feed_normed, inner_pre = stored_two
    inner_grad, shrink_grad = feed_backward_shrink(shrink_full, places, depth, inner_pre, grad_two)
    if shrink_rows % 16:
        blocks = order(shrink_rows) // shrink_rows
        pick = (blocks[:, None] == jnp.arange(devices, dtype=jnp.int32)).astype(BF16)
        shrink_grad = dot(pick, shrink_grad[0].reshape(devices, -1)).astype(BF16).reshape(2, -1, features)
        shrink_grad = [shrink_grad[0], shrink_grad[1]]

    upper_part, squared, inner_grad, shrink_grad = at_once((upper_part, squared, inner_grad, shrink_grad))
    upper_part = scatter_near(upper_part)
    squared = hop_loss(squared, 1, 2)
    shrink_mine, shrink_other = shrink_grad
    shrink_other = swap_cores(shrink_other)
    grad_one, expand_grad, feed_small = feed_backward_expand(
        stream_one, rows, expand_full, mix, depth, feed_normed, inner_grad, grad_two
    )

    upper_part, squared, shrink_mine, shrink_other, expand_grad, grad_one = at_once(
        (upper_part, squared, shrink_mine, shrink_other, expand_grad, grad_one)
    )
    shrink_part = scatter_far(sum_cores(shrink_mine, shrink_other))
    expand_part = scatter_cores(*expand_grad)

    upper_part, expand_part, shrink_part, grad_one, squared = at_once(
        (upper_part, expand_part, shrink_part, grad_one, squared)
    )
    expand_part = scatter_far(expand_part)
    shrink_part = scatter_near(shrink_part)
    upper_part = scatter_line(upper_part)
    grad_in, *lower_grad, _ = attend_backward(
        0, stream_in, rows, lower, 0, mix, piece_start, length, stored_one, grad_one, (mixer_small, upper_small, feed_small)
    )

    upper_part, expand_part, shrink_part, grad_in, lower_grad, squared = at_once(
        (upper_part, expand_part, shrink_part, grad_in, lower_grad, squared)
    )
    lower_part = scatter_cores(*lower_grad)
    expand_part = scatter_near(expand_part)
    shrink_part = scatter_line(shrink_part)

    lower_part, expand_part, shrink_part, upper_part, squared = at_once(
        (lower_part, expand_part, shrink_part, upper_part, squared)
    )
    lower_part = scatter_far(lower_part)
    expand_part = scatter_line(expand_part)
    upper_part = total(upper_part)
    squared = hop_loss(squared, 2, 3)

    lower_part, expand_part, shrink_part, upper_part, squared = at_once(
        (lower_part, expand_part, shrink_part, upper_part, squared)
    )
    lower_part = scatter_near(lower_part)
    squared = hop_loss(squared, 3, 4)
    shrink_part = total(shrink_part)
    expert_out_grad, expert_in_grad = expert_out_grad.astype(F32), expert_in_grad.astype(F32)

    lower_part, expand_part, shrink_part, upper_part, squared, expert_in_grad, expert_out_grad = at_once(
        (lower_part, expand_part, shrink_part, upper_part, squared, expert_in_grad, expert_out_grad)
    )
    squared = hop_loss(squared, 4, None)
    lower_part, expand_part = total(scatter_line(lower_part)), total(expand_part)
    if hops is None:
        squared = lax.psum(squared, AXES)
    small = lower_part[:, wide + features :]
    squared_total = squared[0, 0]
    mean_loss = loss_ratio * squared_total / (total_tokens * features)
    return (
        states.reshape(tokens.shape),
        grad_in.reshape(tokens.shape),
        small[:, 0],
        small[:, 1],
        lower_part[:, :wide],
        lower_part[:, wide : wide + features],
        small[:, 2],
        small[:, 3],
        expand_part,
        shrink_part,
        small[:, 4],
        small[:, 5],
        upper_part[:, :wide],
        upper_part[:, wide:],
        small[:, 6],
        small[:, 7],
        small[:, 8 : 8 + experts],
        expert_in_grad[None],
        expert_out_grad[None],
        mean_loss,
    )


def solution(mesh):
    both = ("dp", "expert")
    token = P(both, None, None)
    vector = P(both)
    matrix = P(both, None)
    expert = P("expert", "dp", None)
    dense = (vector, vector, matrix, matrix, vector, vector, matrix, matrix)
    weights = dense + (vector, vector, matrix, matrix, vector, vector, matrix, expert, expert)
    return jax.shard_map(
        body,
        mesh=mesh,
        in_specs=(token, token, token, vector, matrix) + weights,
        out_specs=(token, token) + weights + (P(),),
        check_vma=False,
    )
```

```python
import math

import jax
import jax.numpy as jnp
from jax import lax
from jax.experimental import pallas as pl
from jax.experimental.pallas import tpu as pltpu
from jax.sharding import PartitionSpec as P

HD = 64
AXES = ("dp", "expert")
F32 = jnp.float32
BF16 = jnp.bfloat16


def place():
    depth = lax.axis_size("dp") // 2
    row = lax.axis_index("dp")
    return depth, lax.axis_size("expert"), row // 2, row % 2, lax.axis_index("expert")


def pairs(target):
    depth, across = lax.axis_size("dp") // 2, lax.axis_size("expert")
    out = []
    for z in range(depth):
        for c in range(2):
            for e in range(across):
                to = target(z, c, e)
                if to is not None and 0 <= to[0] < depth:
                    out.append(((z * 2 + c) * across + e, (to[0] * 2 + to[1]) * across + to[2]))
    return out


def hop(values, target):
    return lax.ppermute(values, AXES, pairs(target))


def swap_cores(values):
    return hop(values, lambda z, c, e: (z, 1 - c, e))


def first_side(values):
    return hop(values, lambda z, c, e: (z, c, e ^ (1 + c)))


def second_side(values):
    return hop(values, lambda z, c, e: (z, c, e ^ (2 - c)))


at_once = lax.optimization_barrier


def after(value, *others):
    return lax.optimization_barrier((value, *others))[0]


def shift(values, by):
    depth = place()[0]
    return hop(values, lambda z, c, e: ((z + by) % depth, c, e))


def pull_line(own):
    return [shift(own, k) for k in range(1, place()[0])]


def gather_lines(own):
    depth, _, z, c, _ = place()
    both = lax.all_gather(own, "dp", axis=0, tiled=True).reshape(depth, 2, *own.shape)
    zero = jnp.zeros_like(z)
    at = lambda k, core: lax.dynamic_slice(both, ((z - k) % depth, core, zero, zero), (1, 1, *own.shape))[0]
    return [jnp.concatenate([at(k, core) for k in range(depth)]) for core in (c, 1 - c)]


def pull_near(line):
    return first_side(line) if place()[1] == 4 else line


def pull_far(line, near, over=None):
    if place()[1] != 4:
        whole = lax.all_gather(line, "expert", axis=1)
        return [whole], None, [swap_cores(whole)]
    pair = jnp.stack([line, near])
    side = [swap_cores(pair)] if over is None else [over, swap_cores(near)]
    return [pair], second_side(pair), side


def pull_over(far):
    return None if far is None else swap_cores(far)


def in_order(pair, far, pair_over, far_over):
    return [p.reshape(-1, p.shape[-1]) for p in (*pair, far, *pair_over, far_over) if p is not None]


def order(rows):
    depth, across, z, c, e = place()
    k = jnp.arange(depth, dtype=jnp.int32)
    layer = (z - k) % depth
    if across == 4:
        there = jnp.stack([e, e ^ (1 + c), e ^ (2 - c), e ^ 3])
        over = jnp.stack([e, e ^ (2 - c), e ^ (1 + c), e ^ 3])
    else:
        there = over = jnp.arange(across, dtype=jnp.int32)
    first = (layer * 2 + c)[None, :] * across + there[:, None]
    second = (layer * 2 + 1 - c)[None, :] * across + over[:, None]
    if across != 4:
        first, second = first.T, second.T
    return jnp.concatenate([first.reshape(-1), second.reshape(-1)]) * rows


def add(first, second):
    return (first.astype(F32) + second.astype(F32)).astype(BF16)


def scatter_line(line):
    return [line[0]] + [shift(line[k], -k) for k in range(1, place()[0])]


def total(parts):
    return sum(p.astype(F32) for p in parts[1:]) + parts[0].astype(F32)


def scatter_cores(mine, other):
    return sum_cores(mine, swap_cores(other))


def sum_cores(mine, other):
    depth, across, _, _, _ = place()
    if across != 4:
        return [add(mine, other).reshape(depth, across, -1, mine.shape[1])]
    half = mine.shape[0] // 2
    return [add(mine[:half], other[:half]), add(mine[half:], other[half:])]


def scatter_far(parts):
    return [parts[0], second_side(parts[1])] if len(parts) == 2 else parts


def scatter_near(parts):
    depth = place()[0]
    if len(parts) == 1:
        return lax.psum_scatter(parts[0], "expert", scatter_dimension=1, tiled=True)[:, 0]
    half = parts[0].shape[0] // 2
    mine, come = parts
    line = add(add(mine[:half], come[:half]), first_side(add(mine[half:], come[half:])))
    return line.reshape(depth, -1, line.shape[1])


def total_hops():
    depth, across, _, _, _ = place()
    if across & (across - 1) or depth & (depth - 1):
        return None
    hops = [lambda z, c, e: (z, 1 - c, e)]
    step = 1
    while step < across:
        hops.append(lambda z, c, e, step=step: (z, c, e ^ step))
        step *= 2
    step = 1
    while step < depth:
        hops.append(lambda z, c, e, step=step: (z ^ step, c, e))
        step *= 2
    return hops


def exchange(blocks):
    return [blocks[0]] + [
        hop(blocks[k], lambda z, c, e: (z, c, e ^ k)) for k in range(1, len(blocks))
    ]


LIMIT = 60 * 1024 * 1024
LANE = 8
LIGHT = 1000


def cost(flops, moved, light=1):
    return pl.CostEstimate(flops=flops // light, bytes_accessed=moved // light, transcendentals=0)


WHOLE = pl.BlockSpec(memory_space=pltpu.VMEM)
SCALAR = pl.BlockSpec(memory_space=pltpu.SMEM)


def dot(a, b):
    return jnp.dot(a, b, preferred_element_type=F32)


def dot_nt(a, b):
    return lax.dot_general(a, b, (((1,), (1,)), ((), ())), preferred_element_type=F32)


def dot_tn(a, b):
    return lax.dot_general(a, b, (((0,), (0,)), ((), ())), preferred_element_type=F32)


def call(kernel, outs, ins, flops, grid=(), in_specs=None, out_specs=None, scratch=(), light=1):
    moved = sum(a.size * a.dtype.itemsize for a in (*ins, *outs))
    return pl.pallas_call(
        kernel,
        out_shape=outs,
        grid=grid,
        in_specs=in_specs or [WHOLE] * len(ins),
        out_specs=out_specs or [WHOLE] * len(outs),
        scratch_shapes=scratch,
        compiler_params=pltpu.CompilerParams(vmem_limit_bytes=LIMIT),
        cost_estimate=cost(flops, moved, light),
    )(*ins)


ANYWHERE = pl.BlockSpec(memory_space=pl.ANY)


def start_parts(parts, whole, sems, first=0):
    copies, at = [], 0
    for k, part in enumerate(parts):
        rows = part.shape[0]
        copies.append(pltpu.make_async_copy(part.at[:, first : first + whole.shape[1]], whole.at[at : at + rows], sems.at[k]))
        at += rows
    for copy in copies:
        copy.start()

    def wait():
        for copy in copies:
            copy.wait()

    return wait


def start_blocks(parts, places, whole, sems):
    rows = whole.shape[0] // places.shape[0]
    copies = []
    for part in parts:
        for b in range(part.shape[0] // rows):
            k = len(copies)
            at = pl.multiple_of(places[k], 16)
            copies.append(
                pltpu.make_async_copy(part.at[b * rows : (b + 1) * rows], whole.at[pl.ds(at, rows)], sems.at[k])
            )
    for copy in copies:
        copy.start()

    def wait():
        for copy in copies:
            copy.wait()

    return wait


def mixed(values, mix):
    return dot(values, mix).astype(BF16)


def unmixed(values, mix):
    high = values.astype(BF16)
    low = (values - high.astype(F32)).astype(BF16)
    return dot_nt(low, mix) + dot_nt(high, mix)


def shaped(shape, dtype):
    return jax.ShapeDtypeStruct(shape, dtype)


def normalize(x):
    centered = x - jnp.mean(x, axis=-1, keepdims=True)
    scale = lax.rsqrt(jnp.mean(centered * centered, axis=-1, keepdims=True) + 1e-05)
    return centered * scale, scale


def norm_back(x, gain, grad, gains_ref, upstream):
    unit, scale = normalize(x)
    gains_ref[0:1, :] = jnp.sum(grad * unit, axis=0, keepdims=True)
    gains_ref[1:2, :] = jnp.sum(grad, axis=0, keepdims=True)
    inner = grad * gain
    middle = jnp.mean(inner, axis=-1, keepdims=True)
    tilt = jnp.mean(inner * unit, axis=-1, keepdims=True)
    return upstream + scale * (inner - middle - unit * tilt)


ROOT = math.sqrt(2.0 / math.pi)


def gelu(x):
    return 0.5 * x * (1.0 + jnp.tanh(ROOT * (x + 0.044715 * (x * x * x))))


def gelu_both(x):
    square = x * x
    slope = jnp.tanh(ROOT * x * (1.0 + 0.044715 * square))
    half = 0.5 * (1.0 + slope)
    return x * half, half + 0.5 * x * (1.0 - slope * slope) * (ROOT * (1.0 + 0.134145 * square))


def allowed_pair(start, length):
    row = lax.broadcasted_iota(jnp.int32, (2 * length, length), 0)
    row = jnp.where(row >= length, row - length, row)
    column = lax.broadcasted_iota(jnp.int32, (2 * length, length), 1)
    piece = length // 4
    inside = (row >= start) & (row < start + piece) & (column >= start) & (column < start + piece)
    return (column <= row) | inside


def apart(pair):
    low = lax.broadcasted_iota(jnp.int32, pair.shape, 1) < HD
    zero = jnp.zeros_like(pair)
    return jnp.concatenate([jnp.where(low, pair, zero), jnp.where(low, zero, pair)], axis=0)


def together(stacked):
    half = stacked.shape[0] // 2
    low = lax.broadcasted_iota(jnp.int32, (half, stacked.shape[1]), 1) < HD
    return jnp.where(low, stacked[:half], stacked[half:])


def softmax_pair(queries, keys, allowed):
    scores = jnp.where(allowed, dot_nt(queries, keys) * HD ** (-0.5), -1e30)
    exponent = jnp.exp(scores - jnp.max(scores, axis=-1, keepdims=True))
    return exponent / jnp.sum(exponent, axis=-1, keepdims=True)


def pack_lower(triple, output, vectors, router, route, valid):
    share = triple.shape[0]
    experts = router.shape[0]
    wide, features = triple.shape[1], output.shape[1]

    def kernel(triple_ref, output_ref, *refs):
        vector_refs = refs[:LANE]
        router_ref, route_ref, valid_ref, out_ref, turned_ref = refs[LANE:]
        turned_ref[...] = jnp.zeros_like(turned_ref)
        for k in range(LANE):
            turned_ref[k : k + 1, :share] = vector_refs[k][...].astype(F32)
        turned_ref[LANE : LANE + experts, :share] = router_ref[...].astype(F32)
        valid = valid_ref[...].astype(F32)
        route = route_ref[...]
        lane = lax.broadcasted_iota(jnp.int32, (valid.shape[0], 128), 1) - LANE - experts
        counts = jnp.where(lane == experts, jnp.sum(valid, axis=-1, keepdims=True), 0.0)
        for e in range(experts):
            count = jnp.sum(jnp.where(route == e, valid, 0.0), axis=-1, keepdims=True)
            counts += jnp.where(lane == e, count, 0.0)
        counts = jnp.concatenate([counts, jnp.zeros((share - counts.shape[0], 128), F32)], axis=0)
        out_ref[:, :wide] = triple_ref[...]
        out_ref[:, wide : wide + features] = output_ref[...]
        out_ref[:, wide + features :] = (turned_ref[...].T[:share] + counts).astype(BF16)

    [packed] = call(
        kernel,
        [shaped((share, wide + features + 128), BF16)],
        [triple, output, *(v.reshape(1, share) for v in vectors), router, route, valid],
        1,
        scratch=[pltpu.VMEM((128, 128), F32)],
    )
    return packed


def attend_forward(at, stream, rows, parts, first, mix, start, length):
    tokens, features = stream.shape
    wide = 3 * features
    width = parts[0].shape[1] - first
    count = len(parts)

    def kernel(*refs):
        start_ref, stream_ref, mix_ref = refs[:3]
        part_refs = refs[3 : 3 + count]
        out_ref, normed_ref, packed_ref, context_ref = refs[-6:-2]
        rows_ref, weights_ref, sems = refs[-7 if rows is None else 3 + count], refs[-2], refs[-1]
        wait = start_parts(part_refs, weights_ref, sems, first)
        x = stream_ref[...].astype(F32)
        unit = normalize(x)[0]
        mix = mix_ref[...]
        wait()
        if rows is None:
            rows_ref[...] = lax.dot_general(
                weights_ref[:, wide + features :], mix, (((0,), (1,)), ((), ())), preferred_element_type=F32
            )
        normed = (unit * rows_ref[at : at + 1, :] + rows_ref[at + 1 : at + 2, :]).astype(BF16)
        normed = mixed(normed, mix)
        normed_ref[...] = normed
        for j in range(3):
            columns = slice(j * features, (j + 1) * features)
            packed_ref[:, columns] = dot(normed, weights_ref[:, columns]).astype(BF16)
        for s in range(tokens // length):
            allowed = allowed_pair(start_ref[s], length)
            here = slice(s * length, (s + 1) * length)
            for p in range(features // (2 * HD)):
                at_q, at_k, at_v = (slice(j * features + p * 2 * HD, j * features + (p + 1) * 2 * HD) for j in range(3))
                probs = softmax_pair(apart(packed_ref[here, at_q]), packed_ref[here, at_k], allowed)
                context_ref[here, at_q] = together(dot(probs.astype(BF16), packed_ref[here, at_v])).astype(BF16)
        context = mixed(context_ref[...], mix)
        context_ref[...] = context
        out_ref[...] = x + dot(context, weights_ref[:, wide : wide + features])

    outs = [
        shaped((tokens, features), F32),
        shaped((tokens, features), BF16),
        shaped((tokens, wide), BF16),
        shaped((tokens, features), BF16),
    ]
    ins = [start, stream, mix, *parts]
    specs = [SCALAR, WHOLE, WHOLE] + [ANYWHERE] * count
    if rows is None:
        outs = [shaped((width - wide - features, features), F32)] + outs
    else:
        ins, specs = ins + [rows], specs + [WHOLE]
    scratch = [
        pltpu.VMEM((features, width), BF16),
        pltpu.SemaphoreType.DMA((count,)),
    ]
    return call(kernel, outs, ins, 10 * tokens * features * features, (), specs, None, scratch, LIGHT)


def attend_backward(at, stream, rows, parts, first, mix, start, length, stored, upstream, extra=()):
    normed, packed, context = stored
    tokens, features = stream.shape
    wide = 3 * features
    width = parts[0].shape[1] - first
    small = width - wide - features if extra else 0
    count = len(parts)

    def kernel(*refs):
        start_ref = refs[0]
        part_refs = refs[1 : 1 + count]
        mix_ref, stream_ref, rows_ref, normed_ref, packed_ref, context_ref, up_ref = refs[1 + count : 8 + count]
        extra_refs = refs[8 + count : 8 + count + len(extra)]
        out_ref, mine_ref, other_ref, gains_ref, delta_ref, weights_ref, sems = refs[8 + count + len(extra) :]
        wait = start_parts(part_refs, weights_ref, sems, first)

        def put(columns, values):
            mine_ref[:, columns] = values[: features // 2].astype(BF16)
            other_ref[:, columns] = values[features // 2 :].astype(BF16)

        upstream = up_ref[...]
        branch = upstream.astype(BF16)
        mix = mix_ref[...]
        put(slice(wide, wide + features), dot_tn(context_ref[...], branch))
        wait()
        context_grad = dot_nt(branch, weights_ref[:, wide : wide + features]).astype(BF16)
        context_grad = dot_nt(context_grad, mix).astype(BF16)
        scale = HD ** (-0.5)
        for s in range(tokens // length):
            allowed = allowed_pair(start_ref[s], length)
            here = slice(s * length, (s + 1) * length)
            for p in range(features // (2 * HD)):
                at_q, at_k, at_v = (slice(j * features + p * 2 * HD, j * features + (p + 1) * 2 * HD) for j in range(3))
                queries, keys, values = apart(packed_ref[here, at_q]), packed_ref[here, at_k], packed_ref[here, at_v]
                probs = softmax_pair(queries, keys, allowed)
                out_grad = apart(context_grad[here, at_q])
                delta_ref[here, at_v] = dot_tn(probs.astype(BF16), out_grad).astype(BF16)
                prob_grad = dot_nt(out_grad, values)
                middle = jnp.sum(probs * prob_grad, axis=-1, keepdims=True)
                score_grad = (probs * (prob_grad - middle)).astype(BF16)
                delta_ref[here, at_q] = (together(dot(score_grad, keys)) * scale).astype(BF16)
                delta_ref[here, at_k] = (dot_tn(score_grad, queries) * scale).astype(BF16)
        turned = normed_ref[...].T
        normed_grad = jnp.zeros((tokens, features), F32)
        for j in range(3):
            columns = slice(j * features, (j + 1) * features)
            put(columns, dot(turned, delta_ref[:, columns]))
            normed_grad += dot_nt(delta_ref[:, columns], weights_ref[:, columns])
        out_ref[...] = norm_back(
            stream_ref[...].astype(F32), rows_ref[at : at + 1, :], unmixed(normed_grad, mix), gains_ref, upstream
        )
        if extra:
            mixer_ref, upper_ref, feed_ref = extra_refs
            lines = [gains_ref[0:2, :], feed_ref[0:2, :], upper_ref[0:2, :], mixer_ref[6:, :]]
            lines = dot(jnp.concatenate(lines, axis=0).astype(BF16), mix)
            put(slice(wide + features, width), lines.T)

    outs = [
        shaped((tokens, features), F32),
        shaped((features // 2, wide + features + small), BF16),
        shaped((features // 2, wide + features + small), BF16),
        shaped((8, features), F32),
    ]
    ins = [start, *parts, mix, stream, rows, normed, packed, context, upstream, *extra]
    specs = [SCALAR] + [ANYWHERE] * count + [WHOLE] * (7 + len(extra))
    scratch = [
        pltpu.VMEM((tokens, wide), BF16),
        pltpu.VMEM((features, width), BF16),
        pltpu.SemaphoreType.DMA((count,)),
    ]
    return call(kernel, outs, ins, 22 * tokens * features * features, (), specs, None, scratch, LIGHT)


def feed_forward(stream, rows, expand, shrink, places, mix, depth):
    tokens, features = stream.shape
    inner_width = sum(p.shape[0] for p in shrink)
    step = inner_width // depth
    count, blocks = len(expand), places.shape[0]

    def kernel(*refs):
        places_ref = refs[0]
        expand_refs, shrink_refs = refs[1 : 1 + count], refs[1 + count : -10]
        mix_ref, stream_ref, rows_ref, out_ref, normed_ref, inner_ref = refs[-10:-4]
        expand_ref, shrink_ref, expand_sems, shrink_sems = refs[-4:]
        j = pl.program_id(0)

        @pl.when(j == 0)
        def _():
            wait_expand = start_parts(expand_refs, expand_ref, expand_sems)
            wait_shrink = start_blocks(shrink_refs, places_ref, shrink_ref, shrink_sems)
            x = stream_ref[...]
            normed = (normalize(x)[0] * rows_ref[2:3, :] + rows_ref[3:4, :]).astype(BF16)
            normed_ref[...] = mixed(normed, mix_ref[...])
            out_ref[...] = x
            wait_expand()
            wait_shrink()

        here = pl.ds(pl.multiple_of(j * step, 128), step)
        inner = dot(normed_ref[...], expand_ref[:, here])
        inner_ref[...] = inner
        out_ref[...] += dot(gelu(inner).astype(BF16), shrink_ref[here, :])

    fixed = lambda a: pl.BlockSpec(a.shape, lambda j: (0, 0))
    outs = [
        shaped((tokens, features), F32),
        shaped((tokens, features), BF16),
        shaped((tokens, inner_width), F32),
    ]
    return call(
        kernel,
        outs,
        [places, *expand, *shrink, mix, stream, rows],
        4 * tokens * features * inner_width,
        (depth,),
        [SCALAR] + [ANYWHERE] * (count + len(shrink)) + [fixed(mix), fixed(stream), fixed(rows)],
        [fixed(outs[0]), fixed(outs[1]), pl.BlockSpec((tokens, step), lambda j: (0, j))],
        [
            pltpu.VMEM((features, inner_width), BF16),
            pltpu.VMEM((inner_width, features), BF16),
            pltpu.SemaphoreType.DMA((count,)),
            pltpu.SemaphoreType.DMA((blocks,)),
        ],
        LIGHT,
    )


def feed_backward_shrink(shrink, places, depth, inner, upstream):
    tokens, features = upstream.shape
    inner_width = inner.shape[1]
    step = inner_width // depth
    count, blocks = len(shrink), places.shape[0]
    pieces = max(1, blocks // depth)
    piece = step // pieces
    side, half = max(1, pieces // 2), min(piece, step // 2)

    def kernel(places_ref, *refs):
        shrink_refs = refs[:count]
        inner_ref, up_ref, inner_grad_ref, near_ref, over_ref, active_ref, shrink_ref, sems = refs[count:]
        j = pl.program_id(0)

        @pl.when(j == 0)
        def _():
            start_blocks(shrink_refs, places_ref, shrink_ref, sems)()

        branch = up_ref[...].astype(BF16)
        active, slope = gelu_both(inner_ref[...])
        active_ref[...] = active.astype(BF16).T
        for p in range(pieces):
            start = 0
            if pieces > 1:
                start = pl.multiple_of(places_ref[p * depth + chunk_at(j, places_ref)] - j * step, 16)
            grad = dot(active_ref[pl.ds(start, piece), :], branch).astype(BF16)
            if pieces == 1:
                near_ref[0, 0] = grad[: step // 2]
                over_ref[0, 0] = grad[step // 2 :]
            elif p < pieces // 2:
                near_ref[p, 0] = grad
            else:
                over_ref[p - pieces // 2, 0] = grad
        here = pl.ds(pl.multiple_of(j * step, 128), step)
        inner_grad_ref[...] = (dot_nt(branch, shrink_ref[here, :]) * slope).astype(BF16)

    def chunk_at(j, places_ref):
        return lax.rem(places_ref[0] // step - j + depth, depth)

    def layer(j, places_ref):
        return (0, j if pieces == 1 else chunk_at(j, places_ref), 0, 0)

    columns = pl.BlockSpec((tokens, step), lambda j, places_ref: (0, j))
    outs = [
        shaped((tokens, inner_width), BF16),
        shaped((side, depth, half, features), BF16),
        shaped((side, depth, half, features), BF16),
    ]
    ins = [places, *shrink, inner, upstream]
    moved = sum(a.size * a.dtype.itemsize for a in (*ins, *outs))
    inner_grad, near, over = pl.pallas_call(
        kernel,
        out_shape=outs,
        grid_spec=pltpu.PrefetchScalarGridSpec(
            num_scalar_prefetch=1,
            grid=(depth,),
            in_specs=[ANYWHERE] * count
            + [columns, pl.BlockSpec(upstream.shape, lambda j, places_ref: (0, 0))],
            out_specs=[columns] + [pl.BlockSpec((side, 1, half, features), layer)] * 2,
            scratch_shapes=[
                pltpu.VMEM((step, tokens), BF16),
                pltpu.VMEM((inner_width, features), BF16),
                pltpu.SemaphoreType.DMA((blocks,)),
            ],
        ),
        compiler_params=pltpu.CompilerParams(vmem_limit_bytes=LIMIT),
        cost_estimate=cost(4 * tokens * features * inner_width, moved, LIGHT),
    )(*ins)
    if pieces == 1:
        shrink_grad = [jnp.concatenate([near, over], axis=2).reshape(inner_width, features)]
    else:
        shrink_grad = [near.reshape(-1, features), over.reshape(-1, features)]
    return inner_grad, shrink_grad


def feed_backward_expand(stream, rows, expand, mix, depth, normed, inner_grad, upstream):
    tokens, features = stream.shape
    inner_width = inner_grad.shape[1]
    step = inner_width // depth
    count = len(expand)

    def kernel(*refs):
        expand_refs = refs[:count]
        mix_ref, stream_ref, rows_ref, normed_ref, inner_grad_ref, up_ref = refs[count : count + 6]
        out_ref, mine_ref, other_ref, gains_ref, total_ref, turned_ref, expand_ref, sems = refs[count + 6 :]
        j = pl.program_id(0)

        @pl.when(j == 0)
        def _():
            wait = start_parts(expand_refs, expand_ref, sems)
            turned_ref[...] = normed_ref[...].T
            total_ref[...] = jnp.zeros_like(total_ref)
            wait()

        inner_grad = inner_grad_ref[...]
        expand_grad = dot(turned_ref[...], inner_grad).astype(BF16)
        mine_ref[...] = expand_grad[: features // 2]
        other_ref[...] = expand_grad[features // 2 :]
        here = pl.ds(pl.multiple_of(j * step, 128), step)
        total_ref[...] += dot_nt(inner_grad, expand_ref[:, here])

        @pl.when(j == depth - 1)
        def _():
            grad = unmixed(total_ref[...], mix_ref[...])
            out_ref[...] = norm_back(stream_ref[...], rows_ref[2:3, :], grad, gains_ref, up_ref[...])

    fixed = lambda a: pl.BlockSpec(a.shape, lambda j: (0, 0))
    columns = lambda height: pl.BlockSpec((height, step), lambda j: (0, j))
    outs = [
        shaped((tokens, features), F32),
        shaped((features // 2, inner_width), BF16),
        shaped((features // 2, inner_width), BF16),
        shaped((8, features), F32),
    ]
    out, mine, other, gains = call(
        kernel,
        outs,
        [*expand, mix, stream, rows, normed, inner_grad, upstream],
        4 * tokens * features * inner_width,
        (depth,),
        [ANYWHERE] * count
        + [fixed(mix), fixed(stream), fixed(rows), fixed(normed), columns(tokens), fixed(upstream)],
        [fixed(outs[0]), columns(features // 2), columns(features // 2), fixed(outs[3])],
        [
            pltpu.VMEM((tokens, features), F32),
            pltpu.VMEM((features, tokens), BF16),
            pltpu.VMEM((features, inner_width), BF16),
            pltpu.SemaphoreType.DMA((count,)),
        ],
        LIGHT,
    )
    return out, (mine, other), gains


def gate_of(logits, meta):
    lane = lax.broadcasted_iota(jnp.int32, logits.shape, 1)
    chosen = lane == meta[:, 0:1] + LANE
    return jax.nn.sigmoid(jnp.sum(jnp.where(chosen, logits, 0.0), axis=-1, keepdims=True)), chosen


def put_blocks(refs, columns, values):
    rows = values.shape[0] // len(refs)
    for k, ref in enumerate(refs):
        ref[:, columns] = values[k * rows : (k + 1) * rows]


def mixer_before(stream, rows, facts, teacher, meta, target, slots, experts):
    tokens, features = stream.shape

    def kernel(stream_ref, rows_ref, facts_ref, teacher_ref, meta_ref, target_ref, *refs):
        normed_ref, logits_ref = refs[:2]
        ahead_refs, back_refs = refs[2 : 2 + experts], refs[2 + experts :]
        x = stream_ref[...]
        normed = (normalize(x)[0] * rows_ref[6:7, :] + rows_ref[7:8, :]).astype(BF16)
        normed_ref[...] = normed
        dispatch = lax.broadcasted_iota(jnp.int32, (slots, tokens), 0) == target_ref[...]
        dispatch = dispatch.astype(F32).astype(BF16)
        put_blocks(ahead_refs, slice(None), dot(dispatch, normed).astype(BF16))
        logits = dot_nt(normed, rows_ref[...].astype(BF16))
        logits_ref[...] = logits
        meta = meta_ref[...]
        gate = gate_of(logits, meta)[0]
        factor = facts_ref[1:2, 0:1] * meta[:, 2:3].astype(F32) * gate
        offset = (factor * (x - teacher_ref[...].astype(F32))).astype(BF16)
        slope = factor * gate
        high = slope.astype(BF16)
        low = (slope - high.astype(F32)).astype(BF16)
        lane = lax.broadcasted_iota(jnp.int32, (tokens, 128), 1)
        slope = jnp.where(lane == 0, high.astype(F32), jnp.where(lane == 1, low.astype(F32), 0.0)).astype(BF16)
        put_blocks(back_refs, slice(0, features), dot(dispatch, offset).astype(BF16))
        put_blocks(back_refs, slice(features, None), dot(dispatch, slope).astype(BF16))

    outs = [
        shaped((tokens, features), BF16),
        shaped((tokens, rows.shape[0]), F32),
    ]
    outs += [shaped((slots // experts, features), BF16)] * experts
    outs += [shaped((slots // experts, features + 128), BF16)] * experts
    ins = [stream, rows, facts, teacher, meta, target]
    normed, logits, *blocks = call(kernel, outs, ins, 4 * slots * tokens * features)
    return normed, logits, blocks[:experts], blocks[experts:]


def expert_specs(weights, step):
    owners, height, features = weights.shape
    shrink_rows = height // 2
    expand_rows = features // owners
    each = step // shrink_rows
    first = shrink_rows // expand_rows
    expand = pl.BlockSpec(
        (owners, expand_rows, step), lambda j: (0, first + j * step // features, j * step % features // step)
    )
    return expand, pl.BlockSpec((each, shrink_rows, features), lambda j: (j, 0, 0))


def expert_forward(blocks, weights, depth):
    experts = len(blocks)
    rows, features = blocks[0].shape
    slots = experts * rows
    owners, height, _ = weights.shape
    inner_width = owners * height // 2
    step = inner_width // depth

    def kernel(*refs):
        block_refs, (expand_ref, shrink_ref) = refs[:experts], refs[experts : experts + 2]
        out_refs = refs[experts + 2 : 2 * experts + 2]
        arrived_ref, inner_ref, total_ref = refs[2 * experts + 2 :]
        j = pl.program_id(0)

        @pl.when(j == 0)
        def _():
            for k in range(experts):
                arrived_ref[k * rows : (k + 1) * rows, :] = block_refs[k][...]

        inner = dot(arrived_ref[...], expand_ref[...].reshape(features, step))
        inner_ref[...] = inner
        part = dot(gelu(inner).astype(BF16), shrink_ref[...].reshape(step, features))

        @pl.when(j == 0)
        def _():
            total_ref[...] = part

        @pl.when(j > 0)
        def _():
            total_ref[...] += part

        @pl.when(j == depth - 1)
        def _():
            put_blocks(out_refs, slice(None), total_ref[...].astype(BF16))

    fixed = lambda a: pl.BlockSpec(a.shape, lambda j: (0, 0))
    outs = [shaped((rows, features), BF16)] * experts
    outs += [shaped((slots, features), BF16), shaped((slots, inner_width), F32)]
    *result, arrived, inner = call(
        kernel,
        outs,
        [*blocks, weights, weights],
        4 * slots * features * inner_width,
        (depth,),
        [fixed(b) for b in blocks] + [*expert_specs(weights, step)],
        [fixed(o) for o in outs[:-1]] + [pl.BlockSpec((slots, step), lambda j: (0, j))],
        [pltpu.VMEM((slots, features), F32)],
    )
    return result, arrived, inner


def expert_backward(back, result, inner, weights, depth):
    experts = len(back)
    rows, features = result[0].shape
    slots = experts * rows
    owners, height, _ = weights.shape
    inner_width = owners * height // 2
    step = inner_width // depth

    def kernel(*refs):
        back_refs, result_refs = refs[:experts], refs[experts : 2 * experts]
        inner_ref, expand_ref, shrink_ref = refs[2 * experts : 2 * experts + 3]
        out_refs = refs[2 * experts + 3 : 3 * experts + 3]
        inner_grad_ref, grads_ref, landed_ref, total_ref = refs[3 * experts + 3 :]
        j = pl.program_id(0)

        @pl.when(j == 0)
        def _():
            for k in range(experts):
                terms = back_refs[k][:, features:].astype(F32)
                slope = terms[:, 0:1] + terms[:, 1:2]
                landed = back_refs[k][:, :features].astype(F32) + slope * result_refs[k][...].astype(F32)
                landed_ref[k * rows : (k + 1) * rows, :] = landed.astype(BF16)
            total_ref[...] = jnp.zeros_like(total_ref)

        active, slope = gelu_both(inner_ref[...])
        landed = landed_ref[...]
        inner_grad = (dot_nt(landed, shrink_ref[...].reshape(step, features)) * slope).astype(BF16)
        inner_grad_ref[...] = inner_grad
        grads_ref[...] = dot_tn(active.astype(BF16), landed).astype(BF16)
        total_ref[...] += dot_nt(inner_grad, expand_ref[...].reshape(features, step))

        @pl.when(j == depth - 1)
        def _():
            put_blocks(out_refs, slice(None), total_ref[...].astype(BF16))

    fixed = lambda a: pl.BlockSpec(a.shape, lambda j: (0, 0))
    columns = lambda height: pl.BlockSpec((height, step), lambda j: (0, j))
    outs = [shaped((rows, features), BF16)] * experts
    outs += [shaped((slots, inner_width), BF16), shaped((inner_width, features), BF16)]
    *rows_grad, inner_grad, grads = call(
        kernel,
        outs,
        [*back, *result, inner, weights, weights],
        6 * slots * features * inner_width,
        (depth,),
        [fixed(b) for b in (*back, *result)]
        + [
            columns(slots),
            *expert_specs(weights, step),
        ],
        [fixed(o) for o in outs[:-2]]
        + [columns(slots), pl.BlockSpec((step, features), lambda j: (j, 0))],
        [pltpu.VMEM((slots, features), BF16), pltpu.VMEM((slots, features), F32)],
        LIGHT,
    )
    return rows_grad, inner_grad, grads


def expert_expand_grad(arrived, inner_grad):
    slots, features = arrived.shape
    inner_width = inner_grad.shape[1]

    def kernel(arrived_ref, inner_grad_ref, out_ref, turned_ref):
        @pl.when(pl.program_id(0) == 0)
        def _():
            turned_ref[...] = arrived_ref[...].T

        out_ref[...] = dot(turned_ref[...], inner_grad_ref[...]).astype(BF16)

    columns = lambda height: pl.BlockSpec((height, features), lambda j: (0, j))
    [grad] = call(
        kernel,
        [shaped((features, inner_width), BF16)],
        [arrived, inner_grad],
        2 * slots * features * inner_width,
        (inner_width // features,),
        [pl.BlockSpec(arrived.shape, lambda j: (0, 0)), columns(slots)],
        [columns(features)],
        [pltpu.VMEM((features, slots), BF16)],
        LIGHT,
    )
    return grad


def mixer_after(stream, rows, facts, teacher, meta, normed, logits, returned, rows_grad, experts):
    tokens, features = stream.shape
    block = returned[0].shape[0]
    slots = experts * block

    def kernel(*refs):
        stream_ref, rows_ref, facts_ref, teacher_ref, meta_ref, normed_ref, logits_ref = refs[:7]
        returned_refs, rows_grad_refs = refs[7 : 7 + experts], refs[7 + experts : 7 + 2 * experts]
        states_ref, grad_ref, small_ref, squared_ref = refs[7 + 2 * experts :]
        x = stream_ref[...]
        meta = meta_ref[...]
        combine = lax.broadcasted_iota(jnp.int32, (tokens, slots), 1) == meta[:, 1:2]
        combine = combine.astype(F32).astype(BF16)
        combined = dot(combine, jnp.concatenate([r[...] for r in returned_refs], axis=0))
        logits = logits_ref[...]
        gate, chosen = gate_of(logits, meta)
        final = x + gate * combined
        states_ref[...] = final.astype(BF16)
        valid = meta[:, 2:3].astype(F32)
        difference = final - teacher_ref[...].astype(F32)
        masked = valid * difference
        squared = 0.5 * jnp.sum(jnp.sum(masked * difference, axis=-1, keepdims=True), axis=0, keepdims=True)
        squared_ref[...] = jnp.broadcast_to(squared, squared_ref.shape)
        upstream = facts_ref[1:2, 0:1] * masked
        gate_grad = jnp.sum(upstream * combined, axis=-1, keepdims=True)
        lane = lax.broadcasted_iota(jnp.int32, logits.shape, 1)
        real = (lane >= LANE) & (lane < LANE + experts)
        shown = jnp.where(real, logits, -1e30)
        exponent = jnp.exp(shown - jnp.max(shown, axis=-1, keepdims=True))
        probs = exponent / jnp.sum(exponent, axis=-1, keepdims=True)
        share = facts_ref[0:1, :]
        tilt = jnp.sum(probs * share, axis=-1, keepdims=True)
        logits_grad = facts_ref[2:3, 0:1] * valid * probs * (share - tilt)
        logits_grad = jnp.where(real, logits_grad, 0.0)
        logits_grad += jnp.where(chosen, gate_grad * gate * (1.0 - gate), 0.0)
        first = logits_grad.astype(BF16)
        left = logits_grad - first.astype(F32)
        second = left.astype(BF16)
        third = (left - second.astype(F32)).astype(BF16)
        weights = rows_ref[...].astype(BF16)
        normed = normed_ref[...]
        normed_grad = dot(combine, jnp.concatenate([r[...] for r in rows_grad_refs], axis=0))
        normed_grad += dot(third, weights) + dot(second, weights) + dot(first, weights)
        small_ref[...] = dot_tn(third, normed) + dot_tn(second, normed) + dot_tn(first, normed)
        grad_ref[...] = norm_back(x, rows_ref[6:7, :], normed_grad, small_ref.at[6:8], upstream)

    outs = [
        shaped((tokens, features), BF16),
        shaped((tokens, features), F32),
        shaped(rows.shape, F32),
        shaped((8, 128), F32),
    ]
    ins = [stream, rows, facts, teacher, meta, normed, logits, *returned, *rows_grad]
    return call(kernel, outs, ins, 4 * slots * tokens * features)


def body(
    tokens,
    teacher,
    routes,
    piece_start,
    valid_mask,
    lower_gain,
    lower_bias,
    lower_triple,
    lower_output,
    feed_gain,
    feed_bias,
    feed_expand,
    feed_shrink,
    upper_gain,
    upper_bias,
    upper_triple,
    upper_output,
    mixer_gain,
    mixer_bias,
    router,
    expert_expand,
    expert_shrink,
):
    count, length, features = tokens.shape
    local = count * length
    experts = router.shape[1]
    share_rows = router.shape[0]
    devices = lax.axis_size("dp") * lax.axis_size("expert")
    capacity = max(2, 2 * length // experts)
    total_tokens = local * devices
    valid = valid_mask.astype(F32)
    route = routes[..., 0]
    chosen = (route[..., None] == jnp.arange(experts, dtype=jnp.int32)).astype(F32)

    vectors = [lower_gain, lower_bias, feed_gain, feed_bias, upper_gain, upper_bias, mixer_gain, mixer_bias]
    extra_width = 128

    wide = 3 * features
    depth = lax.axis_size("dp") // 2

    row_order = (order(share_rows)[:, None] + jnp.arange(share_rows, dtype=jnp.int32)).reshape(1, features)
    mix = (jnp.arange(features, dtype=jnp.int32)[:, None] == row_order).astype(BF16)
    shrink_rows = feed_shrink.shape[0]
    inner_width = feed_expand.shape[1]
    inner_width = feed_expand.shape[1]
    lower_own = pack_lower(lower_triple, lower_output, vectors, router.T, route, valid_mask)
    upper_own = jnp.concatenate([upper_triple, upper_output], axis=1)

    position = jnp.arange(length, dtype=jnp.int32)
    earlier = (position[:, None] > position[None, :]).astype(BF16)
    before = jnp.einsum("qk,mke->mqe", earlier, chosen.astype(BF16), preferred_element_type=F32)
    slot = jnp.sum(before * chosen, axis=-1).astype(jnp.int32)
    target = (route ^ lax.axis_index("expert")) * (count * capacity) + jnp.arange(count, dtype=jnp.int32)[:, None] * capacity + slot
    slots = experts * count * capacity
    meta = jnp.stack([route.reshape(-1), target.reshape(-1), valid_mask.reshape(-1)], axis=1)
    target = target.reshape(1, local)

    stream_in = tokens.reshape(local, features)
    labels = teacher.reshape(local, features)
    places = order(shrink_rows)
    pieces = expert_expand[0].reshape(-1, inner_width // features, features)
    experts_own = jnp.concatenate([expert_shrink[0], jnp.moveaxis(pieces, 1, 0).reshape(-1, features)])

    shrink_line, shrink_over = gather_lines(feed_shrink)
    wide_line, wide_over = gather_lines(jnp.concatenate([feed_expand, upper_own], axis=1))
    lower = pull_line(lower_own)

    lower, experts_own, mix, meta, target, places = at_once((lower, experts_own, mix, meta, target, places))
    experts_full = lax.all_gather(experts_own, "dp")
    lower = jnp.stack([lower_own, *lower])
    near = pull_near(lower)

    lower, near, shrink_line, shrink_over = at_once((lower, near, shrink_line, shrink_over))
    lower = pull_far(lower, near)
    shrink_near = pull_near(shrink_line)

    lower, shrink_line, shrink_near = at_once((lower, shrink_line, shrink_near))
    lower_over = pull_over(lower[1])

    lower, lower_over, wide_line, wide_over = at_once((lower, lower_over, wide_line, wide_over))
    lower = in_order(*lower, lower_over)
    shrink_full = pull_far(shrink_line, shrink_near, shrink_over)
    expand_line, expand_over = wide_line[..., :inner_width], wide_over[..., :inner_width]
    upper_line, upper_over = wide_line[..., inner_width:], wide_over[..., inner_width:]
    expand_near = pull_near(expand_line)
    rows, stream_one, *stored_one = attend_forward(0, stream_in, None, lower, 0, mix, piece_start, length)

    shrink_full, expand_line, expand_near, rows, stream_one = at_once(
        (shrink_full, expand_line, expand_near, rows, stream_one)
    )
    shrink_full = in_order(*shrink_full, pull_over(shrink_full[1]))
    expand_full = pull_far(expand_line, expand_near, expand_over)
    upper_near = pull_near(upper_line)
    lane = jnp.arange(features, dtype=jnp.int32)
    sums = rows[LANE + experts : LANE + 2 * experts + 1]
    sums = jnp.sum(jnp.where(lane % share_rows < count, sums, 0.0), axis=1)
    valid_total = sums[experts]
    loss_ratio = total_tokens / valid_total
    balance_scale = total_tokens * features * 0.1 * experts / valid_total
    share = jnp.pad(sums[:experts] / valid_total, (LANE, extra_width - LANE - experts))
    facts = jnp.stack([share, jnp.full_like(share, loss_ratio), jnp.full_like(share, balance_scale)])
    facts = jnp.pad(facts, ((0, 5), (0, 0)))

    shrink_full, expand_full, upper_line, upper_near, stream_one, facts = at_once(
        (shrink_full, expand_full, upper_line, upper_near, stream_one, facts)
    )
    expand_full = in_order(*expand_full, pull_over(expand_full[1]))

    expand_full, upper_line, upper_near, stream_one = at_once((expand_full, upper_line, upper_near, stream_one))
    upper = pull_far(upper_line, upper_near, upper_over)

    if shrink_rows % 16:
        whole = jnp.concatenate(shrink_full, axis=0).reshape(devices, shrink_rows, features)
        shrink_full = [jnp.zeros_like(whole).at[places // shrink_rows].set(whole).reshape(-1, features)]
        places = jnp.zeros((1,), jnp.int32)
    stream_two, *stored_two = feed_forward(stream_one, rows, expand_full, shrink_full, places, mix, depth)

    upper, stream_two = at_once((upper, stream_two))
    upper = in_order(*upper, pull_over(upper[1]))
    stream_three, *stored_three = attend_forward(4, stream_two, rows, upper, 0, mix, piece_start, length)
    normed, logits, ahead, back = mixer_before(
        stream_three, rows, facts, labels, meta, target, slots, experts
    )
    ahead = exchange(ahead)
    back = exchange([after(b, *ahead) for b in back])
    result, arrived, inner = expert_forward(ahead, experts_full, depth)
    returned = exchange(result)
    rows_grad, inner_grad, expert_out_grad = expert_backward(back, result, inner, experts_full, depth)
    returned, rows_grad, inner_grad, expert_out_grad = at_once((returned, rows_grad, inner_grad, expert_out_grad))
    expert_out_grad = lax.psum_scatter(expert_out_grad, "dp", scatter_dimension=0, tiled=True)
    rows_grad = exchange(rows_grad)
    states, grad_three, mixer_small, squared = mixer_after(
        stream_three, rows, facts, labels, meta, normed, logits, returned, rows_grad, experts
    )
    grad_two, *upper_grad, upper_small = attend_backward(
        4, stream_two, rows, upper, 0, mix, piece_start, length, stored_three, grad_three
    )
    hops = total_hops()

    def hop_loss(value, first, last):
        for target in hops[first:last] if hops else ():
            value = value + hop(value, target)
        return value

    inner_grad = after(inner_grad, grad_two)
    upper_mine, upper_other = upper_grad
    upper_other = swap_cores(upper_other)
    expert_in_grad = expert_expand_grad(arrived, inner_grad)

    upper_mine, upper_other, expert_in_grad, grad_two = at_once((upper_mine, upper_other, expert_in_grad, grad_two))
    expert_in_grad = lax.psum_scatter(expert_in_grad, "dp", scatter_dimension=0, tiled=True)
    upper_part = sum_cores(upper_mine, upper_other)

    grad_two, *upper_part = at_once((grad_two, *upper_part))
    upper_part = scatter_far(upper_part)
    squared = hop_loss(squared, 0, 1)
    feed_normed, inner_pre = stored_two
    inner_grad, shrink_grad = feed_backward_shrink(shrink_full, places, depth, inner_pre, grad_two)
    if shrink_rows % 16:
        blocks = order(shrink_rows) // shrink_rows
        pick = (blocks[:, None] == jnp.arange(devices, dtype=jnp.int32)).astype(BF16)
        shrink_grad = dot(pick, shrink_grad[0].reshape(devices, -1)).astype(BF16).reshape(2, -1, features)
        shrink_grad = [shrink_grad[0], shrink_grad[1]]

    upper_part, squared, inner_grad, shrink_grad = at_once((upper_part, squared, inner_grad, shrink_grad))
    upper_part = scatter_near(upper_part)
    squared = hop_loss(squared, 1, 2)
    shrink_mine, shrink_other = shrink_grad
    shrink_other = swap_cores(shrink_other)
    grad_one, expand_grad, feed_small = feed_backward_expand(
        stream_one, rows, expand_full, mix, depth, feed_normed, inner_grad, grad_two
    )

    upper_part, squared, shrink_mine, shrink_other, expand_grad, grad_one = at_once(
        (upper_part, squared, shrink_mine, shrink_other, expand_grad, grad_one)
    )
    shrink_part = scatter_far(sum_cores(shrink_mine, shrink_other))
    expand_part = scatter_cores(*expand_grad)
    squared = hop_loss(squared, 2, 3)

    upper_part, expand_part, shrink_part, grad_one, squared = at_once(
        (upper_part, expand_part, shrink_part, grad_one, squared)
    )
    expand_part = scatter_far(expand_part)
    shrink_part = scatter_near(shrink_part)
    upper_part = scatter_line(upper_part)
    grad_in, *lower_grad, _ = attend_backward(
        0, stream_in, rows, lower, 0, mix, piece_start, length, stored_one, grad_one, (mixer_small, upper_small, feed_small)
    )

    upper_part, expand_part, shrink_part, grad_in, lower_grad, squared = at_once(
        (upper_part, expand_part, shrink_part, grad_in, lower_grad, squared)
    )
    lower_part = scatter_cores(*lower_grad)
    expand_part = scatter_near(expand_part)
    shrink_part = scatter_line(shrink_part)

    lower_part, expand_part, shrink_part, upper_part, squared = at_once(
        (lower_part, expand_part, shrink_part, upper_part, squared)
    )
    lower_part = scatter_far(lower_part)
    expand_part = scatter_line(expand_part)
    squared = hop_loss(squared, 3, 4)
    upper_part, shrink_part = total(upper_part), total(shrink_part)
    expert_out_grad, expert_in_grad = expert_out_grad.astype(F32), expert_in_grad.astype(F32)

    lower_part, expand_part, shrink_part, upper_part, squared, expert_in_grad, expert_out_grad = at_once(
        (lower_part, expand_part, shrink_part, upper_part, squared, expert_in_grad, expert_out_grad)
    )
    lower_part = scatter_near(lower_part)
    squared = hop_loss(squared, 4, None)

    lower_part, expand_part, squared = at_once((lower_part, expand_part, squared))
    lower_part, expand_part = total(scatter_line(lower_part)), total(expand_part)
    if hops is None:
        squared = lax.psum(squared, AXES)
    small = lower_part[:, wide + features :]
    squared_total = squared[0, 0]
    mean_loss = loss_ratio * squared_total / (total_tokens * features)
    return (
        states.reshape(tokens.shape),
        grad_in.reshape(tokens.shape),
        small[:, 0],
        small[:, 1],
        lower_part[:, :wide],
        lower_part[:, wide : wide + features],
        small[:, 2],
        small[:, 3],
        expand_part,
        shrink_part,
        small[:, 4],
        small[:, 5],
        upper_part[:, :wide],
        upper_part[:, wide:],
        small[:, 6],
        small[:, 7],
        small[:, 8 : 8 + experts],
        expert_in_grad[None],
        expert_out_grad[None],
        mean_loss,
    )


def solution(mesh):
    both = ("dp", "expert")
    token = P(both, None, None)
    vector = P(both)
    matrix = P(both, None)
    expert = P("expert", "dp", None)
    dense = (vector, vector, matrix, matrix, vector, vector, matrix, matrix)
    weights = dense + (vector, vector, matrix, matrix, vector, vector, matrix, expert, expert)
    return jax.shard_map(
        body,
        mesh=mesh,
        in_specs=(token, token, token, vector, matrix) + weights,
        out_specs=(token, token) + weights + (P(),),
        check_vma=False,
    )
```

```python
import math

import jax
import jax.numpy as jnp
from jax import lax
from jax.experimental import pallas as pl
from jax.experimental.pallas import tpu as pltpu
from jax.sharding import PartitionSpec as P

HD = 64
AXES = ("dp", "expert")
F32 = jnp.float32
BF16 = jnp.bfloat16


def place():
    depth = lax.axis_size("dp") // 2
    row = lax.axis_index("dp")
    return depth, lax.axis_size("expert"), row // 2, row % 2, lax.axis_index("expert")


def pairs(target):
    depth, across = lax.axis_size("dp") // 2, lax.axis_size("expert")
    out = []
    for z in range(depth):
        for c in range(2):
            for e in range(across):
                to = target(z, c, e)
                if to is not None and 0 <= to[0] < depth:
                    out.append(((z * 2 + c) * across + e, (to[0] * 2 + to[1]) * across + to[2]))
    return out


def hop(values, target):
    return lax.ppermute(values, AXES, pairs(target))


def swap_cores(values):
    return hop(values, lambda z, c, e: (z, 1 - c, e))


def first_side(values):
    return hop(values, lambda z, c, e: (z, c, e ^ (1 + c)))


def second_side(values):
    return hop(values, lambda z, c, e: (z, c, e ^ (2 - c)))


at_once = lax.optimization_barrier


def after(value, *others):
    return lax.optimization_barrier((value, *others))[0]


def shift(values, by):
    depth = place()[0]
    return hop(values, lambda z, c, e: ((z + by) % depth, c, e))


def pull_line(own):
    return [shift(own, k) for k in range(1, place()[0])]


def gather_lines(own):
    depth, _, z, c, _ = place()
    both = lax.all_gather(own, "dp", axis=0, tiled=True).reshape(depth, 2, *own.shape)
    zero = jnp.zeros_like(z)
    at = lambda k, core: lax.dynamic_slice(both, ((z - k) % depth, core, zero, zero), (1, 1, *own.shape))[0]
    return [jnp.concatenate([at(k, core) for k in range(depth)]) for core in (c, 1 - c)]


def pull_near(line):
    return first_side(line) if place()[1] == 4 else line


def pull_far(line, near, over=None):
    if place()[1] != 4:
        whole = lax.all_gather(line, "expert", axis=1)
        return [whole], None, [swap_cores(whole)]
    pair = jnp.stack([line, near])
    side = [swap_cores(pair)] if over is None else [over, swap_cores(near)]
    return [pair], second_side(pair), side


def pull_over(far):
    return None if far is None else swap_cores(far)


def in_order(pair, far, pair_over, far_over):
    return [p.reshape(-1, p.shape[-1]) for p in (*pair, far, *pair_over, far_over) if p is not None]


def order(rows):
    depth, across, z, c, e = place()
    k = jnp.arange(depth, dtype=jnp.int32)
    layer = (z - k) % depth
    if across == 4:
        there = jnp.stack([e, e ^ (1 + c), e ^ (2 - c), e ^ 3])
        over = jnp.stack([e, e ^ (2 - c), e ^ (1 + c), e ^ 3])
    else:
        there = over = jnp.arange(across, dtype=jnp.int32)
    first = (layer * 2 + c)[None, :] * across + there[:, None]
    second = (layer * 2 + 1 - c)[None, :] * across + over[:, None]
    if across != 4:
        first, second = first.T, second.T
    return jnp.concatenate([first.reshape(-1), second.reshape(-1)]) * rows


def add(first, second):
    return (first.astype(F32) + second.astype(F32)).astype(BF16)


def scatter_line(line):
    return [line[0]] + [shift(line[k], -k) for k in range(1, place()[0])]


def total(parts):
    return sum(p.astype(F32) for p in parts[1:]) + parts[0].astype(F32)


def scatter_cores(mine, other):
    return sum_cores(mine, swap_cores(other))


def sum_cores(mine, other):
    depth, across, _, _, _ = place()
    if across != 4:
        return [add(mine, other).reshape(depth, across, -1, mine.shape[1])]
    half = mine.shape[0] // 2
    return [add(mine[:half], other[:half]), add(mine[half:], other[half:])]


def scatter_far(parts):
    return [parts[0], second_side(parts[1])] if len(parts) == 2 else parts


def scatter_near(parts):
    depth = place()[0]
    if len(parts) == 1:
        return lax.psum_scatter(parts[0], "expert", scatter_dimension=1, tiled=True)[:, 0]
    half = parts[0].shape[0] // 2
    mine, come = parts
    line = add(add(mine[:half], come[:half]), first_side(add(mine[half:], come[half:])))
    return line.reshape(depth, -1, line.shape[1])


def total_hops():
    depth, across, _, _, _ = place()
    if across & (across - 1) or depth & (depth - 1):
        return None
    hops = [lambda z, c, e: (z, 1 - c, e)]
    step = 1
    while step < across:
        hops.append(lambda z, c, e, step=step: (z, c, e ^ step))
        step *= 2
    step = 1
    while step < depth:
        hops.append(lambda z, c, e, step=step: (z ^ step, c, e))
        step *= 2
    return hops


def exchange(blocks):
    return [blocks[0]] + [
        hop(blocks[k], lambda z, c, e: (z, c, e ^ k)) for k in range(1, len(blocks))
    ]


LIMIT = 60 * 1024 * 1024
LANE = 8
LIGHT = 1000


def cost(flops, moved, light=1):
    return pl.CostEstimate(flops=flops // light, bytes_accessed=moved // light, transcendentals=0)


WHOLE = pl.BlockSpec(memory_space=pltpu.VMEM)
SCALAR = pl.BlockSpec(memory_space=pltpu.SMEM)


def dot(a, b):
    return jnp.dot(a, b, preferred_element_type=F32)


def dot_nt(a, b):
    return lax.dot_general(a, b, (((1,), (1,)), ((), ())), preferred_element_type=F32)


def dot_tn(a, b):
    return lax.dot_general(a, b, (((0,), (0,)), ((), ())), preferred_element_type=F32)


def call(kernel, outs, ins, flops, grid=(), in_specs=None, out_specs=None, scratch=(), light=1):
    moved = sum(a.size * a.dtype.itemsize for a in (*ins, *outs))
    return pl.pallas_call(
        kernel,
        out_shape=outs,
        grid=grid,
        in_specs=in_specs or [WHOLE] * len(ins),
        out_specs=out_specs or [WHOLE] * len(outs),
        scratch_shapes=scratch,
        compiler_params=pltpu.CompilerParams(vmem_limit_bytes=LIMIT),
        cost_estimate=cost(flops, moved, light),
    )(*ins)


ANYWHERE = pl.BlockSpec(memory_space=pl.ANY)


def start_parts(parts, whole, sems, first=0):
    copies, at = [], 0
    for k, part in enumerate(parts):
        rows = part.shape[0]
        copies.append(pltpu.make_async_copy(part.at[:, first : first + whole.shape[1]], whole.at[at : at + rows], sems.at[k]))
        at += rows
    for copy in copies:
        copy.start()

    def wait():
        for copy in copies:
            copy.wait()

    return wait


def start_blocks(parts, places, whole, sems):
    rows = whole.shape[0] // places.shape[0]
    copies = []
    for part in parts:
        for b in range(part.shape[0] // rows):
            k = len(copies)
            at = pl.multiple_of(places[k], 16)
            copies.append(
                pltpu.make_async_copy(part.at[b * rows : (b + 1) * rows], whole.at[pl.ds(at, rows)], sems.at[k])
            )
    for copy in copies:
        copy.start()

    def wait():
        for copy in copies:
            copy.wait()

    return wait


def mixed(values, mix):
    return dot(values, mix).astype(BF16)


def unmixed(values, mix):
    high = values.astype(BF16)
    low = (values - high.astype(F32)).astype(BF16)
    return dot_nt(low, mix) + dot_nt(high, mix)


def shaped(shape, dtype):
    return jax.ShapeDtypeStruct(shape, dtype)


def normalize(x):
    centered = x - jnp.mean(x, axis=-1, keepdims=True)
    scale = lax.rsqrt(jnp.mean(centered * centered, axis=-1, keepdims=True) + 1e-05)
    return centered * scale, scale


def norm_back(x, gain, grad, gains_ref, upstream):
    unit, scale = normalize(x)
    gains_ref[0:1, :] = jnp.sum(grad * unit, axis=0, keepdims=True)
    gains_ref[1:2, :] = jnp.sum(grad, axis=0, keepdims=True)
    inner = grad * gain
    middle = jnp.mean(inner, axis=-1, keepdims=True)
    tilt = jnp.mean(inner * unit, axis=-1, keepdims=True)
    return upstream + scale * (inner - middle - unit * tilt)


ROOT = math.sqrt(2.0 / math.pi)


def gelu(x):
    return 0.5 * x * (1.0 + jnp.tanh(ROOT * (x + 0.044715 * (x * x * x))))


def gelu_both(x):
    square = x * x
    slope = jnp.tanh(ROOT * x * (1.0 + 0.044715 * square))
    half = 0.5 * (1.0 + slope)
    return x * half, half + 0.5 * x * (1.0 - slope * slope) * (ROOT * (1.0 + 0.134145 * square))


def allowed_pair(start, length):
    row = lax.broadcasted_iota(jnp.int32, (2 * length, length), 0)
    row = jnp.where(row >= length, row - length, row)
    column = lax.broadcasted_iota(jnp.int32, (2 * length, length), 1)
    piece = length // 4
    inside = (row >= start) & (row < start + piece) & (column >= start) & (column < start + piece)
    return (column <= row) | inside


def apart(pair):
    low = lax.broadcasted_iota(jnp.int32, pair.shape, 1) < HD
    zero = jnp.zeros_like(pair)
    return jnp.concatenate([jnp.where(low, pair, zero), jnp.where(low, zero, pair)], axis=0)


def together(stacked):
    half = stacked.shape[0] // 2
    low = lax.broadcasted_iota(jnp.int32, (half, stacked.shape[1]), 1) < HD
    return jnp.where(low, stacked[:half], stacked[half:])


def softmax_pair(queries, keys, allowed):
    scores = jnp.where(allowed, dot_nt(queries, keys) * HD ** (-0.5), -1e30)
    exponent = jnp.exp(scores - jnp.max(scores, axis=-1, keepdims=True))
    return exponent / jnp.sum(exponent, axis=-1, keepdims=True)


def pack_lower(triple, output, vectors, router, route, valid):
    share = triple.shape[0]
    experts = router.shape[0]
    wide, features = triple.shape[1], output.shape[1]

    def kernel(triple_ref, output_ref, *refs):
        vector_refs = refs[:LANE]
        router_ref, route_ref, valid_ref, out_ref, turned_ref = refs[LANE:]
        turned_ref[...] = jnp.zeros_like(turned_ref)
        for k in range(LANE):
            turned_ref[k : k + 1, :share] = vector_refs[k][...].astype(F32)
        turned_ref[LANE : LANE + experts, :share] = router_ref[...].astype(F32)
        valid = valid_ref[...].astype(F32)
        route = route_ref[...]
        lane = lax.broadcasted_iota(jnp.int32, (valid.shape[0], 128), 1) - LANE - experts
        counts = jnp.where(lane == experts, jnp.sum(valid, axis=-1, keepdims=True), 0.0)
        for e in range(experts):
            count = jnp.sum(jnp.where(route == e, valid, 0.0), axis=-1, keepdims=True)
            counts += jnp.where(lane == e, count, 0.0)
        counts = jnp.concatenate([counts, jnp.zeros((share - counts.shape[0], 128), F32)], axis=0)
        out_ref[:, :wide] = triple_ref[...]
        out_ref[:, wide : wide + features] = output_ref[...]
        out_ref[:, wide + features :] = (turned_ref[...].T[:share] + counts).astype(BF16)

    [packed] = call(
        kernel,
        [shaped((share, wide + features + 128), BF16)],
        [triple, output, *(v.reshape(1, share) for v in vectors), router, route, valid],
        1,
        scratch=[pltpu.VMEM((128, 128), F32)],
    )
    return packed


def attend_forward(at, stream, rows, parts, first, mix, start, length):
    tokens, features = stream.shape
    wide = 3 * features
    width = parts[0].shape[1] - first
    count = len(parts)

    def kernel(*refs):
        start_ref, stream_ref, mix_ref = refs[:3]
        part_refs = refs[3 : 3 + count]
        out_ref, normed_ref, packed_ref, context_ref = refs[-6:-2]
        rows_ref, weights_ref, sems = refs[-7 if rows is None else 3 + count], refs[-2], refs[-1]
        wait = start_parts(part_refs, weights_ref, sems, first)
        x = stream_ref[...].astype(F32)
        unit = normalize(x)[0]
        mix = mix_ref[...]
        wait()
        if rows is None:
            rows_ref[...] = lax.dot_general(
                weights_ref[:, wide + features :], mix, (((0,), (1,)), ((), ())), preferred_element_type=F32
            )
        normed = (unit * rows_ref[at : at + 1, :] + rows_ref[at + 1 : at + 2, :]).astype(BF16)
        normed = mixed(normed, mix)
        normed_ref[...] = normed
        for j in range(3):
            columns = slice(j * features, (j + 1) * features)
            packed_ref[:, columns] = dot(normed, weights_ref[:, columns]).astype(BF16)
        for s in range(tokens // length):
            allowed = allowed_pair(start_ref[s], length)
            here = slice(s * length, (s + 1) * length)
            for p in range(features // (2 * HD)):
                at_q, at_k, at_v = (slice(j * features + p * 2 * HD, j * features + (p + 1) * 2 * HD) for j in range(3))
                probs = softmax_pair(apart(packed_ref[here, at_q]), packed_ref[here, at_k], allowed)
                context_ref[here, at_q] = together(dot(probs.astype(BF16), packed_ref[here, at_v])).astype(BF16)
        context = mixed(context_ref[...], mix)
        context_ref[...] = context
        out_ref[...] = x + dot(context, weights_ref[:, wide : wide + features])

    outs = [
        shaped((tokens, features), F32),
        shaped((tokens, features), BF16),
        shaped((tokens, wide), BF16),
        shaped((tokens, features), BF16),
    ]
    ins = [start, stream, mix, *parts]
    specs = [SCALAR, WHOLE, WHOLE] + [ANYWHERE] * count
    if rows is None:
        outs = [shaped((width - wide - features, features), F32)] + outs
    else:
        ins, specs = ins + [rows], specs + [WHOLE]
    scratch = [
        pltpu.VMEM((features, width), BF16),
        pltpu.SemaphoreType.DMA((count,)),
    ]
    return call(kernel, outs, ins, 10 * tokens * features * features, (), specs, None, scratch, LIGHT)


def attend_backward(at, stream, rows, parts, first, mix, start, length, stored, upstream, extra=()):
    normed, packed, context = stored
    tokens, features = stream.shape
    wide = 3 * features
    width = parts[0].shape[1] - first
    small = width - wide - features if extra else 0
    count = len(parts)

    def kernel(*refs):
        start_ref = refs[0]
        part_refs = refs[1 : 1 + count]
        mix_ref, stream_ref, rows_ref, normed_ref, packed_ref, context_ref, up_ref = refs[1 + count : 8 + count]
        extra_refs = refs[8 + count : 8 + count + len(extra)]
        out_ref, mine_ref, other_ref, gains_ref, delta_ref, weights_ref, sems = refs[8 + count + len(extra) :]
        wait = start_parts(part_refs, weights_ref, sems, first)

        def put(columns, values):
            mine_ref[:, columns] = values[: features // 2].astype(BF16)
            other_ref[:, columns] = values[features // 2 :].astype(BF16)

        upstream = up_ref[...]
        branch = upstream.astype(BF16)
        mix = mix_ref[...]
        put(slice(wide, wide + features), dot_tn(context_ref[...], branch))
        wait()
        context_grad = dot_nt(branch, weights_ref[:, wide : wide + features]).astype(BF16)
        context_grad = dot_nt(context_grad, mix).astype(BF16)
        scale = HD ** (-0.5)
        for s in range(tokens // length):
            allowed = allowed_pair(start_ref[s], length)
            here = slice(s * length, (s + 1) * length)
            for p in range(features // (2 * HD)):
                at_q, at_k, at_v = (slice(j * features + p * 2 * HD, j * features + (p + 1) * 2 * HD) for j in range(3))
                queries, keys, values = apart(packed_ref[here, at_q]), packed_ref[here, at_k], packed_ref[here, at_v]
                probs = softmax_pair(queries, keys, allowed)
                out_grad = apart(context_grad[here, at_q])
                delta_ref[here, at_v] = dot_tn(probs.astype(BF16), out_grad).astype(BF16)
                prob_grad = dot_nt(out_grad, values)
                middle = jnp.sum(probs * prob_grad, axis=-1, keepdims=True)
                score_grad = (probs * (prob_grad - middle)).astype(BF16)
                delta_ref[here, at_q] = (together(dot(score_grad, keys)) * scale).astype(BF16)
                delta_ref[here, at_k] = (dot_tn(score_grad, queries) * scale).astype(BF16)
        turned = normed_ref[...].T
        normed_grad = jnp.zeros((tokens, features), F32)
        for j in range(3):
            columns = slice(j * features, (j + 1) * features)
            put(columns, dot(turned, delta_ref[:, columns]))
            normed_grad += dot_nt(delta_ref[:, columns], weights_ref[:, columns])
        out_ref[...] = norm_back(
            stream_ref[...].astype(F32), rows_ref[at : at + 1, :], unmixed(normed_grad, mix), gains_ref, upstream
        )
        if extra:
            mixer_ref, upper_ref, feed_ref = extra_refs
            lines = [gains_ref[0:2, :], feed_ref[0:2, :], upper_ref[0:2, :], mixer_ref[6:, :]]
            lines = dot(jnp.concatenate(lines, axis=0).astype(BF16), mix)
            put(slice(wide + features, width), lines.T)

    outs = [
        shaped((tokens, features), F32),
        shaped((features // 2, wide + features + small), BF16),
        shaped((features // 2, wide + features + small), BF16),
        shaped((8, features), F32),
    ]
    ins = [start, *parts, mix, stream, rows, normed, packed, context, upstream, *extra]
    specs = [SCALAR] + [ANYWHERE] * count + [WHOLE] * (7 + len(extra))
    scratch = [
        pltpu.VMEM((tokens, wide), BF16),
        pltpu.VMEM((features, width), BF16),
        pltpu.SemaphoreType.DMA((count,)),
    ]
    return call(kernel, outs, ins, 22 * tokens * features * features, (), specs, None, scratch, LIGHT)


def feed_forward(stream, rows, expand, shrink, places, mix, depth):
    tokens, features = stream.shape
    inner_width = sum(p.shape[0] for p in shrink)
    step = inner_width // depth
    count, blocks = len(expand), places.shape[0]

    def kernel(*refs):
        places_ref = refs[0]
        expand_refs, shrink_refs = refs[1 : 1 + count], refs[1 + count : -10]
        mix_ref, stream_ref, rows_ref, out_ref, normed_ref, inner_ref = refs[-10:-4]
        expand_ref, shrink_ref, expand_sems, shrink_sems = refs[-4:]
        j = pl.program_id(0)

        @pl.when(j == 0)
        def _():
            wait_expand = start_parts(expand_refs, expand_ref, expand_sems)
            wait_shrink = start_blocks(shrink_refs, places_ref, shrink_ref, shrink_sems)
            x = stream_ref[...]
            normed = (normalize(x)[0] * rows_ref[2:3, :] + rows_ref[3:4, :]).astype(BF16)
            normed_ref[...] = mixed(normed, mix_ref[...])
            out_ref[...] = x
            wait_expand()
            wait_shrink()

        here = pl.ds(pl.multiple_of(j * step, 128), step)
        inner = dot(normed_ref[...], expand_ref[:, here])
        inner_ref[...] = inner
        out_ref[...] += dot(gelu(inner).astype(BF16), shrink_ref[here, :])

    fixed = lambda a: pl.BlockSpec(a.shape, lambda j: (0, 0))
    outs = [
        shaped((tokens, features), F32),
        shaped((tokens, features), BF16),
        shaped((tokens, inner_width), F32),
    ]
    return call(
        kernel,
        outs,
        [places, *expand, *shrink, mix, stream, rows],
        4 * tokens * features * inner_width,
        (depth,),
        [SCALAR] + [ANYWHERE] * (count + len(shrink)) + [fixed(mix), fixed(stream), fixed(rows)],
        [fixed(outs[0]), fixed(outs[1]), pl.BlockSpec((tokens, step), lambda j: (0, j))],
        [
            pltpu.VMEM((features, inner_width), BF16),
            pltpu.VMEM((inner_width, features), BF16),
            pltpu.SemaphoreType.DMA((count,)),
            pltpu.SemaphoreType.DMA((blocks,)),
        ],
        LIGHT,
    )


def feed_backward_shrink(shrink, places, depth, inner, upstream):
    tokens, features = upstream.shape
    inner_width = inner.shape[1]
    step = inner_width // depth
    count, blocks = len(shrink), places.shape[0]
    pieces = max(1, blocks // depth)
    piece = step // pieces
    side, half = max(1, pieces // 2), min(piece, step // 2)

    def kernel(places_ref, *refs):
        shrink_refs = refs[:count]
        inner_ref, up_ref, inner_grad_ref, near_ref, over_ref, active_ref, shrink_ref, sems = refs[count:]
        j = pl.program_id(0)

        @pl.when(j == 0)
        def _():
            start_blocks(shrink_refs, places_ref, shrink_ref, sems)()

        branch = up_ref[...].astype(BF16)
        active, slope = gelu_both(inner_ref[...])
        active_ref[...] = active.astype(BF16).T
        for p in range(pieces):
            start = 0
            if pieces > 1:
                start = pl.multiple_of(places_ref[p * depth + chunk_at(j, places_ref)] - j * step, 16)
            grad = dot(active_ref[pl.ds(start, piece), :], branch).astype(BF16)
            if pieces == 1:
                near_ref[0, 0] = grad[: step // 2]
                over_ref[0, 0] = grad[step // 2 :]
            elif p < pieces // 2:
                near_ref[p, 0] = grad
            else:
                over_ref[p - pieces // 2, 0] = grad
        here = pl.ds(pl.multiple_of(j * step, 128), step)
        inner_grad_ref[...] = (dot_nt(branch, shrink_ref[here, :]) * slope).astype(BF16)

    def chunk_at(j, places_ref):
        return lax.rem(places_ref[0] // step - j + depth, depth)

    def layer(j, places_ref):
        return (0, j if pieces == 1 else chunk_at(j, places_ref), 0, 0)

    columns = pl.BlockSpec((tokens, step), lambda j, places_ref: (0, j))
    outs = [
        shaped((tokens, inner_width), BF16),
        shaped((side, depth, half, features), BF16),
        shaped((side, depth, half, features), BF16),
    ]
    ins = [places, *shrink, inner, upstream]
    moved = sum(a.size * a.dtype.itemsize for a in (*ins, *outs))
    inner_grad, near, over = pl.pallas_call(
        kernel,
        out_shape=outs,
        grid_spec=pltpu.PrefetchScalarGridSpec(
            num_scalar_prefetch=1,
            grid=(depth,),
            in_specs=[ANYWHERE] * count
            + [columns, pl.BlockSpec(upstream.shape, lambda j, places_ref: (0, 0))],
            out_specs=[columns] + [pl.BlockSpec((side, 1, half, features), layer)] * 2,
            scratch_shapes=[
                pltpu.VMEM((step, tokens), BF16),
                pltpu.VMEM((inner_width, features), BF16),
                pltpu.SemaphoreType.DMA((blocks,)),
            ],
        ),
        compiler_params=pltpu.CompilerParams(vmem_limit_bytes=LIMIT),
        cost_estimate=cost(4 * tokens * features * inner_width, moved, LIGHT),
    )(*ins)
    if pieces == 1:
        shrink_grad = [jnp.concatenate([near, over], axis=2).reshape(inner_width, features)]
    else:
        shrink_grad = [near.reshape(-1, features), over.reshape(-1, features)]
    return inner_grad, shrink_grad


def feed_backward_expand(stream, rows, expand, mix, depth, normed, inner_grad, upstream):
    tokens, features = stream.shape
    inner_width = inner_grad.shape[1]
    step = inner_width // depth
    count = len(expand)

    def kernel(*refs):
        expand_refs = refs[:count]
        mix_ref, stream_ref, rows_ref, normed_ref, inner_grad_ref, up_ref = refs[count : count + 6]
        out_ref, mine_ref, other_ref, gains_ref, total_ref, turned_ref, expand_ref, sems = refs[count + 6 :]
        j = pl.program_id(0)

        @pl.when(j == 0)
        def _():
            wait = start_parts(expand_refs, expand_ref, sems)
            turned_ref[...] = normed_ref[...].T
            total_ref[...] = jnp.zeros_like(total_ref)
            wait()

        inner_grad = inner_grad_ref[...]
        expand_grad = dot(turned_ref[...], inner_grad).astype(BF16)
        mine_ref[...] = expand_grad[: features // 2]
        other_ref[...] = expand_grad[features // 2 :]
        here = pl.ds(pl.multiple_of(j * step, 128), step)
        total_ref[...] += dot_nt(inner_grad, expand_ref[:, here])

        @pl.when(j == depth - 1)
        def _():
            grad = unmixed(total_ref[...], mix_ref[...])
            out_ref[...] = norm_back(stream_ref[...], rows_ref[2:3, :], grad, gains_ref, up_ref[...])

    fixed = lambda a: pl.BlockSpec(a.shape, lambda j: (0, 0))
    columns = lambda height: pl.BlockSpec((height, step), lambda j: (0, j))
    outs = [
        shaped((tokens, features), F32),
        shaped((features // 2, inner_width), BF16),
        shaped((features // 2, inner_width), BF16),
        shaped((8, features), F32),
    ]
    out, mine, other, gains = call(
        kernel,
        outs,
        [*expand, mix, stream, rows, normed, inner_grad, upstream],
        4 * tokens * features * inner_width,
        (depth,),
        [ANYWHERE] * count
        + [fixed(mix), fixed(stream), fixed(rows), fixed(normed), columns(tokens), fixed(upstream)],
        [fixed(outs[0]), columns(features // 2), columns(features // 2), fixed(outs[3])],
        [
            pltpu.VMEM((tokens, features), F32),
            pltpu.VMEM((features, tokens), BF16),
            pltpu.VMEM((features, inner_width), BF16),
            pltpu.SemaphoreType.DMA((count,)),
        ],
        LIGHT,
    )
    return out, (mine, other), gains


def gate_of(logits, meta):
    lane = lax.broadcasted_iota(jnp.int32, logits.shape, 1)
    chosen = lane == meta[:, 0:1] + LANE
    return jax.nn.sigmoid(jnp.sum(jnp.where(chosen, logits, 0.0), axis=-1, keepdims=True)), chosen


def put_blocks(refs, columns, values):
    rows = values.shape[0] // len(refs)
    for k, ref in enumerate(refs):
        ref[:, columns] = values[k * rows : (k + 1) * rows]


def mixer_before(stream, rows, facts, teacher, meta, target, slots, experts):
    tokens, features = stream.shape

    def kernel(stream_ref, rows_ref, facts_ref, teacher_ref, meta_ref, target_ref, *refs):
        normed_ref, logits_ref = refs[:2]
        ahead_refs, back_refs = refs[2 : 2 + experts], refs[2 + experts :]
        x = stream_ref[...]
        normed = (normalize(x)[0] * rows_ref[6:7, :] + rows_ref[7:8, :]).astype(BF16)
        normed_ref[...] = normed
        dispatch = lax.broadcasted_iota(jnp.int32, (slots, tokens), 0) == target_ref[...]
        dispatch = dispatch.astype(F32).astype(BF16)
        put_blocks(ahead_refs, slice(None), dot(dispatch, normed).astype(BF16))
        logits = dot_nt(normed, rows_ref[...].astype(BF16))
        logits_ref[...] = logits
        meta = meta_ref[...]
        gate = gate_of(logits, meta)[0]
        factor = facts_ref[1:2, 0:1] * meta[:, 2:3].astype(F32) * gate
        offset = (factor * (x - teacher_ref[...].astype(F32))).astype(BF16)
        slope = factor * gate
        high = slope.astype(BF16)
        low = (slope - high.astype(F32)).astype(BF16)
        lane = lax.broadcasted_iota(jnp.int32, (tokens, 128), 1)
        slope = jnp.where(lane == 0, high.astype(F32), jnp.where(lane == 1, low.astype(F32), 0.0)).astype(BF16)
        put_blocks(back_refs, slice(0, features), dot(dispatch, offset).astype(BF16))
        put_blocks(back_refs, slice(features, None), dot(dispatch, slope).astype(BF16))

    outs = [
        shaped((tokens, features), BF16),
        shaped((tokens, rows.shape[0]), F32),
    ]
    outs += [shaped((slots // experts, features), BF16)] * experts
    outs += [shaped((slots // experts, features + 128), BF16)] * experts
    ins = [stream, rows, facts, teacher, meta, target]
    normed, logits, *blocks = call(kernel, outs, ins, 4 * slots * tokens * features)
    return normed, logits, blocks[:experts], blocks[experts:]


def expert_specs(weights, step):
    owners, height, features = weights.shape
    shrink_rows = height // 2
    expand_rows = features // owners
    each = step // shrink_rows
    first = shrink_rows // expand_rows
    expand = pl.BlockSpec(
        (owners, expand_rows, step), lambda j: (0, first + j * step // features, j * step % features // step)
    )
    return expand, pl.BlockSpec((each, shrink_rows, features), lambda j: (j, 0, 0))


def expert_forward(blocks, weights, depth):
    experts = len(blocks)
    rows, features = blocks[0].shape
    slots = experts * rows
    owners, height, _ = weights.shape
    inner_width = owners * height // 2
    step = inner_width // depth

    def kernel(*refs):
        block_refs, (expand_ref, shrink_ref) = refs[:experts], refs[experts : experts + 2]
        out_refs = refs[experts + 2 : 2 * experts + 2]
        arrived_ref, inner_ref, total_ref = refs[2 * experts + 2 :]
        j = pl.program_id(0)

        @pl.when(j == 0)
        def _():
            for k in range(experts):
                arrived_ref[k * rows : (k + 1) * rows, :] = block_refs[k][...]

        inner = dot(arrived_ref[...], expand_ref[...].reshape(features, step))
        inner_ref[...] = inner
        part = dot(gelu(inner).astype(BF16), shrink_ref[...].reshape(step, features))

        @pl.when(j == 0)
        def _():
            total_ref[...] = part

        @pl.when(j > 0)
        def _():
            total_ref[...] += part

        @pl.when(j == depth - 1)
        def _():
            put_blocks(out_refs, slice(None), total_ref[...].astype(BF16))

    fixed = lambda a: pl.BlockSpec(a.shape, lambda j: (0, 0))
    outs = [shaped((rows, features), BF16)] * experts
    outs += [shaped((slots, features), BF16), shaped((slots, inner_width), F32)]
    *result, arrived, inner = call(
        kernel,
        outs,
        [*blocks, weights, weights],
        4 * slots * features * inner_width,
        (depth,),
        [fixed(b) for b in blocks] + [*expert_specs(weights, step)],
        [fixed(o) for o in outs[:-1]] + [pl.BlockSpec((slots, step), lambda j: (0, j))],
        [pltpu.VMEM((slots, features), F32)],
    )
    return result, arrived, inner


def expert_backward(back, result, inner, weights, depth):
    experts = len(back)
    rows, features = result[0].shape
    slots = experts * rows
    owners, height, _ = weights.shape
    inner_width = owners * height // 2
    step = inner_width // depth

    def kernel(*refs):
        back_refs, result_refs = refs[:experts], refs[experts : 2 * experts]
        inner_ref, expand_ref, shrink_ref = refs[2 * experts : 2 * experts + 3]
        out_refs = refs[2 * experts + 3 : 3 * experts + 3]
        inner_grad_ref, grads_ref, landed_ref, total_ref = refs[3 * experts + 3 :]
        j = pl.program_id(0)

        @pl.when(j == 0)
        def _():
            for k in range(experts):
                terms = back_refs[k][:, features:].astype(F32)
                slope = terms[:, 0:1] + terms[:, 1:2]
                landed = back_refs[k][:, :features].astype(F32) + slope * result_refs[k][...].astype(F32)
                landed_ref[k * rows : (k + 1) * rows, :] = landed.astype(BF16)
            total_ref[...] = jnp.zeros_like(total_ref)

        active, slope = gelu_both(inner_ref[...])
        landed = landed_ref[...]
        inner_grad = (dot_nt(landed, shrink_ref[...].reshape(step, features)) * slope).astype(BF16)
        inner_grad_ref[...] = inner_grad
        grads_ref[...] = dot_tn(active.astype(BF16), landed).astype(BF16)
        total_ref[...] += dot_nt(inner_grad, expand_ref[...].reshape(features, step))

        @pl.when(j == depth - 1)
        def _():
            put_blocks(out_refs, slice(None), total_ref[...].astype(BF16))

    fixed = lambda a: pl.BlockSpec(a.shape, lambda j: (0, 0))
    columns = lambda height: pl.BlockSpec((height, step), lambda j: (0, j))
    outs = [shaped((rows, features), BF16)] * experts
    outs += [shaped((slots, inner_width), BF16), shaped((inner_width, features), BF16)]
    *rows_grad, inner_grad, grads = call(
        kernel,
        outs,
        [*back, *result, inner, weights, weights],
        6 * slots * features * inner_width,
        (depth,),
        [fixed(b) for b in (*back, *result)]
        + [
            columns(slots),
            *expert_specs(weights, step),
        ],
        [fixed(o) for o in outs[:-2]]
        + [columns(slots), pl.BlockSpec((step, features), lambda j: (j, 0))],
        [pltpu.VMEM((slots, features), BF16), pltpu.VMEM((slots, features), F32)],
        LIGHT,
    )
    return rows_grad, inner_grad, grads


def expert_expand_grad(arrived, inner_grad):
    slots, features = arrived.shape
    inner_width = inner_grad.shape[1]

    def kernel(arrived_ref, inner_grad_ref, out_ref, turned_ref):
        @pl.when(pl.program_id(0) == 0)
        def _():
            turned_ref[...] = arrived_ref[...].T

        out_ref[...] = dot(turned_ref[...], inner_grad_ref[...]).astype(BF16)

    columns = lambda height: pl.BlockSpec((height, features), lambda j: (0, j))
    [grad] = call(
        kernel,
        [shaped((features, inner_width), BF16)],
        [arrived, inner_grad],
        2 * slots * features * inner_width,
        (inner_width // features,),
        [pl.BlockSpec(arrived.shape, lambda j: (0, 0)), columns(slots)],
        [columns(features)],
        [pltpu.VMEM((features, slots), BF16)],
        LIGHT,
    )
    return grad


def mixer_after(stream, rows, facts, teacher, meta, normed, logits, returned, rows_grad, experts):
    tokens, features = stream.shape
    block = returned[0].shape[0]
    slots = experts * block

    def kernel(*refs):
        stream_ref, rows_ref, facts_ref, teacher_ref, meta_ref, normed_ref, logits_ref = refs[:7]
        returned_refs, rows_grad_refs = refs[7 : 7 + experts], refs[7 + experts : 7 + 2 * experts]
        states_ref, grad_ref, small_ref, squared_ref = refs[7 + 2 * experts :]
        x = stream_ref[...]
        meta = meta_ref[...]
        combine = lax.broadcasted_iota(jnp.int32, (tokens, slots), 1) == meta[:, 1:2]
        combine = combine.astype(F32).astype(BF16)
        combined = dot(combine, jnp.concatenate([r[...] for r in returned_refs], axis=0))
        logits = logits_ref[...]
        gate, chosen = gate_of(logits, meta)
        final = x + gate * combined
        states_ref[...] = final.astype(BF16)
        valid = meta[:, 2:3].astype(F32)
        difference = final - teacher_ref[...].astype(F32)
        masked = valid * difference
        squared = 0.5 * jnp.sum(jnp.sum(masked * difference, axis=-1, keepdims=True), axis=0, keepdims=True)
        squared_ref[...] = jnp.broadcast_to(squared, squared_ref.shape)
        upstream = facts_ref[1:2, 0:1] * masked
        gate_grad = jnp.sum(upstream * combined, axis=-1, keepdims=True)
        lane = lax.broadcasted_iota(jnp.int32, logits.shape, 1)
        real = (lane >= LANE) & (lane < LANE + experts)
        shown = jnp.where(real, logits, -1e30)
        exponent = jnp.exp(shown - jnp.max(shown, axis=-1, keepdims=True))
        probs = exponent / jnp.sum(exponent, axis=-1, keepdims=True)
        share = facts_ref[0:1, :]
        tilt = jnp.sum(probs * share, axis=-1, keepdims=True)
        logits_grad = facts_ref[2:3, 0:1] * valid * probs * (share - tilt)
        logits_grad = jnp.where(real, logits_grad, 0.0)
        logits_grad += jnp.where(chosen, gate_grad * gate * (1.0 - gate), 0.0)
        first = logits_grad.astype(BF16)
        left = logits_grad - first.astype(F32)
        second = left.astype(BF16)
        third = (left - second.astype(F32)).astype(BF16)
        weights = rows_ref[...].astype(BF16)
        normed = normed_ref[...]
        normed_grad = dot(combine, jnp.concatenate([r[...] for r in rows_grad_refs], axis=0))
        normed_grad += dot(third, weights) + dot(second, weights) + dot(first, weights)
        small_ref[...] = dot_tn(third, normed) + dot_tn(second, normed) + dot_tn(first, normed)
        grad_ref[...] = norm_back(x, rows_ref[6:7, :], normed_grad, small_ref.at[6:8], upstream)

    outs = [
        shaped((tokens, features), BF16),
        shaped((tokens, features), F32),
        shaped(rows.shape, F32),
        shaped((8, 128), F32),
    ]
    ins = [stream, rows, facts, teacher, meta, normed, logits, *returned, *rows_grad]
    return call(kernel, outs, ins, 4 * slots * tokens * features)


def body(
    tokens,
    teacher,
    routes,
    piece_start,
    valid_mask,
    lower_gain,
    lower_bias,
    lower_triple,
    lower_output,
    feed_gain,
    feed_bias,
    feed_expand,
    feed_shrink,
    upper_gain,
    upper_bias,
    upper_triple,
    upper_output,
    mixer_gain,
    mixer_bias,
    router,
    expert_expand,
    expert_shrink,
):
    count, length, features = tokens.shape
    local = count * length
    experts = router.shape[1]
    share_rows = router.shape[0]
    devices = lax.axis_size("dp") * lax.axis_size("expert")
    capacity = max(2, 2 * length // experts)
    total_tokens = local * devices
    valid = valid_mask.astype(F32)
    route = routes[..., 0]
    chosen = (route[..., None] == jnp.arange(experts, dtype=jnp.int32)).astype(F32)

    vectors = [lower_gain, lower_bias, feed_gain, feed_bias, upper_gain, upper_bias, mixer_gain, mixer_bias]
    extra_width = 128

    wide = 3 * features
    depth = lax.axis_size("dp") // 2

    row_order = (order(share_rows)[:, None] + jnp.arange(share_rows, dtype=jnp.int32)).reshape(1, features)
    mix = (jnp.arange(features, dtype=jnp.int32)[:, None] == row_order).astype(BF16)
    shrink_rows = feed_shrink.shape[0]
    inner_width = feed_expand.shape[1]
    inner_width = feed_expand.shape[1]
    lower_own = pack_lower(lower_triple, lower_output, vectors, router.T, route, valid_mask)
    upper_own = jnp.concatenate([upper_triple, upper_output], axis=1)

    position = jnp.arange(length, dtype=jnp.int32)
    earlier = (position[:, None] > position[None, :]).astype(BF16)
    before = jnp.einsum("qk,mke->mqe", earlier, chosen.astype(BF16), preferred_element_type=F32)
    slot = jnp.sum(before * chosen, axis=-1).astype(jnp.int32)
    target = (route ^ lax.axis_index("expert")) * (count * capacity) + jnp.arange(count, dtype=jnp.int32)[:, None] * capacity + slot
    slots = experts * count * capacity
    meta = jnp.stack([route.reshape(-1), target.reshape(-1), valid_mask.reshape(-1)], axis=1)
    target = target.reshape(1, local)

    stream_in = tokens.reshape(local, features)
    labels = teacher.reshape(local, features)
    places = order(shrink_rows)
    pieces = expert_expand[0].reshape(-1, inner_width // features, features)
    experts_own = jnp.concatenate([expert_shrink[0], jnp.moveaxis(pieces, 1, 0).reshape(-1, features)])

    shrink_line, shrink_over = gather_lines(feed_shrink)
    wide_line, wide_over = gather_lines(jnp.concatenate([feed_expand, upper_own], axis=1))
    lower = pull_line(lower_own)

    lower, experts_own, mix, meta, target, places = at_once((lower, experts_own, mix, meta, target, places))
    experts_full = lax.all_gather(experts_own, "dp")
    lower = jnp.stack([lower_own, *lower])
    near = pull_near(lower)

    lower, near, shrink_line, shrink_over = at_once((lower, near, shrink_line, shrink_over))
    lower = pull_far(lower, near)
    shrink_near = pull_near(shrink_line)

    lower, shrink_line, shrink_near = at_once((lower, shrink_line, shrink_near))
    lower_over = pull_over(lower[1])

    lower, lower_over, wide_line, wide_over = at_once((lower, lower_over, wide_line, wide_over))
    lower = in_order(*lower, lower_over)
    shrink_full = pull_far(shrink_line, shrink_near, shrink_over)
    expand_line, expand_over = wide_line[..., :inner_width], wide_over[..., :inner_width]
    upper_line, upper_over = wide_line[..., inner_width:], wide_over[..., inner_width:]
    expand_near = pull_near(expand_line)
    rows, stream_one, *stored_one = attend_forward(0, stream_in, None, lower, 0, mix, piece_start, length)

    shrink_full, expand_line, expand_near, rows, stream_one = at_once(
        (shrink_full, expand_line, expand_near, rows, stream_one)
    )
    shrink_full = in_order(*shrink_full, pull_over(shrink_full[1]))
    expand_full = pull_far(expand_line, expand_near, expand_over)
    upper_near = pull_near(upper_line)
    lane = jnp.arange(features, dtype=jnp.int32)
    sums = rows[LANE + experts : LANE + 2 * experts + 1]
    sums = jnp.sum(jnp.where(lane % share_rows < count, sums, 0.0), axis=1)
    valid_total = sums[experts]
    loss_ratio = total_tokens / valid_total
    balance_scale = total_tokens * features * 0.1 * experts / valid_total
    share = jnp.pad(sums[:experts] / valid_total, (LANE, extra_width - LANE - experts))
    facts = jnp.stack([share, jnp.full_like(share, loss_ratio), jnp.full_like(share, balance_scale)])
    facts = jnp.pad(facts, ((0, 5), (0, 0)))

    shrink_full, expand_full, upper_line, upper_near, stream_one, facts = at_once(
        (shrink_full, expand_full, upper_line, upper_near, stream_one, facts)
    )
    expand_full = in_order(*expand_full, pull_over(expand_full[1]))

    expand_full, upper_line, upper_near, stream_one = at_once((expand_full, upper_line, upper_near, stream_one))
    upper = pull_far(upper_line, upper_near, upper_over)

    if shrink_rows % 16:
        whole = jnp.concatenate(shrink_full, axis=0).reshape(devices, shrink_rows, features)
        shrink_full = [jnp.zeros_like(whole).at[places // shrink_rows].set(whole).reshape(-1, features)]
        places = jnp.zeros((1,), jnp.int32)
    stream_two, *stored_two = feed_forward(stream_one, rows, expand_full, shrink_full, places, mix, depth)

    upper, stream_two = at_once((upper, stream_two))
    upper = in_order(*upper, pull_over(upper[1]))
    stream_three, *stored_three = attend_forward(4, stream_two, rows, upper, 0, mix, piece_start, length)
    normed, logits, ahead, back = mixer_before(
        stream_three, rows, facts, labels, meta, target, slots, experts
    )
    ahead = exchange(ahead)
    back = exchange([after(b, *ahead) for b in back])
    result, arrived, inner = expert_forward(ahead, experts_full, depth)
    returned = exchange(result)
    rows_grad, inner_grad, expert_out_grad = expert_backward(back, result, inner, experts_full, depth)
    returned, rows_grad, inner_grad, expert_out_grad = at_once((returned, rows_grad, inner_grad, expert_out_grad))
    expert_out_grad = lax.psum_scatter(expert_out_grad, "dp", scatter_dimension=0, tiled=True)
    rows_grad = exchange(rows_grad)
    states, grad_three, mixer_small, squared = mixer_after(
        stream_three, rows, facts, labels, meta, normed, logits, returned, rows_grad, experts
    )
    grad_two, *upper_grad, upper_small = attend_backward(
        4, stream_two, rows, upper, 0, mix, piece_start, length, stored_three, grad_three
    )
    hops = total_hops()

    def hop_loss(value, first, last):
        for target in hops[first:last] if hops else ():
            value = value + hop(value, target)
        return value

    inner_grad = after(inner_grad, grad_two)
    upper_mine, upper_other = upper_grad
    upper_other = swap_cores(upper_other)
    expert_in_grad = expert_expand_grad(arrived, inner_grad)

    upper_mine, upper_other, expert_in_grad, grad_two = at_once((upper_mine, upper_other, expert_in_grad, grad_two))
    expert_in_grad = lax.psum_scatter(expert_in_grad, "dp", scatter_dimension=0, tiled=True)
    upper_part = sum_cores(upper_mine, upper_other)

    grad_two, *upper_part = at_once((grad_two, *upper_part))
    upper_part = scatter_far(upper_part)
    squared = hop_loss(squared, 0, 1)
    feed_normed, inner_pre = stored_two
    inner_grad, shrink_grad = feed_backward_shrink(shrink_full, places, depth, inner_pre, grad_two)
    if shrink_rows % 16:
        blocks = order(shrink_rows) // shrink_rows
        pick = (blocks[:, None] == jnp.arange(devices, dtype=jnp.int32)).astype(BF16)
        shrink_grad = dot(pick, shrink_grad[0].reshape(devices, -1)).astype(BF16).reshape(2, -1, features)
        shrink_grad = [shrink_grad[0], shrink_grad[1]]

    upper_part, squared, inner_grad, shrink_grad = at_once((upper_part, squared, inner_grad, shrink_grad))
    upper_part = scatter_near(upper_part)
    squared = hop_loss(squared, 1, 2)
    shrink_mine, shrink_other = shrink_grad
    shrink_other = swap_cores(shrink_other)
    grad_one, expand_grad, feed_small = feed_backward_expand(
        stream_one, rows, expand_full, mix, depth, feed_normed, inner_grad, grad_two
    )

    upper_part, squared, shrink_mine, shrink_other, expand_grad, grad_one = at_once(
        (upper_part, squared, shrink_mine, shrink_other, expand_grad, grad_one)
    )
    shrink_part = scatter_far(sum_cores(shrink_mine, shrink_other))
    expand_part = scatter_cores(*expand_grad)
    squared = hop_loss(squared, 2, 3)

    upper_part, expand_part, shrink_part, grad_one, squared = at_once(
        (upper_part, expand_part, shrink_part, grad_one, squared)
    )
    expand_part = scatter_far(expand_part)
    shrink_part = scatter_near(shrink_part)
    upper_part = scatter_line(upper_part)
    grad_in, *lower_grad, _ = attend_backward(
        0, stream_in, rows, lower, 0, mix, piece_start, length, stored_one, grad_one, (mixer_small, upper_small, feed_small)
    )

    upper_part, expand_part, shrink_part, grad_in, lower_grad, squared = at_once(
        (upper_part, expand_part, shrink_part, grad_in, lower_grad, squared)
    )
    lower_part = scatter_cores(*lower_grad)
    expand_part = scatter_near(expand_part)
    shrink_part = scatter_line(shrink_part)

    lower_part, expand_part, shrink_part, upper_part, squared, expert_out_grad, expert_in_grad = at_once(
        (lower_part, expand_part, shrink_part, upper_part, squared, expert_out_grad, expert_in_grad)
    )
    lower_part = scatter_far(lower_part)
    expand_part = scatter_line(expand_part)
    squared = hop_loss(squared, 3, 4)
    upper_part, shrink_part = total(upper_part), total(shrink_part)
    expert_out_grad, expert_in_grad = expert_out_grad.astype(F32), expert_in_grad.astype(F32)

    lower_part, expand_part, shrink_part, upper_part, squared, expert_in_grad, expert_out_grad = at_once(
        (lower_part, expand_part, shrink_part, upper_part, squared, expert_in_grad, expert_out_grad)
    )
    lower_part = scatter_near(lower_part)
    squared = hop_loss(squared, 4, None)

    lower_part, expand_part, squared = at_once((lower_part, expand_part, squared))
    lower_part, expand_part = total(scatter_line(lower_part)), total(expand_part)
    if hops is None:
        squared = lax.psum(squared, AXES)
    small = lower_part[:, wide + features :]
    squared_total = squared[0, 0]
    mean_loss = loss_ratio * squared_total / (total_tokens * features)
    return (
        states.reshape(tokens.shape),
        grad_in.reshape(tokens.shape),
        small[:, 0],
        small[:, 1],
        lower_part[:, :wide],
        lower_part[:, wide : wide + features],
        small[:, 2],
        small[:, 3],
        expand_part,
        shrink_part,
        small[:, 4],
        small[:, 5],
        upper_part[:, :wide],
        upper_part[:, wide:],
        small[:, 6],
        small[:, 7],
        small[:, 8 : 8 + experts],
        expert_in_grad[None],
        expert_out_grad[None],
        mean_loss,
    )


def solution(mesh):
    both = ("dp", "expert")
    token = P(both, None, None)
    vector = P(both)
    matrix = P(both, None)
    expert = P("expert", "dp", None)
    dense = (vector, vector, matrix, matrix, vector, vector, matrix, matrix)
    weights = dense + (vector, vector, matrix, matrix, vector, vector, matrix, expert, expert)
    return jax.shard_map(
        body,
        mesh=mesh,
        in_specs=(token, token, token, vector, matrix) + weights,
        out_specs=(token, token) + weights + (P(),),
        check_vma=False,
    )
```

```python
import math

import jax
import jax.numpy as jnp
from jax import lax
from jax.experimental import pallas as pl
from jax.experimental.pallas import tpu as pltpu
from jax.sharding import PartitionSpec as P

HD = 64
AXES = ("dp", "expert")
F32 = jnp.float32
BF16 = jnp.bfloat16


def place():
    depth = lax.axis_size("dp") // 2
    row = lax.axis_index("dp")
    return depth, lax.axis_size("expert"), row // 2, row % 2, lax.axis_index("expert")


def pairs(target):
    depth, across = lax.axis_size("dp") // 2, lax.axis_size("expert")
    out = []
    for z in range(depth):
        for c in range(2):
            for e in range(across):
                to = target(z, c, e)
                if to is not None and 0 <= to[0] < depth:
                    out.append(((z * 2 + c) * across + e, (to[0] * 2 + to[1]) * across + to[2]))
    return out


def hop(values, target):
    return lax.ppermute(values, AXES, pairs(target))


def swap_cores(values):
    return hop(values, lambda z, c, e: (z, 1 - c, e))


def first_side(values):
    return hop(values, lambda z, c, e: (z, c, e ^ (1 + c)))


def second_side(values):
    return hop(values, lambda z, c, e: (z, c, e ^ (2 - c)))


at_once = lax.optimization_barrier


def after(value, *others):
    return lax.optimization_barrier((value, *others))[0]


def shift(values, by):
    depth = place()[0]
    return hop(values, lambda z, c, e: ((z + by) % depth, c, e))


def pull_line(own):
    return [shift(own, k) for k in range(1, place()[0])]


def gather_lines(own):
    depth, _, z, c, _ = place()
    both = lax.all_gather(own, "dp", axis=0, tiled=True).reshape(depth, 2, *own.shape)
    zero = jnp.zeros_like(z)
    at = lambda k, core: lax.dynamic_slice(both, ((z - k) % depth, core, zero, zero), (1, 1, *own.shape))[0]
    return [jnp.concatenate([at(k, core) for k in range(depth)]) for core in (c, 1 - c)]


def pull_near(line):
    return first_side(line) if place()[1] == 4 else line


def pull_far(line, near, over=None):
    if place()[1] != 4:
        whole = lax.all_gather(line, "expert", axis=1)
        return [whole], None, [swap_cores(whole)]
    pair = jnp.stack([line, near])
    side = [swap_cores(pair)] if over is None else [over, swap_cores(near)]
    return [pair], second_side(pair), side


def pull_over(far):
    return None if far is None else swap_cores(far)


def in_order(pair, far, pair_over, far_over):
    return [p.reshape(-1, p.shape[-1]) for p in (*pair, far, *pair_over, far_over) if p is not None]


def order(rows):
    depth, across, z, c, e = place()
    k = jnp.arange(depth, dtype=jnp.int32)
    layer = (z - k) % depth
    if across == 4:
        there = jnp.stack([e, e ^ (1 + c), e ^ (2 - c), e ^ 3])
        over = jnp.stack([e, e ^ (2 - c), e ^ (1 + c), e ^ 3])
    else:
        there = over = jnp.arange(across, dtype=jnp.int32)
    first = (layer * 2 + c)[None, :] * across + there[:, None]
    second = (layer * 2 + 1 - c)[None, :] * across + over[:, None]
    if across != 4:
        first, second = first.T, second.T
    return jnp.concatenate([first.reshape(-1), second.reshape(-1)]) * rows


def add(first, second):
    return (first.astype(F32) + second.astype(F32)).astype(BF16)


def scatter_line(line):
    return [line[0]] + [shift(line[k], -k) for k in range(1, place()[0])]


def total(parts):
    return sum(p.astype(F32) for p in parts[1:]) + parts[0].astype(F32)


def scatter_cores(mine, other):
    return sum_cores(mine, swap_cores(other))


def sum_cores(mine, other):
    depth, across, _, _, _ = place()
    if across != 4:
        return [add(mine, other).reshape(depth, across, -1, mine.shape[1])]
    half = mine.shape[0] // 2
    return [add(mine[:half], other[:half]), add(mine[half:], other[half:])]


def scatter_far(parts):
    return [parts[0], second_side(parts[1])] if len(parts) == 2 else parts


def scatter_near(parts):
    depth = place()[0]
    if len(parts) == 1:
        return lax.psum_scatter(parts[0], "expert", scatter_dimension=1, tiled=True)[:, 0]
    half = parts[0].shape[0] // 2
    mine, come = parts
    line = add(add(mine[:half], come[:half]), first_side(add(mine[half:], come[half:])))
    return line.reshape(depth, -1, line.shape[1])


def total_hops():
    depth, across, _, _, _ = place()
    if across & (across - 1) or depth & (depth - 1):
        return None
    hops = [lambda z, c, e: (z, 1 - c, e)]
    step = 1
    while step < across:
        hops.append(lambda z, c, e, step=step: (z, c, e ^ step))
        step *= 2
    step = 1
    while step < depth:
        hops.append(lambda z, c, e, step=step: (z ^ step, c, e))
        step *= 2
    return hops


def exchange(blocks):
    return [blocks[0]] + [
        hop(blocks[k], lambda z, c, e: (z, c, e ^ k)) for k in range(1, len(blocks))
    ]


LIMIT = 60 * 1024 * 1024
LANE = 8
LIGHT = 1000


def cost(flops, moved, light=1):
    return pl.CostEstimate(flops=flops // light, bytes_accessed=moved // light, transcendentals=0)


WHOLE = pl.BlockSpec(memory_space=pltpu.VMEM)
SCALAR = pl.BlockSpec(memory_space=pltpu.SMEM)


def dot(a, b):
    return jnp.dot(a, b, preferred_element_type=F32)


def dot_nt(a, b):
    return lax.dot_general(a, b, (((1,), (1,)), ((), ())), preferred_element_type=F32)


def dot_tn(a, b):
    return lax.dot_general(a, b, (((0,), (0,)), ((), ())), preferred_element_type=F32)


def call(kernel, outs, ins, flops, grid=(), in_specs=None, out_specs=None, scratch=(), light=1):
    moved = sum(a.size * a.dtype.itemsize for a in (*ins, *outs))
    return pl.pallas_call(
        kernel,
        out_shape=outs,
        grid=grid,
        in_specs=in_specs or [WHOLE] * len(ins),
        out_specs=out_specs or [WHOLE] * len(outs),
        scratch_shapes=scratch,
        compiler_params=pltpu.CompilerParams(vmem_limit_bytes=LIMIT),
        cost_estimate=cost(flops, moved, light),
    )(*ins)


ANYWHERE = pl.BlockSpec(memory_space=pl.ANY)


def start_parts(parts, whole, sems, first=0):
    copies, at = [], 0
    for k, part in enumerate(parts):
        rows = part.shape[0]
        copies.append(pltpu.make_async_copy(part.at[:, first : first + whole.shape[1]], whole.at[at : at + rows], sems.at[k]))
        at += rows
    for copy in copies:
        copy.start()

    def wait():
        for copy in copies:
            copy.wait()

    return wait


def start_blocks(parts, places, whole, sems):
    rows = whole.shape[0] // places.shape[0]
    copies = []
    for part in parts:
        for b in range(part.shape[0] // rows):
            k = len(copies)
            at = pl.multiple_of(places[k], 16)
            copies.append(
                pltpu.make_async_copy(part.at[b * rows : (b + 1) * rows], whole.at[pl.ds(at, rows)], sems.at[k])
            )
    for copy in copies:
        copy.start()

    def wait():
        for copy in copies:
            copy.wait()

    return wait


def mixed(values, mix):
    return dot(values, mix).astype(BF16)


def unmixed(values, mix):
    high = values.astype(BF16)
    low = (values - high.astype(F32)).astype(BF16)
    return dot_nt(low, mix) + dot_nt(high, mix)


def shaped(shape, dtype):
    return jax.ShapeDtypeStruct(shape, dtype)


def normalize(x):
    centered = x - jnp.mean(x, axis=-1, keepdims=True)
    scale = lax.rsqrt(jnp.mean(centered * centered, axis=-1, keepdims=True) + 1e-05)
    return centered * scale, scale


def norm_back(x, gain, grad, gains_ref, upstream):
    unit, scale = normalize(x)
    gains_ref[0:1, :] = jnp.sum(grad * unit, axis=0, keepdims=True)
    gains_ref[1:2, :] = jnp.sum(grad, axis=0, keepdims=True)
    inner = grad * gain
    middle = jnp.mean(inner, axis=-1, keepdims=True)
    tilt = jnp.mean(inner * unit, axis=-1, keepdims=True)
    return upstream + scale * (inner - middle - unit * tilt)


ROOT = math.sqrt(2.0 / math.pi)


def gelu(x):
    return x * (0.5 + 0.5 * jnp.tanh(x * (ROOT + 0.044715 * ROOT * (x * x))))


def gelu_both(x):
    square = x * x
    bend = jnp.tanh(x * (ROOT + 0.044715 * ROOT * square))
    half = 0.5 + 0.5 * bend
    value = x * half
    return value, half + value * ((1.0 - bend) * (ROOT + 0.134145 * ROOT * square))


def allowed_pair(start, length):
    row = lax.broadcasted_iota(jnp.int32, (2 * length, length), 0)
    row = jnp.where(row >= length, row - length, row)
    column = lax.broadcasted_iota(jnp.int32, (2 * length, length), 1)
    piece = length // 4
    inside = (row >= start) & (row < start + piece) & (column >= start) & (column < start + piece)
    return (column <= row) | inside


def apart(pair):
    low = lax.broadcasted_iota(jnp.int32, pair.shape, 1) < HD
    zero = jnp.zeros_like(pair)
    return jnp.concatenate([jnp.where(low, pair, zero), jnp.where(low, zero, pair)], axis=0)


def together(stacked):
    half = stacked.shape[0] // 2
    low = lax.broadcasted_iota(jnp.int32, (half, stacked.shape[1]), 1) < HD
    return jnp.where(low, stacked[:half], stacked[half:])


def softmax_pair(queries, keys, allowed):
    scores = jnp.where(allowed, dot_nt(queries, keys) * HD ** (-0.5), -1e30)
    exponent = jnp.exp(scores - jnp.max(scores, axis=-1, keepdims=True))
    return exponent * (1.0 / jnp.sum(exponent, axis=-1, keepdims=True))


def pack_lower(triple, output, vectors, router, route, valid):
    share = triple.shape[0]
    experts = router.shape[0]
    wide, features = triple.shape[1], output.shape[1]

    def kernel(triple_ref, output_ref, *refs):
        vector_refs = refs[:LANE]
        router_ref, route_ref, valid_ref, out_ref, turned_ref = refs[LANE:]
        turned_ref[...] = jnp.zeros_like(turned_ref)
        for k in range(LANE):
            turned_ref[k : k + 1, :share] = vector_refs[k][...].astype(F32)
        turned_ref[LANE : LANE + experts, :share] = router_ref[...].astype(F32)
        valid = valid_ref[...].astype(F32)
        route = route_ref[...]
        lane = lax.broadcasted_iota(jnp.int32, (valid.shape[0], 128), 1) - LANE - experts
        counts = jnp.where(lane == experts, jnp.sum(valid, axis=-1, keepdims=True), 0.0)
        for e in range(experts):
            count = jnp.sum(jnp.where(route == e, valid, 0.0), axis=-1, keepdims=True)
            counts += jnp.where(lane == e, count, 0.0)
        counts = jnp.concatenate([counts, jnp.zeros((share - counts.shape[0], 128), F32)], axis=0)
        out_ref[:, :wide] = triple_ref[...]
        out_ref[:, wide : wide + features] = output_ref[...]
        out_ref[:, wide + features :] = (turned_ref[...].T[:share] + counts).astype(BF16)

    [packed] = call(
        kernel,
        [shaped((share, wide + features + 128), BF16)],
        [triple, output, *(v.reshape(1, share) for v in vectors), router, route, valid],
        1,
        scratch=[pltpu.VMEM((128, 128), F32)],
    )
    return packed


def attend_forward(at, stream, rows, parts, first, mix, start, length):
    tokens, features = stream.shape
    wide = 3 * features
    width = parts[0].shape[1] - first
    count = len(parts)

    def kernel(*refs):
        start_ref, stream_ref, mix_ref = refs[:3]
        part_refs = refs[3 : 3 + count]
        out_ref, normed_ref, packed_ref, context_ref = refs[-6:-2]
        rows_ref, weights_ref, sems = refs[-7 if rows is None else 3 + count], refs[-2], refs[-1]
        wait = start_parts(part_refs, weights_ref, sems, first)
        x = stream_ref[...].astype(F32)
        unit = normalize(x)[0]
        mix = mix_ref[...]
        wait()
        if rows is None:
            rows_ref[...] = lax.dot_general(
                weights_ref[:, wide + features :], mix, (((0,), (1,)), ((), ())), preferred_element_type=F32
            )
        normed = (unit * rows_ref[at : at + 1, :] + rows_ref[at + 1 : at + 2, :]).astype(BF16)
        normed = mixed(normed, mix)
        normed_ref[...] = normed
        for j in range(3):
            columns = slice(j * features, (j + 1) * features)
            packed_ref[:, columns] = dot(normed, weights_ref[:, columns]).astype(BF16)
        for s in range(tokens // length):
            allowed = allowed_pair(start_ref[s], length)
            here = slice(s * length, (s + 1) * length)
            for p in range(features // (2 * HD)):
                at_q, at_k, at_v = (slice(j * features + p * 2 * HD, j * features + (p + 1) * 2 * HD) for j in range(3))
                probs = softmax_pair(apart(packed_ref[here, at_q]), packed_ref[here, at_k], allowed)
                context_ref[here, at_q] = together(dot(probs.astype(BF16), packed_ref[here, at_v])).astype(BF16)
        context = mixed(context_ref[...], mix)
        context_ref[...] = context
        out_ref[...] = x + dot(context, weights_ref[:, wide : wide + features])

    outs = [
        shaped((tokens, features), F32),
        shaped((tokens, features), BF16),
        shaped((tokens, wide), BF16),
        shaped((tokens, features), BF16),
    ]
    ins = [start, stream, mix, *parts]
    specs = [SCALAR, WHOLE, WHOLE] + [ANYWHERE] * count
    if rows is None:
        outs = [shaped((width - wide - features, features), F32)] + outs
    else:
        ins, specs = ins + [rows], specs + [WHOLE]
    scratch = [
        pltpu.VMEM((features, width), BF16),
        pltpu.SemaphoreType.DMA((count,)),
    ]
    return call(kernel, outs, ins, 10 * tokens * features * features, (), specs, None, scratch, LIGHT)


def attend_backward(at, stream, rows, parts, first, mix, start, length, stored, upstream, extra=()):
    normed, packed, context = stored
    tokens, features = stream.shape
    wide = 3 * features
    width = parts[0].shape[1] - first
    small = width - wide - features if extra else 0
    count = len(parts)

    def kernel(*refs):
        start_ref = refs[0]
        part_refs = refs[1 : 1 + count]
        mix_ref, stream_ref, rows_ref, normed_ref, packed_ref, context_ref, up_ref = refs[1 + count : 8 + count]
        extra_refs = refs[8 + count : 8 + count + len(extra)]
        out_ref, mine_ref, other_ref, gains_ref, delta_ref, weights_ref, sems = refs[8 + count + len(extra) :]
        wait = start_parts(part_refs, weights_ref, sems, first)

        def put(columns, values):
            mine_ref[:, columns] = values[: features // 2].astype(BF16)
            other_ref[:, columns] = values[features // 2 :].astype(BF16)

        upstream = up_ref[...]
        branch = upstream.astype(BF16)
        mix = mix_ref[...]
        put(slice(wide, wide + features), dot_tn(context_ref[...], branch))
        wait()
        context_grad = dot_nt(branch, weights_ref[:, wide : wide + features]).astype(BF16)
        context_grad = dot_nt(context_grad, mix).astype(BF16)
        scale = HD ** (-0.5)
        for s in range(tokens // length):
            allowed = allowed_pair(start_ref[s], length)
            here = slice(s * length, (s + 1) * length)
            for p in range(features // (2 * HD)):
                at_q, at_k, at_v = (slice(j * features + p * 2 * HD, j * features + (p + 1) * 2 * HD) for j in range(3))
                queries, keys, values = apart(packed_ref[here, at_q]), packed_ref[here, at_k], packed_ref[here, at_v]
                probs = softmax_pair(queries, keys, allowed)
                out_grad = apart(context_grad[here, at_q])
                delta_ref[here, at_v] = dot_tn(probs.astype(BF16), out_grad).astype(BF16)
                prob_grad = dot_nt(out_grad, values)
                middle = jnp.sum(probs * prob_grad, axis=-1, keepdims=True)
                score_grad = (probs * (prob_grad - middle)).astype(BF16)
                delta_ref[here, at_q] = (together(dot(score_grad, keys)) * scale).astype(BF16)
                delta_ref[here, at_k] = (dot_tn(score_grad, queries) * scale).astype(BF16)
        turned = normed_ref[...].T
        normed_grad = jnp.zeros((tokens, features), F32)
        for j in range(3):
            columns = slice(j * features, (j + 1) * features)
            put(columns, dot(turned, delta_ref[:, columns]))
            normed_grad += dot_nt(delta_ref[:, columns], weights_ref[:, columns])
        out_ref[...] = norm_back(
            stream_ref[...].astype(F32), rows_ref[at : at + 1, :], unmixed(normed_grad, mix), gains_ref, upstream
        )
        if extra:
            mixer_ref, upper_ref, feed_ref = extra_refs
            lines = [gains_ref[0:2, :], feed_ref[0:2, :], upper_ref[0:2, :], mixer_ref[6:, :]]
            lines = dot(jnp.concatenate(lines, axis=0).astype(BF16), mix)
            put(slice(wide + features, width), lines.T)

    outs = [
        shaped((tokens, features), F32),
        shaped((features // 2, wide + features + small), BF16),
        shaped((features // 2, wide + features + small), BF16),
        shaped((8, features), F32),
    ]
    ins = [start, *parts, mix, stream, rows, normed, packed, context, upstream, *extra]
    specs = [SCALAR] + [ANYWHERE] * count + [WHOLE] * (7 + len(extra))
    scratch = [
        pltpu.VMEM((tokens, wide), BF16),
        pltpu.VMEM((features, width), BF16),
        pltpu.SemaphoreType.DMA((count,)),
    ]
    return call(kernel, outs, ins, 22 * tokens * features * features, (), specs, None, scratch, LIGHT)


def feed_forward(stream, rows, expand, shrink, places, mix, depth):
    tokens, features = stream.shape
    inner_width = sum(p.shape[0] for p in shrink)
    step = inner_width // depth
    count, blocks = len(expand), places.shape[0]

    def kernel(*refs):
        places_ref = refs[0]
        expand_refs, shrink_refs = refs[1 : 1 + count], refs[1 + count : -10]
        mix_ref, stream_ref, rows_ref, out_ref, normed_ref, inner_ref = refs[-10:-4]
        expand_ref, shrink_ref, expand_sems, shrink_sems = refs[-4:]
        j = pl.program_id(0)

        @pl.when(j == 0)
        def _():
            wait_expand = start_parts(expand_refs, expand_ref, expand_sems)
            wait_shrink = start_blocks(shrink_refs, places_ref, shrink_ref, shrink_sems)
            x = stream_ref[...]
            normed = (normalize(x)[0] * rows_ref[2:3, :] + rows_ref[3:4, :]).astype(BF16)
            normed_ref[...] = mixed(normed, mix_ref[...])
            out_ref[...] = x
            wait_expand()
            wait_shrink()

        here = pl.ds(pl.multiple_of(j * step, 128), step)
        inner = dot(normed_ref[...], expand_ref[:, here])
        inner_ref[...] = inner
        out_ref[...] += dot(gelu(inner).astype(BF16), shrink_ref[here, :])

    fixed = lambda a: pl.BlockSpec(a.shape, lambda j: (0, 0))
    outs = [
        shaped((tokens, features), F32),
        shaped((tokens, features), BF16),
        shaped((tokens, inner_width), F32),
    ]
    return call(
        kernel,
        outs,
        [places, *expand, *shrink, mix, stream, rows],
        4 * tokens * features * inner_width,
        (depth,),
        [SCALAR] + [ANYWHERE] * (count + len(shrink)) + [fixed(mix), fixed(stream), fixed(rows)],
        [fixed(outs[0]), fixed(outs[1]), pl.BlockSpec((tokens, step), lambda j: (0, j))],
        [
            pltpu.VMEM((features, inner_width), BF16),
            pltpu.VMEM((inner_width, features), BF16),
            pltpu.SemaphoreType.DMA((count,)),
            pltpu.SemaphoreType.DMA((blocks,)),
        ],
        LIGHT,
    )


def feed_backward_shrink(shrink, places, depth, inner, upstream):
    tokens, features = upstream.shape
    inner_width = inner.shape[1]
    step = inner_width // depth
    count, blocks = len(shrink), places.shape[0]
    pieces = max(1, blocks // depth)
    piece = step // pieces
    side, half = max(1, pieces // 2), min(piece, step // 2)

    def kernel(places_ref, *refs):
        shrink_refs = refs[:count]
        inner_ref, up_ref, inner_grad_ref, near_ref, over_ref, active_ref, shrink_ref, sems = refs[count:]
        j = pl.program_id(0)

        @pl.when(j == 0)
        def _():
            start_blocks(shrink_refs, places_ref, shrink_ref, sems)()

        branch = up_ref[...].astype(BF16)
        active, slope = gelu_both(inner_ref[...])
        active_ref[...] = active.astype(BF16).T
        for p in range(pieces):
            start = 0
            if pieces > 1:
                start = pl.multiple_of(places_ref[p * depth + chunk_at(j, places_ref)] - j * step, 16)
            grad = dot(active_ref[pl.ds(start, piece), :], branch).astype(BF16)
            if pieces == 1:
                near_ref[0, 0] = grad[: step // 2]
                over_ref[0, 0] = grad[step // 2 :]
            elif p < pieces // 2:
                near_ref[p, 0] = grad
            else:
                over_ref[p - pieces // 2, 0] = grad
        here = pl.ds(pl.multiple_of(j * step, 128), step)
        inner_grad_ref[...] = (dot_nt(branch, shrink_ref[here, :]) * slope).astype(BF16)

    def chunk_at(j, places_ref):
        return lax.rem(places_ref[0] // step - j + depth, depth)

    def layer(j, places_ref):
        return (0, j if pieces == 1 else chunk_at(j, places_ref), 0, 0)

    columns = pl.BlockSpec((tokens, step), lambda j, places_ref: (0, j))
    outs = [
        shaped((tokens, inner_width), BF16),
        shaped((side, depth, half, features), BF16),
        shaped((side, depth, half, features), BF16),
    ]
    ins = [places, *shrink, inner, upstream]
    moved = sum(a.size * a.dtype.itemsize for a in (*ins, *outs))
    inner_grad, near, over = pl.pallas_call(
        kernel,
        out_shape=outs,
        grid_spec=pltpu.PrefetchScalarGridSpec(
            num_scalar_prefetch=1,
            grid=(depth,),
            in_specs=[ANYWHERE] * count
            + [columns, pl.BlockSpec(upstream.shape, lambda j, places_ref: (0, 0))],
            out_specs=[columns] + [pl.BlockSpec((side, 1, half, features), layer)] * 2,
            scratch_shapes=[
                pltpu.VMEM((step, tokens), BF16),
                pltpu.VMEM((inner_width, features), BF16),
                pltpu.SemaphoreType.DMA((blocks,)),
            ],
        ),
        compiler_params=pltpu.CompilerParams(vmem_limit_bytes=LIMIT),
        cost_estimate=cost(4 * tokens * features * inner_width, moved, LIGHT),
    )(*ins)
    if pieces == 1:
        shrink_grad = [jnp.concatenate([near, over], axis=2).reshape(inner_width, features)]
    else:
        shrink_grad = [near.reshape(-1, features), over.reshape(-1, features)]
    return inner_grad, shrink_grad


def feed_backward_expand(stream, rows, expand, mix, depth, normed, inner_grad, upstream):
    tokens, features = stream.shape
    inner_width = inner_grad.shape[1]
    step = inner_width // depth
    count = len(expand)

    def kernel(*refs):
        expand_refs = refs[:count]
        mix_ref, stream_ref, rows_ref, normed_ref, inner_grad_ref, up_ref = refs[count : count + 6]
        out_ref, mine_ref, other_ref, gains_ref, total_ref, turned_ref, expand_ref, sems = refs[count + 6 :]
        j = pl.program_id(0)

        @pl.when(j == 0)
        def _():
            wait = start_parts(expand_refs, expand_ref, sems)
            turned_ref[...] = normed_ref[...].T
            total_ref[...] = jnp.zeros_like(total_ref)
            wait()

        inner_grad = inner_grad_ref[...]
        expand_grad = dot(turned_ref[...], inner_grad).astype(BF16)
        mine_ref[...] = expand_grad[: features // 2]
        other_ref[...] = expand_grad[features // 2 :]
        here = pl.ds(pl.multiple_of(j * step, 128), step)
        total_ref[...] += dot_nt(inner_grad, expand_ref[:, here])

        @pl.when(j == depth - 1)
        def _():
            grad = unmixed(total_ref[...], mix_ref[...])
            out_ref[...] = norm_back(stream_ref[...], rows_ref[2:3, :], grad, gains_ref, up_ref[...])

    fixed = lambda a: pl.BlockSpec(a.shape, lambda j: (0, 0))
    columns = lambda height: pl.BlockSpec((height, step), lambda j: (0, j))
    outs = [
        shaped((tokens, features), F32),
        shaped((features // 2, inner_width), BF16),
        shaped((features // 2, inner_width), BF16),
        shaped((8, features), F32),
    ]
    out, mine, other, gains = call(
        kernel,
        outs,
        [*expand, mix, stream, rows, normed, inner_grad, upstream],
        4 * tokens * features * inner_width,
        (depth,),
        [ANYWHERE] * count
        + [fixed(mix), fixed(stream), fixed(rows), fixed(normed), columns(tokens), fixed(upstream)],
        [fixed(outs[0]), columns(features // 2), columns(features // 2), fixed(outs[3])],
        [
            pltpu.VMEM((tokens, features), F32),
            pltpu.VMEM((features, tokens), BF16),
            pltpu.VMEM((features, inner_width), BF16),
            pltpu.SemaphoreType.DMA((count,)),
        ],
        LIGHT,
    )
    return out, (mine, other), gains


def gate_of(logits, meta):
    lane = lax.broadcasted_iota(jnp.int32, logits.shape, 1)
    chosen = lane == meta[:, 0:1] + LANE
    return jax.nn.sigmoid(jnp.sum(jnp.where(chosen, logits, 0.0), axis=-1, keepdims=True)), chosen


def put_blocks(refs, columns, values):
    rows = values.shape[0] // len(refs)
    for k, ref in enumerate(refs):
        ref[:, columns] = values[k * rows : (k + 1) * rows]


def mixer_before(stream, rows, facts, teacher, meta, target, slots, experts):
    tokens, features = stream.shape

    def kernel(stream_ref, rows_ref, facts_ref, teacher_ref, meta_ref, target_ref, *refs):
        normed_ref, logits_ref = refs[:2]
        ahead_refs, back_refs = refs[2 : 2 + experts], refs[2 + experts :]
        x = stream_ref[...]
        normed = (normalize(x)[0] * rows_ref[6:7, :] + rows_ref[7:8, :]).astype(BF16)
        normed_ref[...] = normed
        dispatch = lax.broadcasted_iota(jnp.int32, (slots, tokens), 0) == target_ref[...]
        dispatch = dispatch.astype(F32).astype(BF16)
        put_blocks(ahead_refs, slice(None), dot(dispatch, normed).astype(BF16))
        logits = dot_nt(normed, rows_ref[...].astype(BF16))
        logits_ref[...] = logits
        meta = meta_ref[...]
        gate = gate_of(logits, meta)[0]
        factor = facts_ref[1:2, 0:1] * meta[:, 2:3].astype(F32) * gate
        offset = (factor * (x - teacher_ref[...].astype(F32))).astype(BF16)
        slope = factor * gate
        high = slope.astype(BF16)
        low = (slope - high.astype(F32)).astype(BF16)
        lane = lax.broadcasted_iota(jnp.int32, (tokens, 128), 1)
        slope = jnp.where(lane == 0, high.astype(F32), jnp.where(lane == 1, low.astype(F32), 0.0)).astype(BF16)
        put_blocks(back_refs, slice(0, features), dot(dispatch, offset).astype(BF16))
        put_blocks(back_refs, slice(features, None), dot(dispatch, slope).astype(BF16))

    outs = [
        shaped((tokens, features), BF16),
        shaped((tokens, rows.shape[0]), F32),
    ]
    outs += [shaped((slots // experts, features), BF16)] * experts
    outs += [shaped((slots // experts, features + 128), BF16)] * experts
    ins = [stream, rows, facts, teacher, meta, target]
    normed, logits, *blocks = call(kernel, outs, ins, 4 * slots * tokens * features)
    return normed, logits, blocks[:experts], blocks[experts:]


def expert_specs(weights, step):
    owners, height, features = weights.shape
    shrink_rows = height // 2
    expand_rows = features // owners
    each = step // shrink_rows
    first = shrink_rows // expand_rows
    expand = pl.BlockSpec(
        (owners, expand_rows, step), lambda j: (0, first + j * step // features, j * step % features // step)
    )
    return expand, pl.BlockSpec((each, shrink_rows, features), lambda j: (j, 0, 0))


def expert_forward(blocks, weights, depth):
    experts = len(blocks)
    rows, features = blocks[0].shape
    slots = experts * rows
    owners, height, _ = weights.shape
    inner_width = owners * height // 2
    step = inner_width // depth

    def kernel(*refs):
        block_refs, (expand_ref, shrink_ref) = refs[:experts], refs[experts : experts + 2]
        out_refs = refs[experts + 2 : 2 * experts + 2]
        arrived_ref, inner_ref, total_ref = refs[2 * experts + 2 :]
        j = pl.program_id(0)

        @pl.when(j == 0)
        def _():
            for k in range(experts):
                arrived_ref[k * rows : (k + 1) * rows, :] = block_refs[k][...]

        inner = dot(arrived_ref[...], expand_ref[...].reshape(features, step))
        inner_ref[...] = inner
        part = dot(gelu(inner).astype(BF16), shrink_ref[...].reshape(step, features))

        @pl.when(j == 0)
        def _():
            total_ref[...] = part

        @pl.when(j > 0)
        def _():
            total_ref[...] += part

        @pl.when(j == depth - 1)
        def _():
            put_blocks(out_refs, slice(None), total_ref[...].astype(BF16))

    fixed = lambda a: pl.BlockSpec(a.shape, lambda j: (0, 0))
    outs = [shaped((rows, features), BF16)] * experts
    outs += [shaped((slots, features), BF16), shaped((slots, inner_width), F32)]
    *result, arrived, inner = call(
        kernel,
        outs,
        [*blocks, weights, weights],
        4 * slots * features * inner_width,
        (depth,),
        [fixed(b) for b in blocks] + [*expert_specs(weights, step)],
        [fixed(o) for o in outs[:-1]] + [pl.BlockSpec((slots, step), lambda j: (0, j))],
        [pltpu.VMEM((slots, features), F32)],
    )
    return result, arrived, inner


def expert_backward(back, result, inner, weights, depth):
    experts = len(back)
    rows, features = result[0].shape
    slots = experts * rows
    owners, height, _ = weights.shape
    inner_width = owners * height // 2
    step = inner_width // depth

    def kernel(*refs):
        back_refs, result_refs = refs[:experts], refs[experts : 2 * experts]
        inner_ref, expand_ref, shrink_ref = refs[2 * experts : 2 * experts + 3]
        out_refs = refs[2 * experts + 3 : 3 * experts + 3]
        inner_grad_ref, grads_ref, landed_ref, total_ref = refs[3 * experts + 3 :]
        j = pl.program_id(0)

        @pl.when(j == 0)
        def _():
            for k in range(experts):
                terms = back_refs[k][:, features:].astype(F32)
                slope = terms[:, 0:1] + terms[:, 1:2]
                landed = back_refs[k][:, :features].astype(F32) + slope * result_refs[k][...].astype(F32)
                landed_ref[k * rows : (k + 1) * rows, :] = landed.astype(BF16)
            total_ref[...] = jnp.zeros_like(total_ref)

        active, slope = gelu_both(inner_ref[...])
        landed = landed_ref[...]
        inner_grad = (dot_nt(landed, shrink_ref[...].reshape(step, features)) * slope).astype(BF16)
        inner_grad_ref[...] = inner_grad
        grads_ref[...] = dot_tn(active.astype(BF16), landed).astype(BF16)
        total_ref[...] += dot_nt(inner_grad, expand_ref[...].reshape(features, step))

        @pl.when(j == depth - 1)
        def _():
            put_blocks(out_refs, slice(None), total_ref[...].astype(BF16))

    fixed = lambda a: pl.BlockSpec(a.shape, lambda j: (0, 0))
    columns = lambda height: pl.BlockSpec((height, step), lambda j: (0, j))
    outs = [shaped((rows, features), BF16)] * experts
    outs += [shaped((slots, inner_width), BF16), shaped((inner_width, features), BF16)]
    *rows_grad, inner_grad, grads = call(
        kernel,
        outs,
        [*back, *result, inner, weights, weights],
        6 * slots * features * inner_width,
        (depth,),
        [fixed(b) for b in (*back, *result)]
        + [
            columns(slots),
            *expert_specs(weights, step),
        ],
        [fixed(o) for o in outs[:-2]]
        + [columns(slots), pl.BlockSpec((step, features), lambda j: (j, 0))],
        [pltpu.VMEM((slots, features), BF16), pltpu.VMEM((slots, features), F32)],
        LIGHT,
    )
    return rows_grad, inner_grad, grads


def expert_expand_grad(arrived, inner_grad):
    slots, features = arrived.shape
    inner_width = inner_grad.shape[1]

    def kernel(arrived_ref, inner_grad_ref, out_ref, turned_ref):
        @pl.when(pl.program_id(0) == 0)
        def _():
            turned_ref[...] = arrived_ref[...].T

        out_ref[...] = dot(turned_ref[...], inner_grad_ref[...]).astype(BF16)

    columns = lambda height: pl.BlockSpec((height, features), lambda j: (0, j))
    [grad] = call(
        kernel,
        [shaped((features, inner_width), BF16)],
        [arrived, inner_grad],
        2 * slots * features * inner_width,
        (inner_width // features,),
        [pl.BlockSpec(arrived.shape, lambda j: (0, 0)), columns(slots)],
        [columns(features)],
        [pltpu.VMEM((features, slots), BF16)],
        LIGHT,
    )
    return grad


def mixer_after(stream, rows, facts, teacher, meta, normed, logits, returned, rows_grad, experts):
    tokens, features = stream.shape
    block = returned[0].shape[0]
    slots = experts * block

    def kernel(*refs):
        stream_ref, rows_ref, facts_ref, teacher_ref, meta_ref, normed_ref, logits_ref = refs[:7]
        returned_refs, rows_grad_refs = refs[7 : 7 + experts], refs[7 + experts : 7 + 2 * experts]
        states_ref, grad_ref, small_ref, squared_ref = refs[7 + 2 * experts :]
        x = stream_ref[...]
        meta = meta_ref[...]
        combine = lax.broadcasted_iota(jnp.int32, (tokens, slots), 1) == meta[:, 1:2]
        combine = combine.astype(F32).astype(BF16)
        combined = dot(combine, jnp.concatenate([r[...] for r in returned_refs], axis=0))
        logits = logits_ref[...]
        gate, chosen = gate_of(logits, meta)
        final = x + gate * combined
        states_ref[...] = final.astype(BF16)
        valid = meta[:, 2:3].astype(F32)
        difference = final - teacher_ref[...].astype(F32)
        masked = valid * difference
        squared = 0.5 * jnp.sum(jnp.sum(masked * difference, axis=-1, keepdims=True), axis=0, keepdims=True)
        squared_ref[...] = jnp.broadcast_to(squared, squared_ref.shape)
        upstream = facts_ref[1:2, 0:1] * masked
        gate_grad = jnp.sum(upstream * combined, axis=-1, keepdims=True)
        lane = lax.broadcasted_iota(jnp.int32, logits.shape, 1)
        real = (lane >= LANE) & (lane < LANE + experts)
        shown = jnp.where(real, logits, -1e30)
        exponent = jnp.exp(shown - jnp.max(shown, axis=-1, keepdims=True))
        probs = exponent / jnp.sum(exponent, axis=-1, keepdims=True)
        share = facts_ref[0:1, :]
        tilt = jnp.sum(probs * share, axis=-1, keepdims=True)
        logits_grad = facts_ref[2:3, 0:1] * valid * probs * (share - tilt)
        logits_grad = jnp.where(real, logits_grad, 0.0)
        logits_grad += jnp.where(chosen, gate_grad * gate * (1.0 - gate), 0.0)
        first = logits_grad.astype(BF16)
        left = logits_grad - first.astype(F32)
        second = left.astype(BF16)
        third = (left - second.astype(F32)).astype(BF16)
        weights = rows_ref[...].astype(BF16)
        normed = normed_ref[...]
        normed_grad = dot(combine, jnp.concatenate([r[...] for r in rows_grad_refs], axis=0))
        normed_grad += dot(third, weights) + dot(second, weights) + dot(first, weights)
        small_ref[...] = dot_tn(third, normed) + dot_tn(second, normed) + dot_tn(first, normed)
        grad_ref[...] = norm_back(x, rows_ref[6:7, :], normed_grad, small_ref.at[6:8], upstream)

    outs = [
        shaped((tokens, features), BF16),
        shaped((tokens, features), F32),
        shaped(rows.shape, F32),
        shaped((8, 128), F32),
    ]
    ins = [stream, rows, facts, teacher, meta, normed, logits, *returned, *rows_grad]
    return call(kernel, outs, ins, 4 * slots * tokens * features)


def body(
    tokens,
    teacher,
    routes,
    piece_start,
    valid_mask,
    lower_gain,
    lower_bias,
    lower_triple,
    lower_output,
    feed_gain,
    feed_bias,
    feed_expand,
    feed_shrink,
    upper_gain,
    upper_bias,
    upper_triple,
    upper_output,
    mixer_gain,
    mixer_bias,
    router,
    expert_expand,
    expert_shrink,
):
    count, length, features = tokens.shape
    local = count * length
    experts = router.shape[1]
    share_rows = router.shape[0]
    devices = lax.axis_size("dp") * lax.axis_size("expert")
    capacity = max(2, 2 * length // experts)
    total_tokens = local * devices
    valid = valid_mask.astype(F32)
    route = routes[..., 0]
    chosen = (route[..., None] == jnp.arange(experts, dtype=jnp.int32)).astype(F32)

    vectors = [lower_gain, lower_bias, feed_gain, feed_bias, upper_gain, upper_bias, mixer_gain, mixer_bias]
    extra_width = 128

    wide = 3 * features
    depth = lax.axis_size("dp") // 2

    row_order = (order(share_rows)[:, None] + jnp.arange(share_rows, dtype=jnp.int32)).reshape(1, features)
    mix = (jnp.arange(features, dtype=jnp.int32)[:, None] == row_order).astype(BF16)
    shrink_rows = feed_shrink.shape[0]
    inner_width = feed_expand.shape[1]
    inner_width = feed_expand.shape[1]
    lower_own = pack_lower(lower_triple, lower_output, vectors, router.T, route, valid_mask)
    upper_own = jnp.concatenate([upper_triple, upper_output], axis=1)

    position = jnp.arange(length, dtype=jnp.int32)
    earlier = (position[:, None] > position[None, :]).astype(BF16)
    before = jnp.einsum("qk,mke->mqe", earlier, chosen.astype(BF16), preferred_element_type=F32)
    slot = jnp.sum(before * chosen, axis=-1).astype(jnp.int32)
    target = (route ^ lax.axis_index("expert")) * (count * capacity) + jnp.arange(count, dtype=jnp.int32)[:, None] * capacity + slot
    slots = experts * count * capacity
    meta = jnp.stack([route.reshape(-1), target.reshape(-1), valid_mask.reshape(-1)], axis=1)
    target = target.reshape(1, local)

    stream_in = tokens.reshape(local, features)
    labels = teacher.reshape(local, features)
    places = order(shrink_rows)
    pieces = expert_expand[0].reshape(-1, inner_width // features, features)
    experts_own = jnp.concatenate([expert_shrink[0], jnp.moveaxis(pieces, 1, 0).reshape(-1, features)])

    shrink_line, shrink_over = gather_lines(feed_shrink)
    wide_line, wide_over = gather_lines(jnp.concatenate([feed_expand, upper_own], axis=1))
    lower = pull_line(lower_own)

    lower, experts_own, mix, meta, target, places = at_once((lower, experts_own, mix, meta, target, places))
    experts_full = lax.all_gather(experts_own, "dp")
    lower = jnp.stack([lower_own, *lower])
    near = pull_near(lower)

    lower, near, shrink_line, shrink_over = at_once((lower, near, shrink_line, shrink_over))
    lower = pull_far(lower, near)
    shrink_near = pull_near(shrink_line)

    lower, shrink_line, shrink_near = at_once((lower, shrink_line, shrink_near))
    lower_over = pull_over(lower[1])

    lower, lower_over, wide_line, wide_over = at_once((lower, lower_over, wide_line, wide_over))
    lower = in_order(*lower, lower_over)
    shrink_full = pull_far(shrink_line, shrink_near, shrink_over)
    expand_line, expand_over = wide_line[..., :inner_width], wide_over[..., :inner_width]
    upper_line, upper_over = wide_line[..., inner_width:], wide_over[..., inner_width:]
    expand_near = pull_near(expand_line)
    rows, stream_one, *stored_one = attend_forward(0, stream_in, None, lower, 0, mix, piece_start, length)

    shrink_full, expand_line, expand_near, rows, stream_one = at_once(
        (shrink_full, expand_line, expand_near, rows, stream_one)
    )
    shrink_full = in_order(*shrink_full, pull_over(shrink_full[1]))
    expand_full = pull_far(expand_line, expand_near, expand_over)
    upper_near = pull_near(upper_line)
    lane = jnp.arange(features, dtype=jnp.int32)
    sums = rows[LANE + experts : LANE + 2 * experts + 1]
    sums = jnp.sum(jnp.where(lane % share_rows < count, sums, 0.0), axis=1)
    valid_total = sums[experts]
    loss_ratio = total_tokens / valid_total
    balance_scale = total_tokens * features * 0.1 * experts / valid_total
    share = jnp.pad(sums[:experts] / valid_total, (LANE, extra_width - LANE - experts))
    facts = jnp.stack([share, jnp.full_like(share, loss_ratio), jnp.full_like(share, balance_scale)])
    facts = jnp.pad(facts, ((0, 5), (0, 0)))

    shrink_full, expand_full, upper_line, upper_near, stream_one, facts = at_once(
        (shrink_full, expand_full, upper_line, upper_near, stream_one, facts)
    )
    expand_full = in_order(*expand_full, pull_over(expand_full[1]))

    expand_full, upper_line, upper_near, stream_one = at_once((expand_full, upper_line, upper_near, stream_one))
    upper = pull_far(upper_line, upper_near, upper_over)

    if shrink_rows % 16:
        whole = jnp.concatenate(shrink_full, axis=0).reshape(devices, shrink_rows, features)
        shrink_full = [jnp.zeros_like(whole).at[places // shrink_rows].set(whole).reshape(-1, features)]
        places = jnp.zeros((1,), jnp.int32)
    stream_two, *stored_two = feed_forward(stream_one, rows, expand_full, shrink_full, places, mix, depth)

    upper, stream_two = at_once((upper, stream_two))
    upper = in_order(*upper, pull_over(upper[1]))
    stream_three, *stored_three = attend_forward(4, stream_two, rows, upper, 0, mix, piece_start, length)
    normed, logits, ahead, back = mixer_before(
        stream_three, rows, facts, labels, meta, target, slots, experts
    )
    ahead = exchange(ahead)
    back = exchange([after(b, *ahead) for b in back])
    result, arrived, inner = expert_forward(ahead, experts_full, depth)
    returned = exchange(result)
    rows_grad, inner_grad, expert_out_grad = expert_backward(back, result, inner, experts_full, depth)
    returned, rows_grad, inner_grad, expert_out_grad = at_once((returned, rows_grad, inner_grad, expert_out_grad))
    expert_out_grad = lax.psum_scatter(expert_out_grad, "dp", scatter_dimension=0, tiled=True)
    rows_grad = exchange(rows_grad)
    states, grad_three, mixer_small, squared = mixer_after(
        stream_three, rows, facts, labels, meta, normed, logits, returned, rows_grad, experts
    )
    grad_two, *upper_grad, upper_small = attend_backward(
        4, stream_two, rows, upper, 0, mix, piece_start, length, stored_three, grad_three
    )
    hops = total_hops()

    def hop_loss(value, first, last):
        for target in hops[first:last] if hops else ():
            value = value + hop(value, target)
        return value

    inner_grad = after(inner_grad, grad_two)
    upper_mine, upper_other = upper_grad
    upper_other = swap_cores(upper_other)
    expert_in_grad = expert_expand_grad(arrived, inner_grad)

    upper_mine, upper_other, expert_in_grad, grad_two = at_once((upper_mine, upper_other, expert_in_grad, grad_two))
    expert_in_grad = lax.psum_scatter(expert_in_grad, "dp", scatter_dimension=0, tiled=True)
    upper_part = sum_cores(upper_mine, upper_other)

    grad_two, *upper_part = at_once((grad_two, *upper_part))
    upper_part = scatter_far(upper_part)
    squared = hop_loss(squared, 0, 1)
    feed_normed, inner_pre = stored_two
    inner_grad, shrink_grad = feed_backward_shrink(shrink_full, places, depth, inner_pre, grad_two)
    if shrink_rows % 16:
        blocks = order(shrink_rows) // shrink_rows
        pick = (blocks[:, None] == jnp.arange(devices, dtype=jnp.int32)).astype(BF16)
        shrink_grad = dot(pick, shrink_grad[0].reshape(devices, -1)).astype(BF16).reshape(2, -1, features)
        shrink_grad = [shrink_grad[0], shrink_grad[1]]

    upper_part, squared, inner_grad, shrink_grad = at_once((upper_part, squared, inner_grad, shrink_grad))
    upper_part = scatter_near(upper_part)
    squared = hop_loss(squared, 1, 2)
    shrink_mine, shrink_other = shrink_grad
    shrink_other = swap_cores(shrink_other)
    grad_one, expand_grad, feed_small = feed_backward_expand(
        stream_one, rows, expand_full, mix, depth, feed_normed, inner_grad, grad_two
    )

    upper_part, squared, shrink_mine, shrink_other, expand_grad, grad_one = at_once(
        (upper_part, squared, shrink_mine, shrink_other, expand_grad, grad_one)
    )
    shrink_part = scatter_far(sum_cores(shrink_mine, shrink_other))
    expand_part = scatter_cores(*expand_grad)
    squared = hop_loss(squared, 2, 3)

    upper_part, expand_part, shrink_part, grad_one, squared = at_once(
        (upper_part, expand_part, shrink_part, grad_one, squared)
    )
    expand_part = scatter_far(expand_part)
    shrink_part = scatter_near(shrink_part)
    upper_part = scatter_line(upper_part)
    grad_in, *lower_grad, _ = attend_backward(
        0, stream_in, rows, lower, 0, mix, piece_start, length, stored_one, grad_one, (mixer_small, upper_small, feed_small)
    )

    upper_part, expand_part, shrink_part, grad_in, lower_grad, squared = at_once(
        (upper_part, expand_part, shrink_part, grad_in, lower_grad, squared)
    )
    lower_part = scatter_cores(*lower_grad)
    expand_part = scatter_near(expand_part)
    shrink_part = scatter_line(shrink_part)

    lower_part, expand_part, shrink_part, upper_part, squared, expert_out_grad, expert_in_grad = at_once(
        (lower_part, expand_part, shrink_part, upper_part, squared, expert_out_grad, expert_in_grad)
    )
    lower_part = scatter_far(lower_part)
    expand_part = scatter_line(expand_part)
    squared = hop_loss(squared, 3, 4)
    upper_part, shrink_part = total(upper_part), total(shrink_part)
    expert_out_grad, expert_in_grad = expert_out_grad.astype(F32), expert_in_grad.astype(F32)

    lower_part, expand_part, shrink_part, upper_part, squared, expert_in_grad, expert_out_grad = at_once(
        (lower_part, expand_part, shrink_part, upper_part, squared, expert_in_grad, expert_out_grad)
    )
    lower_part = scatter_near(lower_part)
    squared = hop_loss(squared, 4, None)

    lower_part, expand_part, squared = at_once((lower_part, expand_part, squared))
    lower_part, expand_part = total(scatter_line(lower_part)), total(expand_part)
    if hops is None:
        squared = lax.psum(squared, AXES)
    small = lower_part[:, wide + features :]
    squared_total = squared[0, 0]
    mean_loss = loss_ratio * squared_total / (total_tokens * features)
    return (
        states.reshape(tokens.shape),
        grad_in.reshape(tokens.shape),
        small[:, 0],
        small[:, 1],
        lower_part[:, :wide],
        lower_part[:, wide : wide + features],
        small[:, 2],
        small[:, 3],
        expand_part,
        shrink_part,
        small[:, 4],
        small[:, 5],
        upper_part[:, :wide],
        upper_part[:, wide:],
        small[:, 6],
        small[:, 7],
        small[:, 8 : 8 + experts],
        expert_in_grad[None],
        expert_out_grad[None],
        mean_loss,
    )


def solution(mesh):
    both = ("dp", "expert")
    token = P(both, None, None)
    vector = P(both)
    matrix = P(both, None)
    expert = P("expert", "dp", None)
    dense = (vector, vector, matrix, matrix, vector, vector, matrix, matrix)
    weights = dense + (vector, vector, matrix, matrix, vector, vector, matrix, expert, expert)
    return jax.shard_map(
        body,
        mesh=mesh,
        in_specs=(token, token, token, vector, matrix) + weights,
        out_specs=(token, token) + weights + (P(),),
        check_vma=False,
    )
```
